256 devices in a mesh: grp: 16 (over x, y), seq: 16 (over z, core).
Axes of the slice: x: 4, y: 4, z: 8, core: 2. Of those that a mesh axis runs over, the one named last changes fastest.
Arguments:
- q_spatial: bfloat16 [256, 256, 1536], P(('grp', 'seq')), may hold values from -5 to 5
- k_spatial: bfloat16 [256, 256, 1536], P(('grp', 'seq')), may hold values from -5 to 5
- v_spatial: bfloat16 [256, 256, 1536], P(('grp', 'seq')), may hold values from -6 to 6
- q_temporal: bfloat16 [256, 256, 1536], P(('grp', 'seq')), may hold values from -5 to 5
- k_temporal: bfloat16 [256, 256, 1536], P(('grp', 'seq')), may hold values from -5 to 5
- rel_bias: float32 [12, 31], replicated, may hold values from -4 to 4
- clip_ids: int32 [16, 16], P('grp', 'seq'), may hold values from 0 to 15, as said below
- cotangent: bfloat16 [256, 256, 1536], P(('grp', 'seq')), may hold values from -6 to 6
Outputs:
- result: bfloat16 [256, 256, 1536], P(('grp', 'seq'))
- grad_q_spatial: bfloat16 [256, 256, 1536], P(('grp', 'seq'))
- grad_k_spatial: bfloat16 [256, 256, 1536], P(('grp', 'seq'))
- grad_v_spatial: bfloat16 [256, 256, 1536], P(('grp', 'seq'))
- grad_q_temporal: bfloat16 [256, 256, 1536], P(('grp', 'seq'))
- grad_k_temporal: bfloat16 [256, 256, 1536], P(('grp', 'seq'))
- grad_rel_bias: float32 [12, 31], replicated
The draws below stay inside these ranges and needn't reach their ends.
Inputs may be any that keep to these rules, and one draw needn't show every extreme that they name: `clip_ids`: within a group, clips are numbered from 0 in frame order and a clip's frames are consecutive; some group is a single clip of all 16 frames and some group has only one-frame clips.
All inputs are finite; a program needn't handle non-finite values.
Results may differ from the reference program's by a relative error of at most 0.027.
Values may be sent and summed in bfloat16 or wider, within the bound.
No kernel may reach another device: no remote copies, remote signals or barrier semaphores. Data moves between devices by JAX's collectives and lax.ppermute only.
A program may use at most 64 MiB of HBM per device.

```python
import jax
import jax.numpy as jnp
from jax import lax

HEADS = 12
HEAD_DIM = 128
PATCHES = 256
WIDTH = 1536
FRAMES_GRP = 16
FRAMES = 256
RELS = 31
N_GRP = 16


def draw_q_spatial(key, part):
    own_key = jax.random.fold_in(key, 1)
    return jnp.clip(jax.random.normal(own_key, (FRAMES, PATCHES, WIDTH)), -5.0, 5.0).astype(jnp.bfloat16)


def draw_k_spatial(key, part):
    own_key = jax.random.fold_in(key, 2)
    return jnp.clip(jax.random.normal(own_key, (FRAMES, PATCHES, WIDTH)), -5.0, 5.0).astype(jnp.bfloat16)


def draw_q_temporal(key, part):
    own_key = jax.random.fold_in(key, 3)
    return jnp.clip(jax.random.normal(own_key, (FRAMES, PATCHES, WIDTH)), -5.0, 5.0).astype(jnp.bfloat16)


def draw_k_temporal(key, part):
    own_key = jax.random.fold_in(key, 4)
    return jnp.clip(jax.random.normal(own_key, (FRAMES, PATCHES, WIDTH)), -5.0, 5.0).astype(jnp.bfloat16)


def draw_clip_ids(key, part):
    key = jax.random.fold_in(key, 5)
    starts = jax.random.randint(key, (N_GRP, FRAMES_GRP), 0, 4) == 0
    row = jnp.arange(N_GRP, dtype=jnp.int32)[:, None]
    col = jnp.arange(FRAMES_GRP, dtype=jnp.int32)[None, :]
    starts = jnp.where(col == 0, True, starts)
    starts = jnp.where(row == 0, col == 0, starts)
    starts = jnp.where(row == N_GRP - 1, True, starts)
    return (jnp.cumsum(starts.astype(jnp.int32), axis=1) - 1).astype(jnp.int32)


def levels(stream_key, dims, cuts, least, largest):
    def one(position, shards_of):
        heights = jax.random.uniform(jax.random.fold_in(jax.random.fold_in(stream_key, 6), position), (shards_of,), jnp.float32, least / len(cuts), largest / len(cuts))
        return jnp.repeat(jnp.exp(heights), dims[position] // shards_of).reshape((-1,) + (1,) * (len(dims) - position - 1))

    gain = one(*cuts[0])
    for cut in cuts[1:]:
        gain = gain * one(*cut)
    return gain


def centred(rng, shape, width, limit, cuts=(), held_as=jnp.bfloat16):
    level = levels(rng, shape, cuts, -0.22, 0.18) if cuts else 1.0
    drawn = jax.random.normal(rng, shape, jnp.float32) * width * level
    return jnp.minimum(jnp.maximum(drawn, -limit), limit).astype(held_as)


def setup_inputs(seed: int = 0) -> dict:
    seeds = jax.random.split(jax.random.key(seed), 9)
    q_spatial = draw_q_spatial(jax.random.fold_in(seeds[8], 71), 0)
    k_spatial = draw_k_spatial(jax.random.fold_in(seeds[8], 71), 0)
    v_spatial = centred(seeds[2], (FRAMES, PATCHES, WIDTH), 1.0, 6.0, ((0, 256),))
    q_temporal = draw_q_temporal(jax.random.fold_in(seeds[8], 71), 0)
    k_temporal = draw_k_temporal(jax.random.fold_in(seeds[8], 71), 0)
    rel_bias = centred(seeds[5], (HEADS, RELS), 1.0, 4.0, (), jnp.float32)
    clip_ids = draw_clip_ids(jax.random.fold_in(seeds[8], 71), 0)
    cotangent = centred(seeds[7], (FRAMES, PATCHES, WIDTH), 1.0, 6.0, ((0, 256),))
    return dict(q_spatial=q_spatial, k_spatial=k_spatial, v_spatial=v_spatial, q_temporal=q_temporal, k_temporal=k_temporal, rel_bias=rel_bias, clip_ids=clip_ids, cotangent=cotangent)


SPATIAL = ("bihd,bjhd->bhij", "bhij,bjhd->bihd", "bhij,bihd->bjhd")
TEMPORAL = ("ibhd,jbhd->bhij", "bhij,jbhd->ibhd", "bhij,ibhd->jbhd")
NEG_FILL = -1e30


def product(pattern, left, right):
    return jnp.einsum(pattern, left.astype(jnp.float32), right.astype(jnp.float32))


def attend(queries, key_heads, values, bias_term, same_clip, patterns):
    factor = queries.shape[-1] ** -0.5
    scores = product(patterns[0], queries, key_heads) * factor + bias_term
    scores = jnp.where(same_clip, scores, NEG_FILL)
    row_max = jnp.max(scores, axis=-1, keepdims=True)
    raw_weights = jnp.where(same_clip, jnp.exp(scores - row_max), 0.0)
    attn_prob = raw_weights / jnp.sum(raw_weights, axis=-1, keepdims=True)
    attn_low = attn_prob.astype(jnp.bfloat16)
    mixed = product(patterns[1], attn_low, values).astype(jnp.bfloat16)
    return mixed, attn_prob, attn_low


def attend_back(queries, key_heads, values, attn_prob, attn_low, upstream, patterns):
    factor = queries.shape[-1] ** -0.5
    grad_prob = product(patterns[0], upstream, values)
    grad_values = product(patterns[2], attn_low, upstream).astype(jnp.bfloat16)
    row_dot = jnp.sum(attn_prob * grad_prob, axis=-1, keepdims=True)
    grad_score = attn_prob * (grad_prob - row_dot)
    grad_low = (grad_score * factor).astype(jnp.bfloat16)
    grad_q = product(patterns[1], grad_low, key_heads).astype(jnp.bfloat16)
    grad_k = product(patterns[2], grad_low, queries).astype(jnp.bfloat16)
    return grad_q, grad_k, grad_values, grad_score


def offsets_table(frames):
    rows = jnp.arange(frames, dtype=jnp.int32)
    offset = rows[:, None] - rows[None, :] + (frames - 1)
    slots = jnp.arange(2 * frames - 1, dtype=jnp.int32)
    return (offset[:, :, None] == slots[None, None, :]).astype(jnp.float32)


def group_pass(q_sp, k_sp, v_sp, q_tm, k_tm, upstream, clip_row, rel_bias):
    table = offsets_table(q_sp.shape[0])
    bias_grid = jnp.einsum("hr,ijr->hij", rel_bias, table, precision=lax.Precision.HIGHEST)
    every = jnp.ones((q_sp.shape[1], q_sp.shape[1]), dtype=bool)
    same_clip = clip_row[:, None] == clip_row[None, :]
    spatial_out, sp_prob, sp_low = attend(q_sp, k_sp, v_sp, 0.0, every, SPATIAL)
    result, tm_prob, tm_low = attend(q_tm, k_tm, spatial_out, bias_grid, same_clip, TEMPORAL)
    grad_qt, grad_kt, grad_mid, grad_score = attend_back(q_tm, k_tm, spatial_out, tm_prob, tm_low, upstream, TEMPORAL)
    grad_bias = jnp.einsum("hij,ijr->hr", jnp.sum(grad_score, axis=0), table, precision=lax.Precision.HIGHEST)
    grad_qs, grad_ks, grad_vs, spatial_score = attend_back(q_sp, k_sp, v_sp, sp_prob, sp_low, grad_mid, SPATIAL)
    return result, grad_qs, grad_ks, grad_vs, grad_qt, grad_kt, grad_bias


def reference(q_spatial, k_spatial, v_spatial, q_temporal, k_temporal, rel_bias, clip_ids, cotangent):
    grouped = (N_GRP, FRAMES_GRP, PATCHES, HEADS, HEAD_DIM)
    inputs = (q_spatial.reshape(grouped), k_spatial.reshape(grouped), v_spatial.reshape(grouped),
              q_temporal.reshape(grouped), k_temporal.reshape(grouped), cotangent.reshape(grouped), clip_ids)

    def one_group(group):
        return group_pass(group[0], group[1], group[2], group[3], group[4], group[5], group[6], rel_bias)

    stacked = lax.map(one_group, inputs)
    flat = (FRAMES, PATCHES, WIDTH)
    return (stacked[0].reshape(flat), stacked[1].reshape(flat), stacked[2].reshape(flat),
            stacked[3].reshape(flat), stacked[4].reshape(flat), stacked[5].reshape(flat),
            jnp.sum(stacked[6], axis=0))
```

```python
import functools

import jax
import jax.numpy as jnp
from jax import lax
from jax.experimental import pallas as pl
from jax.experimental.pallas import tpu as pltpu
from jax.sharding import PartitionSpec as P

HEADS = 12
DIM = 128
SEQ = 16
TOK = 16
ROWS = SEQ * TOK
WIDTH = HEADS * DIM
SCALE = DIM ** (-0.5)
NEG = -1e30
BF = jnp.bfloat16
F32 = jnp.float32
PARAMS = pltpu.CompilerParams(vmem_limit_bytes=40 * 1024 * 1024)


def mm(left, right):
    return lax.dot_general(left, right, (((1,), (0,)), ((), ())), preferred_element_type=F32)


def mm_nt(left, right):
    return lax.dot_general(left, right, (((1,), (1,)), ((), ())), preferred_element_type=F32)


def mm_tn(left, right):
    return lax.dot_general(left, right, (((0,), (0,)), ((), ())), preferred_element_type=F32)


def softmax(scores):
    raw = jnp.exp(scores - jnp.max(scores, axis=-1, keepdims=True))
    return raw / jnp.sum(raw, axis=-1, keepdims=True)


def cost(products, rw):
    return pl.CostEstimate(
        flops=2 * products * HEADS * ROWS * ROWS * DIM,
        bytes_accessed=rw * ROWS * WIDTH * 2,
        transcendentals=HEADS * ROWS * ROWS,
    )


FRAME = pl.BlockSpec((1, ROWS, DIM), lambda h: (0, 0, h))
PROB = pl.BlockSpec((1, ROWS, ROWS), lambda h: (h, 0, 0))


def frame_shape():
    return jax.ShapeDtypeStruct((1, ROWS, WIDTH), BF)


def tile_spec(first):
    return pl.BlockSpec((SEQ, 1, TOK, DIM), lambda h: (0, first + h, 0, 0))


def spatial_fwd_kernel(q_ref, k_ref, v_ref, out_ref):
    prob = softmax(mm_nt(q_ref[0], k_ref[0]) * SCALE)
    out = mm(prob.astype(BF), v_ref[0]).astype(BF)
    out_ref[:, 0] = out.reshape(SEQ, TOK, DIM)


def spatial_bwd_kernel(q_ref, k_ref, v_ref, up_ref, gq_ref, gk_ref, gv_ref):
    q, k, v = q_ref[0], k_ref[0], v_ref[0]
    up = up_ref[:, 0].reshape(ROWS, DIM)
    prob = softmax(mm_nt(q, k) * SCALE)
    grad_prob = mm_nt(up, v)
    gv_ref[0] = mm_tn(prob.astype(BF), up).astype(BF)
    row_dot = jnp.sum(prob * grad_prob, axis=-1, keepdims=True)
    low = (prob * (grad_prob - row_dot) * SCALE).astype(BF)
    gq_ref[0] = mm(low, k).astype(BF)
    gk_ref[0] = mm_tn(low, q).astype(BF)


def temporal_a_kernel(q_ref, k_ref, up_ref, bias_ref, ccol_ref, crow_ref, prob_ref, mid_ref):
    q = q_ref[:, 0].reshape(ROWS, DIM)
    k = k_ref[:, 0].reshape(ROWS, DIM)
    up = up_ref[:, 0].reshape(ROWS, DIM)
    row = lax.broadcasted_iota(jnp.int32, (ROWS, ROWS), 0)
    col = lax.broadcasted_iota(jnp.int32, (ROWS, ROWS), 1)
    same = ((row & (TOK - 1)) == (col & (TOK - 1))) & (ccol_ref[...] == crow_ref[...])
    bias = jnp.broadcast_to(bias_ref[0][:, None, :], (SEQ, TOK, ROWS)).reshape(ROWS, ROWS)
    scores = jnp.where(same, mm_nt(q, k) * SCALE + bias, NEG)
    raw = jnp.where(same, jnp.exp(scores - jnp.max(scores, axis=-1, keepdims=True)), 0.0)
    prob = raw / jnp.sum(raw, axis=-1, keepdims=True)
    prob_ref[0] = prob
    mid_ref[:, 0] = mm_tn(prob.astype(BF), up).astype(BF).reshape(SEQ, TOK, DIM)


def temporal_b_kernel(q_ref, k_ref, up_ref, so_ref, prob_ref, out_ref, bias_ref):
    q = q_ref[:, 0].reshape(ROWS, DIM)
    k = k_ref[:, 0].reshape(ROWS, DIM)
    up = up_ref[:, 0].reshape(ROWS, DIM)
    so = so_ref[:, 0].reshape(ROWS, DIM)
    prob = prob_ref[0]
    out_ref[:, 0] = mm(prob.astype(BF), so).astype(BF).reshape(SEQ, TOK, DIM)
    grad_prob = mm_nt(up, so)
    row_dot = jnp.sum(prob * grad_prob, axis=-1, keepdims=True)
    score = prob * (grad_prob - row_dot)
    bias_ref[0] = jnp.sum(score.reshape(SEQ, TOK, ROWS), axis=1)
    low = (score * SCALE).astype(BF)
    out_ref[:, 1] = mm(low, k).astype(BF).reshape(SEQ, TOK, DIM)
    out_ref[:, 2] = mm_tn(low, q).astype(BF).reshape(SEQ, TOK, DIM)


def pack_kernel(clip_ref, q_ref, k_ref, up_ref, out_ref):
    for i, ref in enumerate((q_ref, k_ref, up_ref)):
        for h in range(HEADS):
            block = ref[0, :, h * DIM:(h + 1) * DIM]
            out_ref[:, i * HEADS + h] = block.reshape(SEQ, TOK, DIM)
    clip = jnp.full((SEQ, TOK, DIM), clip_ref[0, 0], jnp.int32)
    out_ref[:, 3 * HEADS] = clip.astype(F32).astype(BF)


def unpack_kernel(in_ref, res_ref, gq_ref, gk_ref):
    for h in range(HEADS):
        for i, ref in enumerate((res_ref, gq_ref, gk_ref)):
            ref[0, :, h * DIM:(h + 1) * DIM] = in_ref[:, 3 * h + i].reshape(ROWS, DIM)


def exchange(packed):
    return lax.all_to_all(packed, "seq", split_axis=0, concat_axis=0, tiled=True)


def sum_of_four(terms, axis, step):
    size = lax.axis_size(axis)

    def partner(mask):
        return lax.ppermute(terms, axis, [(i, i ^ (mask * step)) for i in range(size)])

    return (terms + partner(1)) + (partner(2) + partner(3))


def bias_sum(terms):
    for axis, step in (("grp", 1), ("grp", 4), ("seq", 1), ("seq", 4)):
        terms = sum_of_four(terms, axis, step)
    return terms


def offsets_table():
    rows = jnp.arange(SEQ, dtype=jnp.int32)
    offset = rows[:, None] - rows[None, :] + (SEQ - 1)
    slots = jnp.arange(2 * SEQ - 1, dtype=jnp.int32)
    return (offset[:, :, None] == slots[None, None, :]).astype(F32)


def per_device(
    q_spatial, k_spatial, v_spatial, q_temporal, k_temporal, rel_bias, clip_ids, cotangent
):
    vmem = pl.BlockSpec(memory_space=pltpu.VMEM)
    packed = pl.pallas_call(
        pack_kernel,
        out_shape=jax.ShapeDtypeStruct((SEQ, 3 * HEADS + 1, TOK, DIM), BF),
        in_specs=[pl.BlockSpec(memory_space=pltpu.SMEM), vmem, vmem, vmem],
        out_specs=vmem,
        compiler_params=PARAMS,
        name="pack",
    )(clip_ids, q_temporal, k_temporal, cotangent)
    there = exchange(packed)

    spatial_out = pl.pallas_call(
        spatial_fwd_kernel,
        grid=(HEADS,),
        out_shape=jax.ShapeDtypeStruct((SEQ, HEADS, TOK, DIM), BF),
        in_specs=[FRAME] * 3,
        out_specs=tile_spec(0),
        compiler_params=PARAMS,
        cost_estimate=cost(2, 4),
        name="spatial_fwd",
    )(q_spatial, k_spatial, v_spatial)
    there, spatial_out = lax.optimization_barrier((there, spatial_out))
    so = exchange(spatial_out)

    table = offsets_table()
    wide = jnp.repeat(table, TOK, axis=1)
    bias = jnp.einsum("hr,icr->hic", rel_bias, wide, precision=lax.Precision.HIGHEST)
    clips = there[:, 3 * HEADS, :, 0].astype(F32).reshape(ROWS)
    prob, mid = pl.pallas_call(
        temporal_a_kernel,
        grid=(HEADS,),
        out_shape=(
            jax.ShapeDtypeStruct((HEADS, ROWS, ROWS), F32),
            jax.ShapeDtypeStruct((SEQ, HEADS, TOK, DIM), BF),
        ),
        in_specs=[
            tile_spec(0),
            tile_spec(HEADS),
            tile_spec(2 * HEADS),
            pl.BlockSpec((1, SEQ, ROWS), lambda h: (h, 0, 0)),
            pl.BlockSpec((ROWS, 1), lambda h: (0, 0)),
            pl.BlockSpec((1, ROWS), lambda h: (0, 0)),
        ],
        out_specs=(PROB, tile_spec(0)),
        compiler_params=PARAMS,
        cost_estimate=cost(2, 12),
        name="temporal_a",
    )(there, there, there, bias, clips[:, None], clips[None, :])
    so, mid = lax.optimization_barrier((so, mid))
    grad_mid = exchange(mid)

    back, score_rows = pl.pallas_call(
        temporal_b_kernel,
        grid=(HEADS,),
        out_shape=(
            jax.ShapeDtypeStruct((SEQ, 3 * HEADS, TOK, DIM), BF),
            jax.ShapeDtypeStruct((HEADS, SEQ, ROWS), F32),
        ),
        in_specs=[tile_spec(0), tile_spec(HEADS), tile_spec(2 * HEADS), tile_spec(0), PROB],
        out_specs=(
            pl.BlockSpec((SEQ, 3, TOK, DIM), lambda h: (0, h, 0, 0)),
            pl.BlockSpec((1, SEQ, ROWS), lambda h: (h, 0, 0)),
        ),
        compiler_params=PARAMS,
        cost_estimate=cost(4, 12),
        name="temporal_b",
    )(there, there, there, so, prob)
    grad_mid, back = lax.optimization_barrier((grad_mid, back))
    returned = exchange(back)

    terms = jnp.einsum("hic,icr->hr", score_rows, wide, precision=lax.Precision.HIGHEST)
    total_bias = bias_sum(terms)

    grad_qs, grad_ks, grad_vs = pl.pallas_call(
        spatial_bwd_kernel,
        grid=(HEADS,),
        out_shape=(frame_shape(),) * 3,
        in_specs=[FRAME] * 3 + [tile_spec(0)],
        out_specs=(FRAME,) * 3,
        compiler_params=PARAMS,
        cost_estimate=cost(5, 7),
        name="spatial_bwd",
    )(q_spatial, k_spatial, v_spatial, grad_mid)

    result, grad_qt, grad_kt = pl.pallas_call(
        unpack_kernel,
        out_shape=(frame_shape(),) * 3,
        in_specs=[vmem],
        out_specs=(vmem,) * 3,
        compiler_params=PARAMS,
        name="unpack",
    )(returned)
    return result, grad_qs, grad_ks, grad_vs, grad_qt, grad_kt, total_bias


def solution(mesh):
    frames = P(("grp", "seq"), None, None)
    return jax.shard_map(
        per_device,
        mesh=mesh,
        in_specs=(frames,) * 5 + (P(), P("grp", "seq"), frames),
        out_specs=(frames,) * 6 + (P(),),
        check_vma=False,
    )
```

```python
import functools

import jax
import jax.numpy as jnp
from jax import lax
from jax.experimental import pallas as pl
from jax.experimental.pallas import tpu as pltpu
from jax.sharding import PartitionSpec as P

HEADS = 12
DIM = 128
SEQ = 16
CHIPS = 8
TOK = 16
ROWS = SEQ * TOK
WIDTH = HEADS * DIM
SCALE = DIM ** (-0.5)
NEG = -1e30
BF = jnp.bfloat16
F32 = jnp.float32
PARAMS = pltpu.CompilerParams(vmem_limit_bytes=40 * 1024 * 1024)
VMEM = pl.BlockSpec(memory_space=pltpu.VMEM)
SMEM = pl.BlockSpec(memory_space=pltpu.SMEM)

SHIFTS = (2, -2, 3, -3, 1, -1)
ORDER = (0,) + SHIFTS + (4,)


def units_in(shift):
    return 3 if abs(shift) == 2 else 2


def mm(left, right):
    return lax.dot_general(left, right, (((1,), (0,)), ((), ())), preferred_element_type=F32)


def mm_nt(left, right):
    return lax.dot_general(left, right, (((1,), (1,)), ((), ())), preferred_element_type=F32)


def mm_tn(left, right):
    return lax.dot_general(left, right, (((0,), (0,)), ((), ())), preferred_element_type=F32)


def softmax(scores):
    raw = jnp.exp(scores - jnp.max(scores, axis=-1, keepdims=True))
    return raw / jnp.sum(raw, axis=-1, keepdims=True)


def cost(products, rw):
    return pl.CostEstimate(
        flops=2 * products * HEADS * ROWS * ROWS * DIM,
        bytes_accessed=rw * ROWS * WIDTH * 2,
        transcendentals=HEADS * ROWS * ROWS,
    )


def units(n, tiles):
    return jax.ShapeDtypeStruct((n, tiles, TOK, DIM), BF)


def frame():
    return jax.ShapeDtypeStruct((1, ROWS, WIDTH), BF)


def call(kernel, name, inputs, outputs, scalars=0, estimate=None, scratch=()):
    return pl.pallas_call(
        kernel,
        out_shape=tuple(outputs),
        in_specs=[SMEM] * scalars + [VMEM] * (len(inputs) - scalars),
        out_specs=(VMEM,) * len(outputs),
        scratch_shapes=scratch,
        compiler_params=PARAMS,
        cost_estimate=estimate,
        name=name,
    )(*inputs)


def head(h):
    return slice(h * DIM, (h + 1) * DIM)


def range_row(chip, core):
    return pl.multiple_of((2 * (chip & (CHIPS - 1)) + core) * TOK, TOK)


def pack_kernel(pos_ref, clip_ref, q_ref, k_ref, up_ref, *outs):
    z, c = pos_ref[0], pos_ref[1]
    clip = jnp.full((TOK, DIM), clip_ref[0, 0], jnp.int32).astype(F32).astype(BF)

    def fill(out, unit, shift, core):
        row = range_row(z + shift, core)
        for i, ref in enumerate((q_ref, k_ref, up_ref)):
            for h in range(HEADS):
                out[unit, i * HEADS + h] = ref[0, pl.ds(row, TOK), head(h)]
        out[unit, 3 * HEADS] = clip

    for out, shift in zip(outs, SHIFTS + (0,)):
        fill(out, 0, shift, c)
        fill(out, 1, shift, 1 - c)
        if shift == 2:
            fill(out, 2, 4, c)
        if shift == -2:
            fill(out, 2, 4, 1 - c)


def spatial_fwd_kernel(pos_ref, q_ref, k_ref, v_ref, keep_ref, give_ref):
    z, first = pos_ref[0], pos_ref[1] == 0
    for h in range(HEADS):
        prob = softmax(mm_nt(q_ref[0, :, head(h)], k_ref[0, :, head(h)]) * SCALE)
        out = mm(prob.astype(BF), v_ref[0, :, head(h)])
        for chip in range(CHIPS):
            even = out[2 * chip * TOK:(2 * chip + 1) * TOK]
            odd = out[(2 * chip + 1) * TOK:(2 * chip + 2) * TOK]
            shift = (chip - z) & (CHIPS - 1)
            keep_ref[shift, h] = jnp.where(first, even, odd).astype(BF)
            give_ref[shift, h] = jnp.where(first, odd, even).astype(BF)


def merge_kernel(sign, tiles, keep_ref, got_ref, *outs):
    for out, shift in zip(outs, SHIFTS):
        at = (sign * shift) % CHIPS
        out[0] = keep_ref[at]
        out[1] = got_ref[at]
        if abs(shift) == 2:
            out[2] = (keep_ref if shift == 2 else got_ref)[4]


def give_kernel(own_ref, *refs):
    ins, relayed, out = refs[:6], refs[6], refs[7]
    out[0] = own_ref[1]
    for ref, shift in zip(ins, SHIFTS):
        out[shift % CHIPS] = ref[1]
    out[4] = relayed[0]


def rows_of(tile, firsts, seconds):
    parts = [ref[u, tile] for ref, u in firsts] + [ref[u, tile] for ref, u in seconds]
    return jnp.concatenate(parts, axis=0)


def there_slots(refs):
    own, six, relay, swapped = refs[0], refs[1:7], refs[7], refs[8]
    ins = dict(zip(SHIFTS, six))
    firsts = [(own, 0)]
    for d in range(1, CHIPS):
        s = d if d <= 4 else d - CHIPS
        firsts.append((relay, 0) if s == 4 else (ins[s], 0))
    return firsts, [(swapped, d) for d in range(CHIPS)]


def merged_slots(refs):
    own, swapped, six, relay_0, relay_1 = refs[0], refs[1], refs[2:8], refs[8], refs[9]
    ins = dict(zip(SHIFTS, six))
    firsts, seconds = [(own, 0)], [(swapped, 0)]
    for d in range(1, CHIPS):
        s = d if d <= 4 else d - CHIPS
        firsts.append((relay_0, 0) if s == 4 else (ins[s], 0))
        seconds.append((relay_1, 0) if s == 4 else (ins[s], 1))
    return firsts, seconds


def store_slots(out_keep, out_give, tile, value):
    for d in range(CHIPS):
        out_keep[d, tile] = value[d * TOK:(d + 1) * TOK].astype(BF)
        out_give[d, tile] = value[(CHIPS + d) * TOK:(CHIPS + d + 1) * TOK].astype(BF)


def temporal_a_kernel(*refs):
    slots = there_slots(refs[:9])
    bias_ref, ccol_ref, crow_ref, prob_ref, keep_ref, give_ref = refs[9:]
    row = lax.broadcasted_iota(jnp.int32, (ROWS, ROWS), 0)
    col = lax.broadcasted_iota(jnp.int32, (ROWS, ROWS), 1)
    same = ((row & (TOK - 1)) == (col & (TOK - 1))) & (ccol_ref[...] == crow_ref[...])
    mask = jnp.where(same, 0.0, NEG)

    @pl.loop(0, HEADS)
    def _(h):
        q = rows_of(h, *slots)
        k = rows_of(HEADS + h, *slots)
        up = rows_of(2 * HEADS + h, *slots)
        bias = jnp.broadcast_to(bias_ref[h][:, None, :], (SEQ, TOK, ROWS)).reshape(ROWS, ROWS)
        prob = softmax((mm_nt(q, k) * SCALE + bias) + mask)
        prob_ref[h] = prob
        store_slots(keep_ref, give_ref, h, mm_tn(prob.astype(BF), up))


def temporal_b_kernel(*refs):
    slots = there_slots(refs[:9])
    so_slots = merged_slots(refs[9:19])
    prob_ref, keep_ref, give_ref, bias_ref = refs[19:]

    @pl.loop(0, HEADS)
    def _(h):
        q = rows_of(h, *slots)
        k = rows_of(HEADS + h, *slots)
        up = rows_of(2 * HEADS + h, *slots)
        so = rows_of(h, *so_slots)
        prob = prob_ref[h]
        store_slots(keep_ref, give_ref, h, mm(prob.astype(BF), so))
        grad_prob = mm_nt(up, so)
        score = prob * (grad_prob - jnp.sum(prob * grad_prob, axis=-1, keepdims=True))
        bias_ref[h] = jnp.sum(score.reshape(SEQ, TOK, ROWS), axis=1)
        low = (score * SCALE).astype(BF)
        store_slots(keep_ref, give_ref, HEADS + h, mm(low, k))
        store_slots(keep_ref, give_ref, 2 * HEADS + h, mm_tn(low, q))


def place(z, c, slots, tiles, store):
    firsts, seconds = slots
    for d in range(CHIPS):
        for (ref, unit), core in ((firsts[d], c), (seconds[d], 1 - c)):
            row = range_row(z + d, core)
            for tile in range(tiles):
                store(tile, row, ref[unit, tile])


def back_slots(refs):
    firsts, seconds = merged_slots(refs)
    turn = [(-d) % CHIPS for d in range(CHIPS)]
    return [firsts[d] for d in turn], [seconds[d] for d in turn]


def spatial_bwd_kernel(pos_ref, *refs):
    slots = back_slots(refs[:10])
    q_ref, k_ref, v_ref, gq_ref, gk_ref, gv_ref, up_ref = refs[10:]

    def store(tile, row, value):
        up_ref[pl.ds(row, TOK), head(tile)] = value

    place(pos_ref[0], pos_ref[1], slots, HEADS, store)
    for h in range(HEADS):
        q, k, v = q_ref[0, :, head(h)], k_ref[0, :, head(h)], v_ref[0, :, head(h)]
        up = up_ref[:, head(h)]
        prob = softmax(mm_nt(q, k) * SCALE)
        grad_prob = mm_nt(up, v)
        gv_ref[0, :, head(h)] = mm_tn(prob.astype(BF), up).astype(BF)
        row_dot = jnp.sum(prob * grad_prob, axis=-1, keepdims=True)
        low = (prob * (grad_prob - row_dot) * SCALE).astype(BF)
        gq_ref[0, :, head(h)] = mm(low, k).astype(BF)
        gk_ref[0, :, head(h)] = mm_tn(low, q).astype(BF)


def unpack_kernel(pos_ref, *refs):
    slots, outs = back_slots(refs[:10]), refs[10:]

    def store(tile, row, value):
        outs[tile // HEADS][0, pl.ds(row, TOK), head(tile % HEADS)] = value

    place(pos_ref[0], pos_ref[1], slots, 3 * HEADS, store)


def shift_chips(message, shift):
    perm = [(2 * z + c, 2 * ((z + shift) % CHIPS) + c) for z in range(CHIPS) for c in range(2)]
    return lax.ppermute(message, "seq", perm)


def swap_cores(message):
    return lax.ppermute(message, "seq", [(i, i ^ 1) for i in range(SEQ)])


def send(messages):
    got = [shift_chips(m, s) for m, s in zip(messages, SHIFTS)]
    relay_0 = shift_chips(got[0][2:], 2)
    relay_1 = shift_chips(got[1][2:], -2)
    return got, relay_0, relay_1


def merged(keep, got, sign, name):
    tiles = keep.shape[1]
    outs = [units(units_in(s), tiles) for s in SHIFTS]
    return call(functools.partial(merge_kernel, sign, tiles), name, [keep, got], outs)


def sum_of_four(terms, axis, step):
    size = lax.axis_size(axis)

    def partner(mask):
        return lax.ppermute(terms, axis, [(i, i ^ (mask * step)) for i in range(size)])

    return (terms + partner(1)) + (partner(2) + partner(3))


def bias_sum(terms):
    for axis, step in (("seq", 1), ("grp", 1), ("grp", 4), ("seq", 4)):
        if lax.axis_size(axis) > step:
            terms = sum_of_four(terms, axis, step)
    return terms


def offsets_table(frames):
    offset = frames[:, None] - frames[None, :] + (SEQ - 1)
    slots = jnp.arange(2 * SEQ - 1, dtype=jnp.int32)
    return (offset[:, :, None] == slots[None, None, :]).astype(F32)


def per_device(
    q_spatial, k_spatial, v_spatial, q_temporal, k_temporal, rel_bias, clip_ids, cotangent
):
    index = lax.axis_index("seq")
    z, c = index // 2, index % 2
    pos = jnp.stack([z, c]).astype(jnp.int32)
    back_by = (z - jnp.arange(CHIPS, dtype=jnp.int32)) % CHIPS
    frames = jnp.concatenate([2 * back_by + c, 2 * back_by + 1 - c])
    wide = jnp.repeat(offsets_table(frames), TOK, axis=1)
    bias = jnp.einsum("hr,icr->hic", rel_bias, wide, precision=lax.Precision.HIGHEST)

    tiles = 3 * HEADS + 1
    *messages, own = call(
        pack_kernel,
        "pack",
        [pos, clip_ids, q_temporal, k_temporal, cotangent],
        [units(units_in(s), tiles) for s in SHIFTS] + [units(2, tiles)],
        scalars=2,
    )
    got, relay_0, relay_1 = send(messages)
    (give,) = call(give_kernel, "give", [own, *got, relay_1], [units(CHIPS, tiles)])
    swapped = swap_cores(give)
    there = [own, *got, relay_0, swapped]

    keep_so, give_so = call(
        spatial_fwd_kernel,
        "spatial_fwd",
        [pos, q_spatial, k_spatial, v_spatial],
        [units(CHIPS, HEADS)] * 2,
        scalars=1,
        estimate=cost(2, 4),
    )
    got_so = swap_cores(give_so)
    so_messages = merged(keep_so, got_so, 1, "merge_so")
    so_messages, got, relay_0, relay_1 = lax.optimization_barrier(
        (so_messages, got, relay_0, relay_1)
    )
    so_in, so_0, so_1 = send(so_messages)
    so = [keep_so, got_so, *so_in, so_0, so_1]

    def clip_of(ref, unit):
        return ref[unit, 3 * HEADS, :, 0]

    firsts, seconds = there_slots(there)
    clips = jnp.concatenate([clip_of(*s) for s in firsts + seconds]).astype(F32)
    prob, keep_mid, give_mid = call(
        temporal_a_kernel,
        "temporal_a",
        [*there, bias, clips[:, None], clips[None, :]],
        [jax.ShapeDtypeStruct((HEADS, ROWS, ROWS), F32)] + [units(CHIPS, HEADS)] * 2,
        estimate=cost(2, 12),
    )
    got_mid = swap_cores(give_mid)
    mid_messages = merged(keep_mid, got_mid, -1, "merge_mid")
    mid_messages, so = lax.optimization_barrier((mid_messages, so))
    mid_in, mid_0, mid_1 = send(mid_messages)
    mid = [keep_mid, got_mid, *mid_in, mid_0, mid_1]

    keep_back, give_back, score_rows = call(
        temporal_b_kernel,
        "temporal_b",
        [*there, *so, prob],
        [units(CHIPS, 3 * HEADS)] * 2 + [jax.ShapeDtypeStruct((HEADS, SEQ, ROWS), F32)],
        estimate=cost(4, 12),
    )
    terms = jnp.einsum("hic,icr->hr", score_rows, wide, precision=lax.Precision.HIGHEST)
    total_bias = bias_sum(terms)
    got_back = swap_cores(give_back)
    back_messages = merged(keep_back, got_back, -1, "merge_back")
    back_messages, mid = lax.optimization_barrier((back_messages, mid))
    back_in, back_0, back_1 = send(back_messages)
    back = [keep_back, got_back, *back_in, back_0, back_1]

    grad_qs, grad_ks, grad_vs = call(
        spatial_bwd_kernel,
        "spatial_bwd",
        [pos, *mid, q_spatial, k_spatial, v_spatial],
        [frame()] * 3,
        scalars=1,
        estimate=cost(5, 7),
        scratch=[pltpu.VMEM((ROWS, WIDTH), BF)],
    )
    result, grad_qt, grad_kt = call(
        unpack_kernel, "unpack", [pos, *back], [frame()] * 3, scalars=1
    )
    return result, grad_qs, grad_ks, grad_vs, grad_qt, grad_kt, total_bias


def solution(mesh):
    frames = P(("grp", "seq"), None, None)
    return jax.shard_map(
        per_device,
        mesh=mesh,
        in_specs=(frames,) * 5 + (P(), P("grp", "seq"), frames),
        out_specs=(frames,) * 6 + (P(),),
        check_vma=False,
    )
```

```python
import jax
import jax.numpy as jnp
from jax import lax
from jax.experimental import pallas as pl
from jax.experimental.pallas import tpu as pltpu
from jax.sharding import PartitionSpec as P

HEADS = 12
DIM = 128
SEQ = 16
CHIPS = 8
TOK = 16
ROWS = SEQ * TOK
WIDTH = HEADS * DIM
SCALE = DIM ** (-0.5)
NEG = -1e30
BF = jnp.bfloat16
F32 = jnp.float32
PARAMS = pltpu.CompilerParams(vmem_limit_bytes=48 * 1024 * 1024)
PARTS = 4
LONG = 10**12
VMEM = pl.BlockSpec(memory_space=pltpu.VMEM)
SMEM = pl.BlockSpec(memory_space=pltpu.SMEM)
HBM = pl.BlockSpec(memory_space=pltpu.HBM)


def mm(left, right):
    return lax.dot_general(left, right, (((1,), (0,)), ((), ())), preferred_element_type=F32)


def mm_nt(left, right):
    return lax.dot_general(left, right, (((1,), (1,)), ((), ())), preferred_element_type=F32)


def mm_tn(left, right):
    return lax.dot_general(left, right, (((0,), (0,)), ((), ())), preferred_element_type=F32)


def softmax(scores):
    raw = jnp.exp(scores - jnp.max(scores, axis=-1, keepdims=True))
    return raw / jnp.sum(raw, axis=-1, keepdims=True)


def units(n, tiles):
    return jax.ShapeDtypeStruct((n, tiles, TOK, DIM), BF)


def frame():
    return jax.ShapeDtypeStruct((1, ROWS, WIDTH), BF)


def probs():
    return jax.ShapeDtypeStruct((HEADS, ROWS, ROWS), F32)


def head(h):
    return slice(h * DIM, (h + 1) * DIM)


def rows_of(ref, tile):
    return ref[:, tile].reshape(ROWS, DIM)


SHIFTS = (1, -1, 3, -3, 2, -2, 4)
SLOTS = tuple((d, x) for x in range(2) for d in range(CHIPS))


def slot_rows(frames_ref, ref, tile):
    return jnp.concatenate([ref[frames_ref[s], tile] for s in range(SEQ)], axis=0)


def put_slots(frames_ref, ref, tile, value):
    low = value.astype(BF)
    for s in range(SEQ):
        ref[frames_ref[s], tile] = low[s * TOK:(s + 1) * TOK]


def pack_kernel(clip_ref, q_ref, k_ref, up_ref, out_ref, held, sems):
    copies = []
    size = ROWS // PARTS
    for i, ref in enumerate((q_ref, k_ref, up_ref)):
        for part in range(PARTS):
            rows = pl.ds(part * size, size)
            copies.append(
                pltpu.make_async_copy(ref.at[0, rows], held.at[i, rows], sems.at[i, part])
            )
            copies[-1].start()
    clip = jnp.full((SEQ, TOK, DIM), clip_ref[0, 0], jnp.int32).astype(F32).astype(BF)
    out_ref[:, 3 * HEADS] = clip
    units_of = SEQ // PARTS
    for i in range(3):
        for part in range(PARTS):
            copies[i * PARTS + part].wait()
            for h in range(HEADS):
                block = held[i, part * size:(part + 1) * size, head(h)]
                out_ref[part * units_of:(part + 1) * units_of, i * HEADS + h] = block.reshape(
                    units_of, TOK, DIM
                )


def spatial_fwd_kernel(pos_ref, q_ref, k_ref, v_ref, keep_ref, give_ref, prob_ref):
    z, first = pos_ref[0], pos_ref[1] == 0
    for h in range(HEADS):
        prob = softmax(mm_nt(q_ref[0, :, head(h)], k_ref[0, :, head(h)]) * SCALE)
        prob_ref[h] = prob
        out = mm(prob.astype(BF), v_ref[0, :, head(h)])
        for chip in range(CHIPS):
            even = out[2 * chip * TOK:(2 * chip + 1) * TOK]
            odd = out[(2 * chip + 1) * TOK:(2 * chip + 2) * TOK]
            shift = (chip - z) & (CHIPS - 1)
            keep_ref[shift, h] = jnp.where(first, even, odd).astype(BF)
            give_ref[shift, h] = jnp.where(first, odd, even).astype(BF)


def merge_kernel(keep_ref, got_ref, *outs):
    for out, shift in zip(outs, (0,) + SHIFTS):
        out[0] = keep_ref[shift % CHIPS]
        out[1] = got_ref[shift % CHIPS]


def spatial_bwd_kernel(q_ref, k_ref, v_ref, prob_ref, mid_ref, gq_ref, gk_ref, gv_ref):
    for h in range(HEADS):
        q, k, v = q_ref[0, :, head(h)], k_ref[0, :, head(h)], v_ref[0, :, head(h)]
        up = rows_of(mid_ref, h)
        prob = prob_ref[h]
        grad_prob = mm_nt(up, v)
        gv_ref[0, :, head(h)] = mm_tn(prob.astype(BF), up).astype(BF)
        row_dot = jnp.sum(prob * grad_prob, axis=-1, keepdims=True)
        low = (prob * (grad_prob - row_dot) * SCALE).astype(BF)
        gq_ref[0, :, head(h)] = mm(low, k).astype(BF)
        gk_ref[0, :, head(h)] = mm_tn(low, q).astype(BF)


def temporal_a_kernel(frames_ref, in_ref, bias_ref, prob_ref, mid_ref):
    row = lax.broadcasted_iota(jnp.int32, (ROWS, ROWS), 0)
    col = lax.broadcasted_iota(jnp.int32, (ROWS, ROWS), 1)
    clip = slot_rows(frames_ref, in_ref, 3 * HEADS).astype(F32)
    other = clip.T
    same = (row & (TOK - 1)) == (col & (TOK - 1))
    same &= jnp.concatenate([clip] * 2, axis=1) == jnp.concatenate([other] * 2, axis=0)
    mask = jnp.where(same, 0.0, NEG)
    for h in range(HEADS):
        q, k, up = (slot_rows(frames_ref, in_ref, i * HEADS + h) for i in range(3))
        bias = jnp.broadcast_to(bias_ref[h][:, None, :], (SEQ, TOK, ROWS)).reshape(ROWS, ROWS)
        prob = softmax((mm_nt(q, k) * SCALE + bias) + mask)
        prob_ref[h] = prob
        put_slots(frames_ref, mid_ref, h, mm_tn(prob.astype(BF), up))


def temporal_b_kernel(frames_ref, in_ref, prob_ref, *refs):
    so_refs, (out_ref, bias_ref) = dict(zip((0,) + SHIFTS, refs)), refs[-2:]
    so_at = [(so_refs[d if d <= CHIPS // 2 else d - CHIPS], x) for d, x in SLOTS]
    for h in range(HEADS):
        q, k, up = (slot_rows(frames_ref, in_ref, i * HEADS + h) for i in range(3))
        so = jnp.concatenate([ref[x, h] for ref, x in so_at], axis=0)
        prob = prob_ref[h]
        grad_prob = mm_nt(up, so)
        put_slots(frames_ref, out_ref, h, mm(prob.astype(BF), so))
        score = prob * (grad_prob - jnp.sum(prob * grad_prob, axis=-1, keepdims=True))
        bias_ref[h] = jnp.sum(score.reshape(SEQ, TOK, ROWS), axis=1)
        low = (score * SCALE).astype(BF)
        put_slots(frames_ref, out_ref, HEADS + h, mm(low, k))
        put_slots(frames_ref, out_ref, 2 * HEADS + h, mm_tn(low, q))


def add_tile_kernel(tile_ref, in_ref, out_ref, sem):
    copies = [
        pltpu.make_async_copy(tile_ref, out_ref.at[u, 3 * HEADS], sem.at[u]) for u in range(SEQ)
    ]
    for copy in copies:
        copy.start()
    for copy in copies:
        copy.wait()


def unpack_kernel(in_ref, *outs):
    for tile in range(3 * HEADS):
        outs[tile // HEADS][0, :, head(tile % HEADS)] = rows_of(in_ref, tile)
    outs[3][...] = jnp.sum(in_ref[:, 3 * HEADS].astype(F32), axis=0)


def call(kernel, name, specs, inputs, outputs, scratch=(), estimate=1000, params=PARAMS, **more):
    return pl.pallas_call(
        kernel,
        out_shape=tuple(outputs),
        in_specs=specs,
        out_specs=(VMEM,) * len(outputs),
        scratch_shapes=scratch,
        compiler_params=params,
        cost_estimate=pl.CostEstimate(flops=estimate, bytes_accessed=1000, transcendentals=0),
        name=name,
        **more,
    )(*inputs)


def exchange(packed):
    return lax.all_to_all(packed, "seq", split_axis=0, concat_axis=0, tiled=True)


def pair(terms, axis, mask):
    size = lax.axis_size(axis)
    return lax.ppermute(terms, axis, [(i, i ^ mask) for i in range(size)])


def sum_of_four(terms, axis, step):
    one, two, three = (pair(terms, axis, step * mask) for mask in (1, 2, 3))
    return (terms + one) + (two + three)


def move(message, s, x):
    perm = [(2 * z + c, 2 * ((z + s) % CHIPS) + (c ^ x)) for z in range(CHIPS) for c in range(2)]
    return lax.ppermute(message, "seq", perm)


def bfloat_parts(terms):
    parts = []
    for _ in range(3):
        part = lax.reduce_precision(terms, 8, 7)
        parts.append(jnp.pad(part, ((0, TOK - HEADS), (0, 1))))
        terms = terms - part
    return jnp.pad(jnp.concatenate(parts, axis=1), ((0, 0), (0, DIM - 96))).astype(BF)


def offsets_table(frames):
    offset = frames[:, None] - frames[None, :] + (SEQ - 1)
    slots = jnp.arange(2 * SEQ - 1, dtype=jnp.int32)
    return (offset[:, :, None] == slots[None, None, :]).astype(F32)


def per_device(
    q_spatial, k_spatial, v_spatial, q_temporal, k_temporal, rel_bias, clip_ids, cotangent
):
    index = lax.axis_index("seq").astype(jnp.int32)
    z, c = index >> 1, index & 1
    pos = jnp.stack([z, c])
    away = jnp.array([d for d, x in SLOTS], jnp.int32)
    swapped = jnp.array([x for d, x in SLOTS], jnp.int32)
    frames = 2 * ((z - away) & (CHIPS - 1)) + (c ^ swapped)

    tiles = 3 * HEADS + 1
    (packed,) = call(
        pack_kernel,
        "pack",
        [SMEM] + [HBM] * 3,
        [clip_ids, q_temporal, k_temporal, cotangent],
        [units(SEQ, tiles)],
        [pltpu.VMEM((3, ROWS, WIDTH), BF), pltpu.SemaphoreType.DMA((3, PARTS))],
        params=pltpu.CompilerParams(vmem_limit_bytes=56 * 1024 * 1024),
    )
    there = exchange(packed)

    spatial = [q_spatial, k_spatial, v_spatial]
    spatial, rel_bias, frames, _ = lax.optimization_barrier((spatial, rel_bias, frames, packed))
    wide = jnp.repeat(offsets_table(frames), TOK, axis=1)
    bias = jnp.einsum("hr,icr->hic", rel_bias, wide, precision=lax.Precision.HIGHEST)
    keep_so, give_so, sp_prob = call(
        spatial_fwd_kernel,
        "spatial_fwd",
        [SMEM] + [VMEM] * 3,
        [pos, *spatial],
        [units(CHIPS, HEADS)] * 2 + [probs()],
    )
    got_so = move(give_so, 0, 1)
    stay, *messages = call(
        merge_kernel, "merge", [VMEM] * 2, [keep_so, got_so], [units(2, HEADS)] * CHIPS
    )
    so = [stay, *(move(m, s, 0) for m, s in zip(messages, SHIFTS))]

    there, _, bias = lax.optimization_barrier((there, messages, bias))
    prob, mid = call(
        temporal_a_kernel,
        "temporal_a",
        [SMEM] + [VMEM] * 2,
        [frames, there, bias],
        [probs(), units(SEQ, HEADS)],
    )
    grad_mid = exchange(mid)

    back, score_rows = call(
        temporal_b_kernel,
        "temporal_b",
        [SMEM] + [VMEM] * (2 + CHIPS),
        [frames, there, prob, *so],
        [units(SEQ, tiles), jax.ShapeDtypeStruct((HEADS, SEQ, ROWS), F32)],
        estimate=LONG,
    )
    terms = jnp.einsum("hic,icr->hr", score_rows, wide, precision=lax.Precision.HIGHEST)
    terms = sum_of_four(sum_of_four(terms, "grp", 1), "grp", 4)
    (back,) = call(
        add_tile_kernel,
        "add_tile",
        [VMEM] * 2,
        [bfloat_parts(terms), back],
        [units(SEQ, tiles)],
        [pltpu.SemaphoreType.DMA((SEQ,))],
        input_output_aliases={1: 0},
    )
    grad_mid, back = lax.optimization_barrier((grad_mid, back))
    returned = exchange(back)

    grad_qs, grad_ks, grad_vs = call(
        spatial_bwd_kernel, "spatial_bwd", [VMEM] * 5, [*spatial, sp_prob, grad_mid], [frame()] * 3
    )
    result, grad_qt, grad_kt, total = call(
        unpack_kernel,
        "unpack",
        [VMEM],
        [returned],
        [frame()] * 3 + [jax.ShapeDtypeStruct((TOK, DIM), F32)],
    )
    total = total[:HEADS]
    total_bias = total[:, :31] + total[:, 32:63] + total[:, 64:95]
    return result, grad_qs, grad_ks, grad_vs, grad_qt, grad_kt, total_bias


def solution(mesh):
    frames = P(("grp", "seq"), None, None)
    return jax.shard_map(
        per_device,
        mesh=mesh,
        in_specs=(frames,) * 5 + (P(), P("grp", "seq"), frames),
        out_specs=(frames,) * 6 + (P(),),
        check_vma=False,
    )
```

```python
import jax
import jax.numpy as jnp
from jax import lax
from jax.experimental import pallas as pl
from jax.experimental.pallas import tpu as pltpu
from jax.sharding import PartitionSpec as P

HEADS = 12
DIM = 128
SEQ = 16
CHIPS = 8
TOK = 16
ROWS = SEQ * TOK
WIDTH = HEADS * DIM
SCALE = DIM ** (-0.5)
NEG = -1e30
BF = jnp.bfloat16
F32 = jnp.float32
PARAMS = pltpu.CompilerParams(vmem_limit_bytes=48 * 1024 * 1024)
PARTS = 4
LONG = 10**12
VMEM = pl.BlockSpec(memory_space=pltpu.VMEM)
SMEM = pl.BlockSpec(memory_space=pltpu.SMEM)
HBM = pl.BlockSpec(memory_space=pltpu.HBM)


def mm(left, right):
    return lax.dot_general(left, right, (((1,), (0,)), ((), ())), preferred_element_type=F32)


def mm_nt(left, right):
    return lax.dot_general(left, right, (((1,), (1,)), ((), ())), preferred_element_type=F32)


def mm_tn(left, right):
    return lax.dot_general(left, right, (((0,), (0,)), ((), ())), preferred_element_type=F32)


def softmax(scores):
    raw = jnp.exp(scores - jnp.max(scores, axis=-1, keepdims=True))
    return raw / jnp.sum(raw, axis=-1, keepdims=True)


def units(n, tiles):
    return jax.ShapeDtypeStruct((n, tiles, TOK, DIM), BF)


def frame():
    return jax.ShapeDtypeStruct((1, ROWS, WIDTH), BF)


def probs():
    return jax.ShapeDtypeStruct((HEADS, ROWS, ROWS), F32)


def range_row(chip, core):
    return pl.multiple_of((2 * (chip & (CHIPS - 1)) + core) * TOK, TOK)


def head(h):
    return slice(h * DIM, (h + 1) * DIM)


def rows_of(ref, tile):
    return ref[:, tile].reshape(ROWS, DIM)


SHIFTS = (1, -1, 3, -3, 2, -2, 4)
SLOTS = tuple((d, x) for x in range(2) for d in range(CHIPS))


def slot_rows(frames_ref, ref, tile):
    return jnp.concatenate([ref[frames_ref[s], tile] for s in range(SEQ)], axis=0)


def put_pairs(keep_ref, give_ref, tile, value):
    low = value.astype(BF)
    for d in range(CHIPS):
        keep_ref[d, tile] = low[d * TOK:(d + 1) * TOK]
        give_ref[d, tile] = low[(CHIPS + d) * TOK:(CHIPS + d + 1) * TOK]


def put_slots(frames_ref, ref, tile, value):
    low = value.astype(BF)
    for s in range(SEQ):
        ref[frames_ref[s], tile] = low[s * TOK:(s + 1) * TOK]


def pack_kernel(clip_ref, q_ref, k_ref, up_ref, out_ref, held, sems):
    copies = []
    size = ROWS // PARTS
    for i, ref in enumerate((q_ref, k_ref, up_ref)):
        for part in range(PARTS):
            rows = pl.ds(part * size, size)
            copies.append(
                pltpu.make_async_copy(ref.at[0, rows], held.at[i, rows], sems.at[i, part])
            )
            copies[-1].start()
    clip = jnp.full((SEQ, TOK, DIM), clip_ref[0, 0], jnp.int32).astype(F32).astype(BF)
    out_ref[:, 3 * HEADS] = clip
    units_of = SEQ // PARTS
    for i in range(3):
        for part in range(PARTS):
            copies[i * PARTS + part].wait()
            for h in range(HEADS):
                block = held[i, part * size:(part + 1) * size, head(h)]
                out_ref[part * units_of:(part + 1) * units_of, i * HEADS + h] = block.reshape(
                    units_of, TOK, DIM
                )


def spatial_fwd_kernel(pos_ref, q_ref, k_ref, v_ref, keep_ref, give_ref, prob_ref):
    z, first = pos_ref[0], pos_ref[1] == 0
    for h in range(HEADS):
        prob = softmax(mm_nt(q_ref[0, :, head(h)], k_ref[0, :, head(h)]) * SCALE)
        prob_ref[h] = prob
        out = mm(prob.astype(BF), v_ref[0, :, head(h)])
        for chip in range(CHIPS):
            even = out[2 * chip * TOK:(2 * chip + 1) * TOK]
            odd = out[(2 * chip + 1) * TOK:(2 * chip + 2) * TOK]
            shift = (chip - z) & (CHIPS - 1)
            keep_ref[shift, h] = jnp.where(first, even, odd).astype(BF)
            give_ref[shift, h] = jnp.where(first, odd, even).astype(BF)


def merge_kernel(keep_ref, got_ref, *outs):
    for out, shift in zip(outs, (0,) + SHIFTS):
        out[0] = keep_ref[shift % CHIPS]
        out[1] = got_ref[shift % CHIPS]


def merge_last_kernel(tile_ref, keep_ref, got_ref, *outs):
    for out, shift in zip(outs, (0,) + SHIFTS):
        out[:HEADS] = keep_ref[-shift % CHIPS]
        out[HEADS:2 * HEADS] = got_ref[-shift % CHIPS]
        out[2 * HEADS] = tile_ref[...]


def pair_rows(pos_ref, shift):
    z, c = pos_ref[0], pos_ref[1]
    return range_row(z - shift, c), range_row(z - shift, 1 - c)


def spatial_bwd_kernel(q_ref, k_ref, v_ref, prob_ref, mid_ref, gq_ref, gk_ref, gv_ref):
    for h in range(HEADS):
        q, k, v = q_ref[0, :, head(h)], k_ref[0, :, head(h)], v_ref[0, :, head(h)]
        up = rows_of(mid_ref, h)
        prob = prob_ref[h]
        grad_prob = mm_nt(up, v)
        gv_ref[0, :, head(h)] = mm_tn(prob.astype(BF), up).astype(BF)
        row_dot = jnp.sum(prob * grad_prob, axis=-1, keepdims=True)
        low = (prob * (grad_prob - row_dot) * SCALE).astype(BF)
        gq_ref[0, :, head(h)] = mm(low, k).astype(BF)
        gk_ref[0, :, head(h)] = mm_tn(low, q).astype(BF)


def temporal_a_kernel(frames_ref, in_ref, bias_ref, prob_ref, mid_ref):
    row = lax.broadcasted_iota(jnp.int32, (ROWS, ROWS), 0)
    col = lax.broadcasted_iota(jnp.int32, (ROWS, ROWS), 1)
    clip = slot_rows(frames_ref, in_ref, 3 * HEADS).astype(F32)
    other = clip.T
    same = (row & (TOK - 1)) == (col & (TOK - 1))
    same &= jnp.concatenate([clip] * 2, axis=1) == jnp.concatenate([other] * 2, axis=0)
    mask = jnp.where(same, 0.0, NEG)
    for h in range(HEADS):
        q, k, up = (slot_rows(frames_ref, in_ref, i * HEADS + h) for i in range(3))
        bias = jnp.broadcast_to(bias_ref[h][:, None, :], (SEQ, TOK, ROWS)).reshape(ROWS, ROWS)
        prob = softmax((mm_nt(q, k) * SCALE + bias) + mask)
        prob_ref[h] = prob
        put_slots(frames_ref, mid_ref, h, mm_tn(prob.astype(BF), up))


def temporal_b_kernel(frames_ref, in_ref, prob_ref, *refs):
    so_refs, (out_ref, keep_ref, give_ref, bias_ref) = dict(zip((0,) + SHIFTS, refs)), refs[-4:]
    so_at = [(so_refs[d if d <= CHIPS // 2 else d - CHIPS], x) for d, x in SLOTS]
    for h in range(HEADS):
        q, k, up = (slot_rows(frames_ref, in_ref, i * HEADS + h) for i in range(3))
        so = jnp.concatenate([ref[x, h] for ref, x in so_at], axis=0)
        prob = prob_ref[h]
        grad_prob = mm_nt(up, so)
        put_slots(frames_ref, out_ref, h, mm(prob.astype(BF), so))
        score = prob * (grad_prob - jnp.sum(prob * grad_prob, axis=-1, keepdims=True))
        bias_ref[h] = jnp.sum(score.reshape(SEQ, TOK, ROWS), axis=1)
        low = (score * SCALE).astype(BF)
        put_slots(frames_ref, out_ref, HEADS + h, mm(low, k))
        put_pairs(keep_ref, give_ref, h, mm_tn(low, q))


def unpack_kernel(in_ref, *outs):
    for tile in range(2 * HEADS):
        outs[tile // HEADS][0, :, head(tile % HEADS)] = rows_of(in_ref, tile)


def finish_kernel(pos_ref, *refs):
    messages, (gk_ref, bias_ref) = refs[:CHIPS], refs[CHIPS:]
    for ref, shift in zip(messages, (0,) + SHIFTS):
        for x, row in enumerate(pair_rows(pos_ref, shift)):
            for h in range(HEADS):
                gk_ref[0, pl.ds(row, TOK), head(h)] = ref[x * HEADS + h]
    z = pos_ref[0]
    total = jnp.zeros((TOK, DIM), F32)
    for chip in range(CHIPS):
        for ref, shift in zip(messages, (0,) + SHIFTS):
            mine = ((z - shift) & (CHIPS - 1)) == chip
            total += jnp.where(mine, ref[2 * HEADS].astype(F32), 0.0)
    total = total + pltpu.roll(total, DIM - 32, 1) + pltpu.roll(total, DIM - 64, 1)
    bias_ref[...] = total[:HEADS, :2 * SEQ - 1]


def call(kernel, name, specs, inputs, outputs, scratch=(), estimate=1000, params=PARAMS, **more):
    return pl.pallas_call(
        kernel,
        out_shape=tuple(outputs),
        in_specs=specs,
        out_specs=(VMEM,) * len(outputs),
        scratch_shapes=scratch,
        compiler_params=params,
        cost_estimate=pl.CostEstimate(flops=estimate, bytes_accessed=1000, transcendentals=0),
        name=name,
        **more,
    )(*inputs)


def exchange(packed):
    return lax.all_to_all(packed, "seq", split_axis=0, concat_axis=0, tiled=True)


def pair(terms, axis, mask):
    size = lax.axis_size(axis)
    return lax.ppermute(terms, axis, [(i, i ^ mask) for i in range(size)])


def sum_of_four(terms, axis, step):
    one, two, three = (pair(terms, axis, step * mask) for mask in (1, 2, 3))
    return (terms + one) + (two + three)


def move(message, s, x):
    perm = [(2 * z + c, 2 * ((z + s) % CHIPS) + (c ^ x)) for z in range(CHIPS) for c in range(2)]
    return lax.ppermute(message, "seq", perm)


def sent(messages):
    return [messages[0], *(move(m, s, 0) for m, s in zip(messages[1:], SHIFTS))]


def bfloat_parts(terms):
    parts = []
    for _ in range(3):
        part = lax.reduce_precision(terms, 8, 7)
        parts.append(jnp.pad(part, ((0, TOK - HEADS), (0, 1))))
        terms = terms - part
    return jnp.pad(jnp.concatenate(parts, axis=1), ((0, 0), (0, DIM - 96))).astype(BF)


def offsets_table(frames):
    offset = frames[:, None] - frames[None, :] + (SEQ - 1)
    slots = jnp.arange(2 * SEQ - 1, dtype=jnp.int32)
    return (offset[:, :, None] == slots[None, None, :]).astype(F32)


def per_device(
    q_spatial, k_spatial, v_spatial, q_temporal, k_temporal, rel_bias, clip_ids, cotangent
):
    index = lax.axis_index("seq").astype(jnp.int32)
    z, c = index >> 1, index & 1
    pos = jnp.stack([z, c])
    away = jnp.array([d for d, x in SLOTS], jnp.int32)
    swapped = jnp.array([x for d, x in SLOTS], jnp.int32)
    frames = 2 * ((z - away) & (CHIPS - 1)) + (c ^ swapped)

    tiles = 3 * HEADS + 1
    (packed,) = call(
        pack_kernel,
        "pack",
        [SMEM] + [HBM] * 3,
        [clip_ids, q_temporal, k_temporal, cotangent],
        [units(SEQ, tiles)],
        [pltpu.VMEM((3, ROWS, WIDTH), BF), pltpu.SemaphoreType.DMA((3, PARTS))],
        params=pltpu.CompilerParams(vmem_limit_bytes=56 * 1024 * 1024),
    )
    there = exchange(packed)

    spatial = [q_spatial, k_spatial, v_spatial]
    spatial, rel_bias, frames, _ = lax.optimization_barrier((spatial, rel_bias, frames, packed))
    wide = jnp.repeat(offsets_table(frames), TOK, axis=1)
    bias = jnp.einsum("hr,icr->hic", rel_bias, wide, precision=lax.Precision.HIGHEST)
    keep_so, give_so, sp_prob = call(
        spatial_fwd_kernel,
        "spatial_fwd",
        [SMEM] + [VMEM] * 3,
        [pos, *spatial],
        [units(CHIPS, HEADS)] * 2 + [probs()],
    )
    give_so, bias = lax.optimization_barrier((give_so, bias))
    got_so = move(give_so, 0, 1)
    so_messages = call(
        merge_kernel, "merge", [VMEM] * 2, [keep_so, got_so], [units(2, HEADS)] * CHIPS
    )
    so = sent(so_messages)

    there, _, bias = lax.optimization_barrier((there, so_messages, bias))
    prob, mid = call(
        temporal_a_kernel,
        "temporal_a",
        [SMEM] + [VMEM] * 2,
        [frames, there, bias],
        [probs(), units(SEQ, HEADS)],
    )
    grad_mid = exchange(mid)

    back, keep_back, give_back, score_rows = call(
        temporal_b_kernel,
        "temporal_b",
        [SMEM] + [VMEM] * (2 + CHIPS),
        [frames, there, prob, *so],
        [units(SEQ, 2 * HEADS)]
        + [units(CHIPS, HEADS)] * 2
        + [jax.ShapeDtypeStruct((HEADS, SEQ, ROWS), F32)],
        estimate=LONG,
    )
    back, _ = lax.optimization_barrier((back, grad_mid))
    returned = exchange(back)

    grad_qs, grad_ks, grad_vs = call(
        spatial_bwd_kernel,
        "spatial_bwd",
        [VMEM] * 5,
        [*spatial, sp_prob, grad_mid],
        [frame()] * 3,
        estimate=LONG,
    )
    score_rows, give_back, _ = lax.optimization_barrier((score_rows, give_back, grad_vs))
    terms = jnp.einsum("hic,icr->hr", score_rows, wide, precision=lax.Precision.HIGHEST)
    terms = terms + move(terms, 0, 1)
    terms = sum_of_four(sum_of_four(terms, "grp", 1), "grp", 4)
    got_back = move(give_back, 0, 1)
    tile = bfloat_parts(terms)
    last = call(
        merge_last_kernel,
        "merge_last",
        [VMEM] * 3,
        [tile, keep_back, got_back],
        [jax.ShapeDtypeStruct((2 * HEADS + 1, TOK, DIM), BF)] * CHIPS,
    )
    last = sent(last)
    result, grad_qt = call(unpack_kernel, "unpack", [VMEM], [returned], [frame()] * 2)
    grad_kt, total_bias = call(
        finish_kernel,
        "finish",
        [SMEM] + [VMEM] * CHIPS,
        [pos, *last],
        [frame(), jax.ShapeDtypeStruct((HEADS, 2 * SEQ - 1), F32)],
    )
    return result, grad_qs, grad_ks, grad_vs, grad_qt, grad_kt, total_bias


def solution(mesh):
    frames = P(("grp", "seq"), None, None)
    return jax.shard_map(
        per_device,
        mesh=mesh,
        in_specs=(frames,) * 5 + (P(), P("grp", "seq"), frames),
        out_specs=(frames,) * 6 + (P(),),
        check_vma=False,
    )
```

```python
import jax
import jax.numpy as jnp
from jax import lax
from jax.experimental import pallas as pl
from jax.experimental.pallas import tpu as pltpu
from jax.sharding import PartitionSpec as P

HEADS = 12
DIM = 128
SEQ = 16
CHIPS = 8
TOK = 16
ROWS = SEQ * TOK
WIDTH = HEADS * DIM
SCALE = DIM ** (-0.5)
NEG = -1e30
BF = jnp.bfloat16
F32 = jnp.float32
PARAMS = pltpu.CompilerParams(vmem_limit_bytes=48 * 1024 * 1024)
PARTS = 4
LONG = 10**12
VMEM = pl.BlockSpec(memory_space=pltpu.VMEM)
SMEM = pl.BlockSpec(memory_space=pltpu.SMEM)
HBM = pl.BlockSpec(memory_space=pltpu.HBM)


def mm(left, right):
    return lax.dot_general(left, right, (((1,), (0,)), ((), ())), preferred_element_type=F32)


def mm_nt(left, right):
    return lax.dot_general(left, right, (((1,), (1,)), ((), ())), preferred_element_type=F32)


def mm_tn(left, right):
    return lax.dot_general(left, right, (((0,), (0,)), ((), ())), preferred_element_type=F32)


def softmax(scores):
    raw = jnp.exp(scores - jnp.max(scores, axis=-1, keepdims=True))
    return raw / jnp.sum(raw, axis=-1, keepdims=True)


def units(n, tiles):
    return jax.ShapeDtypeStruct((n, tiles, TOK, DIM), BF)


def frame():
    return jax.ShapeDtypeStruct((1, ROWS, WIDTH), BF)


def probs():
    return jax.ShapeDtypeStruct((HEADS, ROWS, ROWS), F32)


def range_row(chip, core):
    return pl.multiple_of((2 * (chip & (CHIPS - 1)) + core) * TOK, TOK)


def head(h):
    return slice(h * DIM, (h + 1) * DIM)


def rows_of(ref, tile):
    return ref[:, tile].reshape(ROWS, DIM)


SHIFTS = (1, -1, 3, -3, 2, -2, 4)
SLOTS = tuple((d, x) for x in range(2) for d in range(CHIPS))


def slot_rows(frames_ref, ref, tile):
    return jnp.concatenate([ref[frames_ref[s], tile] for s in range(SEQ)], axis=0)


def put_pairs(keep_ref, give_ref, tile, value):
    low = value.astype(BF)
    for d in range(CHIPS):
        keep_ref[d, tile] = low[d * TOK:(d + 1) * TOK]
        give_ref[d, tile] = low[(CHIPS + d) * TOK:(CHIPS + d + 1) * TOK]


def put_slots(frames_ref, ref, tile, value):
    low = value.astype(BF)
    for s in range(SEQ):
        ref[frames_ref[s], tile] = low[s * TOK:(s + 1) * TOK]


def pack_kernel(clip_ref, q_ref, k_ref, up_ref, out_ref, held, made, sems, out_sems):
    copies = []
    size, units_of = ROWS // PARTS, SEQ // PARTS
    for i, ref in enumerate((q_ref, k_ref, up_ref)):
        for part in range(PARTS):
            rows = pl.ds(part * size, size)
            copies.append(
                pltpu.make_async_copy(ref.at[0, rows], held.at[i, rows], sems.at[i, part])
            )
            copies[-1].start()
    last = pl.ds(3 * HEADS, 1)
    clip = jnp.full((SEQ, TOK, DIM), clip_ref[0, 0], jnp.int32).astype(F32).astype(BF)
    made[:, 3 * HEADS] = clip
    outs = [pltpu.make_async_copy(made.at[:, last], out_ref.at[:, last], out_sems.at[3 * PARTS])]
    outs[-1].start()
    for i in range(3):
        for part in range(PARTS):
            copies[i * PARTS + part].wait()
            units = pl.ds(part * units_of, units_of)
            for h in range(HEADS):
                block = held[i, part * size:(part + 1) * size, head(h)]
                made[units, i * HEADS + h] = block.reshape(units_of, TOK, DIM)
            at = (units, pl.ds(i * HEADS, HEADS))
            outs.append(
                pltpu.make_async_copy(made.at[at], out_ref.at[at], out_sems.at[i * PARTS + part])
            )
            outs[-1].start()
    for copy in outs:
        copy.wait()


def spatial_fwd_kernel(pos_ref, q_ref, k_ref, v_ref, keep_ref, give_ref, prob_ref):
    z, first = pos_ref[0], pos_ref[1] == 0
    for h in range(HEADS):
        prob = softmax(mm_nt(q_ref[0, :, head(h)], k_ref[0, :, head(h)]) * SCALE)
        prob_ref[h] = prob
        out = mm(prob.astype(BF), v_ref[0, :, head(h)])
        for chip in range(CHIPS):
            even = out[2 * chip * TOK:(2 * chip + 1) * TOK]
            odd = out[(2 * chip + 1) * TOK:(2 * chip + 2) * TOK]
            shift = (chip - z) & (CHIPS - 1)
            keep_ref[shift, h] = jnp.where(first, even, odd).astype(BF)
            give_ref[shift, h] = jnp.where(first, odd, even).astype(BF)


def merge_kernel(keep_ref, got_ref, *outs):
    for out, shift in zip(outs, (0,) + SHIFTS):
        out[0] = keep_ref[shift % CHIPS]
        out[1] = got_ref[shift % CHIPS]


def merge_last_kernel(tile_ref, keep_ref, got_ref, *outs):
    for out, shift in zip(outs, (0,) + SHIFTS):
        out[:HEADS] = keep_ref[-shift % CHIPS]
        out[HEADS:2 * HEADS] = got_ref[-shift % CHIPS]
        out[2 * HEADS] = tile_ref[...]


def pair_rows(pos_ref, shift):
    z, c = pos_ref[0], pos_ref[1]
    return range_row(z - shift, c), range_row(z - shift, 1 - c)


def spatial_bwd_kernel(q_ref, k_ref, v_ref, prob_ref, mid_ref, gq_ref, gk_ref, gv_ref):
    for h in range(HEADS):
        q, k, v = q_ref[0, :, head(h)], k_ref[0, :, head(h)], v_ref[0, :, head(h)]
        up = rows_of(mid_ref, h)
        prob = prob_ref[h]
        grad_prob = mm_nt(up, v)
        gv_ref[0, :, head(h)] = mm_tn(prob.astype(BF), up).astype(BF)
        row_dot = jnp.sum(prob * grad_prob, axis=-1, keepdims=True)
        low = (prob * (grad_prob - row_dot) * SCALE).astype(BF)
        gq_ref[0, :, head(h)] = mm(low, k).astype(BF)
        gk_ref[0, :, head(h)] = mm_tn(low, q).astype(BF)


def temporal_a_kernel(frames_ref, in_ref, bias_ref, prob_ref, mid_ref):
    row = lax.broadcasted_iota(jnp.int32, (ROWS, ROWS), 0)
    col = lax.broadcasted_iota(jnp.int32, (ROWS, ROWS), 1)
    clip = slot_rows(frames_ref, in_ref, 3 * HEADS).astype(F32)
    other = clip.T
    same = (row & (TOK - 1)) == (col & (TOK - 1))
    same &= jnp.concatenate([clip] * 2, axis=1) == jnp.concatenate([other] * 2, axis=0)
    mask = jnp.where(same, 0.0, NEG)
    for h in range(HEADS):
        q, k, up = (slot_rows(frames_ref, in_ref, i * HEADS + h) for i in range(3))
        bias = jnp.broadcast_to(bias_ref[h][:, None, :], (SEQ, TOK, ROWS)).reshape(ROWS, ROWS)
        prob = softmax((mm_nt(q, k) * SCALE + bias) + mask)
        prob_ref[h] = prob
        put_slots(frames_ref, mid_ref, h, mm_tn(prob.astype(BF), up))


def temporal_b_kernel(frames_ref, in_ref, prob_ref, *refs):
    so_refs, (out_ref, keep_ref, give_ref, bias_ref) = dict(zip((0,) + SHIFTS, refs)), refs[-4:]
    so_at = [(so_refs[d if d <= CHIPS // 2 else d - CHIPS], x) for d, x in SLOTS]
    for h in range(HEADS):
        q, k, up = (slot_rows(frames_ref, in_ref, i * HEADS + h) for i in range(3))
        so = jnp.concatenate([ref[x, h] for ref, x in so_at], axis=0)
        prob = prob_ref[h]
        grad_prob = mm_nt(up, so)
        put_slots(frames_ref, out_ref, h, mm(prob.astype(BF), so))
        score = prob * (grad_prob - jnp.sum(prob * grad_prob, axis=-1, keepdims=True))
        bias_ref[h] = jnp.sum(score.reshape(SEQ, TOK, ROWS), axis=1)
        low = (score * SCALE).astype(BF)
        put_slots(frames_ref, out_ref, HEADS + h, mm(low, k))
        put_pairs(keep_ref, give_ref, h, mm_tn(low, q))


def unpack_kernel(in_ref, *outs):
    for tile in range(2 * HEADS):
        outs[tile // HEADS][0, :, head(tile % HEADS)] = rows_of(in_ref, tile)


def finish_kernel(pos_ref, *refs):
    messages, (gk_ref, bias_ref) = refs[:CHIPS], refs[CHIPS:]
    for ref, shift in zip(messages, (0,) + SHIFTS):
        for x, row in enumerate(pair_rows(pos_ref, shift)):
            for h in range(HEADS):
                gk_ref[0, pl.ds(row, TOK), head(h)] = ref[x * HEADS + h]
    z = pos_ref[0]
    total = jnp.zeros((TOK, DIM), F32)
    for chip in range(CHIPS):
        for ref, shift in zip(messages, (0,) + SHIFTS):
            mine = ((z - shift) & (CHIPS - 1)) == chip
            total += jnp.where(mine, ref[2 * HEADS].astype(F32), 0.0)
    total = total + pltpu.roll(total, DIM - 32, 1) + pltpu.roll(total, DIM - 64, 1)
    bias_ref[...] = total[:HEADS, :2 * SEQ - 1]


def call(kernel, name, specs, inputs, outputs, scratch=(), estimate=1000, params=PARAMS, space=VMEM):
    return pl.pallas_call(
        kernel,
        out_shape=tuple(outputs),
        in_specs=specs,
        out_specs=(space,) * len(outputs),
        scratch_shapes=scratch,
        compiler_params=params,
        cost_estimate=pl.CostEstimate(flops=estimate, bytes_accessed=1000, transcendentals=0),
        name=name,
    )(*inputs)


def exchange(packed):
    return lax.all_to_all(packed, "seq", split_axis=0, concat_axis=0, tiled=True)


def pair(terms, axis, mask):
    size = lax.axis_size(axis)
    return lax.ppermute(terms, axis, [(i, i ^ mask) for i in range(size)])


def sum_of_four(terms, axis, step):
    one, two, three = (pair(terms, axis, step * mask) for mask in (1, 2, 3))
    return (terms + one) + (two + three)


def move(message, s, x):
    perm = [(2 * z + c, 2 * ((z + s) % CHIPS) + (c ^ x)) for z in range(CHIPS) for c in range(2)]
    return lax.ppermute(message, "seq", perm)


def sent(messages):
    return [messages[0], *(move(m, s, 0) for m, s in zip(messages[1:], SHIFTS))]


def bfloat_parts(terms):
    parts = []
    for _ in range(3):
        part = lax.reduce_precision(terms, 8, 7)
        parts.append(jnp.pad(part, ((0, TOK - HEADS), (0, 1))))
        terms = terms - part
    return jnp.pad(jnp.concatenate(parts, axis=1), ((0, 0), (0, DIM - 96))).astype(BF)


def offsets_table(frames):
    offset = frames[:, None] - frames[None, :] + (SEQ - 1)
    slots = jnp.arange(2 * SEQ - 1, dtype=jnp.int32)
    return (offset[:, :, None] == slots[None, None, :]).astype(F32)


def per_device(
    q_spatial, k_spatial, v_spatial, q_temporal, k_temporal, rel_bias, clip_ids, cotangent
):
    index = lax.axis_index("seq").astype(jnp.int32)
    z, c = index >> 1, index & 1
    pos = jnp.stack([z, c])
    away = jnp.array([d for d, x in SLOTS], jnp.int32)
    swapped = jnp.array([x for d, x in SLOTS], jnp.int32)
    frames = 2 * ((z - away) & (CHIPS - 1)) + (c ^ swapped)

    tiles = 3 * HEADS + 1
    (packed,) = call(
        pack_kernel,
        "pack",
        [SMEM] + [HBM] * 3,
        [clip_ids, q_temporal, k_temporal, cotangent],
        [units(SEQ, tiles)],
        [
            pltpu.VMEM((3, ROWS, WIDTH), BF),
            pltpu.VMEM((SEQ, tiles, TOK, DIM), BF),
            pltpu.SemaphoreType.DMA((3, PARTS)),
            pltpu.SemaphoreType.DMA((3 * PARTS + 1,)),
        ],
        space=HBM,
        params=pltpu.CompilerParams(vmem_limit_bytes=56 * 1024 * 1024),
    )
    there = exchange(packed)

    spatial = [q_spatial, k_spatial, v_spatial]
    spatial, rel_bias, frames, _ = lax.optimization_barrier((spatial, rel_bias, frames, packed))
    wide = jnp.repeat(offsets_table(frames), TOK, axis=1)
    bias = jnp.einsum("hr,icr->hic", rel_bias, wide, precision=lax.Precision.HIGHEST)
    keep_so, give_so, sp_prob = call(
        spatial_fwd_kernel,
        "spatial_fwd",
        [SMEM] + [VMEM] * 3,
        [pos, *spatial],
        [units(CHIPS, HEADS)] * 2 + [probs()],
    )
    give_so, bias = lax.optimization_barrier((give_so, bias))
    got_so = move(give_so, 0, 1)
    so_messages = call(
        merge_kernel, "merge", [VMEM] * 2, [keep_so, got_so], [units(2, HEADS)] * CHIPS
    )
    so = sent(so_messages)

    there, _, bias = lax.optimization_barrier((there, so_messages, bias))
    prob, mid = call(
        temporal_a_kernel,
        "temporal_a",
        [SMEM] + [VMEM] * 2,
        [frames, there, bias],
        [probs(), units(SEQ, HEADS)],
    )
    grad_mid = exchange(mid)

    back, keep_back, give_back, score_rows = call(
        temporal_b_kernel,
        "temporal_b",
        [SMEM] + [VMEM] * (2 + CHIPS),
        [frames, there, prob, *so],
        [units(SEQ, 2 * HEADS)]
        + [units(CHIPS, HEADS)] * 2
        + [jax.ShapeDtypeStruct((HEADS, SEQ, ROWS), F32)],
        estimate=LONG,
    )
    terms = jnp.einsum("hic,icr->hr", score_rows, wide, precision=lax.Precision.HIGHEST)
    terms = terms + move(terms, 0, 1)
    got_back = move(give_back, 0, 1)
    last = sent(
        call(
            merge_last_kernel,
            "merge_last",
            [VMEM] * 3,
            [bfloat_parts(terms), keep_back, got_back],
            [jax.ShapeDtypeStruct((2 * HEADS + 1, TOK, DIM), BF)] * CHIPS,
        )
    )
    returned = exchange(back)

    grad_mid, _ = lax.optimization_barrier((grad_mid, last))
    grad_qs, grad_ks, grad_vs = call(
        spatial_bwd_kernel,
        "spatial_bwd",
        [VMEM] * 5,
        [*spatial, sp_prob, grad_mid],
        [frame()] * 3,
        estimate=LONG,
    )
    last, _ = lax.optimization_barrier((last, grad_vs))
    grad_kt, total = call(
        finish_kernel,
        "finish",
        [SMEM] + [VMEM] * CHIPS,
        [pos, *last],
        [frame(), jax.ShapeDtypeStruct((HEADS, 2 * SEQ - 1), F32)],
    )
    total_bias = sum_of_four(sum_of_four(total, "grp", 1), "grp", 4)
    result, grad_qt = call(unpack_kernel, "unpack", [VMEM], [returned], [frame()] * 2)
    return result, grad_qs, grad_ks, grad_vs, grad_qt, grad_kt, total_bias


def solution(mesh):
    frames = P(("grp", "seq"), None, None)
    return jax.shard_map(
        per_device,
        mesh=mesh,
        in_specs=(frames,) * 5 + (P(), P("grp", "seq"), frames),
        out_specs=(frames,) * 6 + (P(),),
        check_vma=False,
    )
```

```python
import jax
import jax.numpy as jnp
from jax import lax
from jax.experimental import pallas as pl
from jax.experimental.pallas import tpu as pltpu
from jax.sharding import PartitionSpec as P

HEADS = 12
DIM = 128
SEQ = 16
CHIPS = 8
TOK = 16
ROWS = SEQ * TOK
WIDTH = HEADS * DIM
SCALE = DIM ** (-0.5)
NEG = -1e30
BF = jnp.bfloat16
F32 = jnp.float32
PARAMS = pltpu.CompilerParams(vmem_limit_bytes=48 * 1024 * 1024)
PARTS = 4
GROUP = 3
LONG = 10**12
VMEM = pl.BlockSpec(memory_space=pltpu.VMEM)
SMEM = pl.BlockSpec(memory_space=pltpu.SMEM)
HBM = pl.BlockSpec(memory_space=pltpu.HBM)


def mm(left, right):
    return lax.dot_general(left, right, (((1,), (0,)), ((), ())), preferred_element_type=F32)


def mm_nt(left, right):
    return lax.dot_general(left, right, (((1,), (1,)), ((), ())), preferred_element_type=F32)


def mm_tn(left, right):
    return lax.dot_general(left, right, (((0,), (0,)), ((), ())), preferred_element_type=F32)


def softmax(scores):
    raw = jnp.exp(scores - jnp.max(scores, axis=-1, keepdims=True))
    return raw / jnp.sum(raw, axis=-1, keepdims=True)


def units(n, tiles):
    return jax.ShapeDtypeStruct((n, tiles, TOK, DIM), BF)


def frame():
    return jax.ShapeDtypeStruct((1, ROWS, WIDTH), BF)


def probs():
    return jax.ShapeDtypeStruct((HEADS, ROWS, ROWS), F32)


def range_row(chip, core):
    return pl.multiple_of((2 * (chip & (CHIPS - 1)) + core) * TOK, TOK)


def head(h):
    return slice(h * DIM, (h + 1) * DIM)


def rows_of(ref, tile):
    return ref[:, tile].reshape(ROWS, DIM)


SHIFTS = (1, -1, 3, -3, 2, -2, 4)
SLOTS = tuple((d, x) for x in range(2) for d in range(CHIPS))


def slot_rows(frames_ref, ref, tile):
    return jnp.concatenate([ref[frames_ref[s], tile] for s in range(SEQ)], axis=0)


def put_pairs(keep_ref, give_ref, tile, value):
    low = value.astype(BF)
    for d in range(CHIPS):
        keep_ref[d, tile] = low[d * TOK:(d + 1) * TOK]
        give_ref[d, tile] = low[(CHIPS + d) * TOK:(CHIPS + d + 1) * TOK]


def put_frames(frames_ref, ref, i, h, value):
    low = value.astype(BF)
    for s in range(SEQ):
        ref[frames_ref[s], i, :, head(h)] = low[s * TOK:(s + 1) * TOK]


def pack_kernel(clip_ref, q_ref, k_ref, up_ref, out_ref, held, made, sems, out_sems):
    copies = []
    size, units_of = ROWS // PARTS, SEQ // PARTS
    for i, ref in enumerate((q_ref, k_ref, up_ref)):
        for part in range(PARTS):
            rows = pl.ds(part * size, size)
            copies.append(
                pltpu.make_async_copy(ref.at[0, rows], held.at[i, rows], sems.at[i, part])
            )
            copies[-1].start()
    last = pl.ds(3 * HEADS, 1)
    clip = jnp.full((SEQ, TOK, DIM), clip_ref[0, 0], jnp.int32).astype(F32).astype(BF)
    made[:, 3 * HEADS] = clip
    outs = [pltpu.make_async_copy(made.at[:, last], out_ref.at[:, last], out_sems.at[3 * PARTS])]
    outs[-1].start()
    for i in range(3):
        for part in range(PARTS):
            copies[i * PARTS + part].wait()
            units = pl.ds(part * units_of, units_of)
            for h in range(HEADS):
                block = held[i, part * size:(part + 1) * size, head(h)]
                made[units, i * HEADS + h] = block.reshape(units_of, TOK, DIM)
            at = (units, pl.ds(i * HEADS, HEADS))
            outs.append(
                pltpu.make_async_copy(made.at[at], out_ref.at[at], out_sems.at[i * PARTS + part])
            )
            outs[-1].start()
    for copy in outs:
        copy.wait()


def spatial_fwd_kernel(pos_ref, q_ref, k_ref, v_ref, keep_ref, give_ref, prob_ref):
    z, first = pos_ref[0], pos_ref[1] == 0
    for h in range(HEADS):
        prob = softmax(mm_nt(q_ref[0, :, head(h)], k_ref[0, :, head(h)]) * SCALE)
        prob_ref[h] = prob
        out = mm(prob.astype(BF), v_ref[0, :, head(h)])
        for chip in range(CHIPS):
            even = out[2 * chip * TOK:(2 * chip + 1) * TOK]
            odd = out[(2 * chip + 1) * TOK:(2 * chip + 2) * TOK]
            shift = (chip - z) & (CHIPS - 1)
            keep_ref[shift, h] = jnp.where(first, even, odd).astype(BF)
            give_ref[shift, h] = jnp.where(first, odd, even).astype(BF)


def merge_kernel(keep_ref, got_ref, bias_ref, *outs):
    for out, shift in zip(outs, (0,) + SHIFTS):
        out[0] = keep_ref[shift % CHIPS]
        out[1] = got_ref[shift % CHIPS]


def merge_last_kernel(tile_ref, keep_ref, got_ref, *outs):
    for out, shift in zip(outs, (0,) + SHIFTS):
        out[:HEADS] = keep_ref[-shift % CHIPS]
        out[HEADS:2 * HEADS] = got_ref[-shift % CHIPS]
        out[2 * HEADS] = tile_ref[...]


def pair_rows(pos_ref, shift):
    z, c = pos_ref[0], pos_ref[1]
    return range_row(z - shift, c), range_row(z - shift, 1 - c)


def spatial_bwd_kernel(q_ref, k_ref, v_ref, prob_ref, mid_ref, gq_ref, gk_ref, gv_ref):
    for h in range(HEADS):
        q, k, v = q_ref[0, :, head(h)], k_ref[0, :, head(h)], v_ref[0, :, head(h)]
        up = rows_of(mid_ref, h)
        prob = prob_ref[h]
        grad_prob = mm_nt(up, v)
        gv_ref[0, :, head(h)] = mm_tn(prob.astype(BF), up).astype(BF)
        row_dot = jnp.sum(prob * grad_prob, axis=-1, keepdims=True)
        low = (prob * (grad_prob - row_dot) * SCALE).astype(BF)
        gq_ref[0, :, head(h)] = mm(low, k).astype(BF)
        gk_ref[0, :, head(h)] = mm_tn(low, q).astype(BF)


def temporal_a_kernel(frames_ref, in_ref, bias_ref, prob_ref, mid_ref, made, sems):
    row = lax.broadcasted_iota(jnp.int32, (ROWS, ROWS), 0)
    col = lax.broadcasted_iota(jnp.int32, (ROWS, ROWS), 1)
    clip = slot_rows(frames_ref, in_ref, 3 * HEADS).astype(F32)
    other = clip.T
    same = (row & (TOK - 1)) == (col & (TOK - 1))
    same &= jnp.concatenate([clip] * 2, axis=1) == jnp.concatenate([other] * 2, axis=0)
    mask = jnp.where(same, 0.0, NEG)
    copies = []
    for h in range(HEADS):
        q, k, up = (slot_rows(frames_ref, in_ref, i * HEADS + h) for i in range(3))
        bias = jnp.broadcast_to(bias_ref[h][:, None, :], (SEQ, TOK, ROWS)).reshape(ROWS, ROWS)
        prob = softmax((mm_nt(q, k) * SCALE + bias) + mask)
        prob_ref[h] = prob
        mid = mm_tn(prob.astype(BF), up).astype(BF)
        for s in range(SEQ):
            made[frames_ref[s], h] = mid[s * TOK:(s + 1) * TOK]
        if (h + 1) % GROUP == 0:
            at = (slice(None), pl.ds(h + 1 - GROUP, GROUP))
            copies.append(
                pltpu.make_async_copy(made.at[at], mid_ref.at[at], sems.at[h // GROUP])
            )
            copies[-1].start()
    for copy in copies:
        copy.wait()


def temporal_b_kernel(frames_ref, in_ref, prob_ref, *refs):
    so_refs, (out_ref, keep_ref, give_ref, bias_ref) = dict(zip((0,) + SHIFTS, refs)), refs[-4:]
    so_at = [(so_refs[d if d <= CHIPS // 2 else d - CHIPS], x) for d, x in SLOTS]
    for h in range(HEADS):
        q, k, up = (slot_rows(frames_ref, in_ref, i * HEADS + h) for i in range(3))
        so = jnp.concatenate([ref[x, h] for ref, x in so_at], axis=0)
        prob = prob_ref[h]
        grad_prob = mm_nt(up, so)
        put_frames(frames_ref, out_ref, 0, h, mm(prob.astype(BF), so))
        score = prob * (grad_prob - jnp.sum(prob * grad_prob, axis=-1, keepdims=True))
        bias_ref[h] = jnp.sum(score.reshape(SEQ, TOK, ROWS), axis=1)
        low = (score * SCALE).astype(BF)
        put_frames(frames_ref, out_ref, 1, h, mm(low, k))
        put_pairs(keep_ref, give_ref, h, mm_tn(low, q))


def unpack_kernel(in_ref, res_ref, gq_ref, sems):
    copies = []
    for i, out in enumerate((res_ref, gq_ref)):
        for u in range(SEQ):
            rows = pl.ds(u * TOK, TOK)
            copies.append(pltpu.make_async_copy(in_ref.at[u, i], out.at[0, rows], sems.at[i, u]))
            copies[-1].start()
    for copy in copies:
        copy.wait()


def finish_kernel(pos_ref, *refs):
    messages, (gk_ref, bias_ref) = refs[:CHIPS], refs[CHIPS:]
    for ref, shift in zip(messages, (0,) + SHIFTS):
        for x, row in enumerate(pair_rows(pos_ref, shift)):
            for h in range(HEADS):
                gk_ref[0, pl.ds(row, TOK), head(h)] = ref[x * HEADS + h]
    z = pos_ref[0]
    total = jnp.zeros((TOK, DIM), F32)
    for chip in range(CHIPS):
        for ref, shift in zip(messages, (0,) + SHIFTS):
            mine = ((z - shift) & (CHIPS - 1)) == chip
            total += jnp.where(mine, ref[2 * HEADS].astype(F32), 0.0)
    total = total + pltpu.roll(total, DIM - 32, 1) + pltpu.roll(total, DIM - 64, 1)
    bias_ref[...] = total[:HEADS, :2 * SEQ - 1]


def call(kernel, name, specs, inputs, outputs, scratch=(), estimate=1000, params=PARAMS, space=VMEM):
    return pl.pallas_call(
        kernel,
        out_shape=tuple(outputs),
        in_specs=specs,
        out_specs=space if isinstance(space, tuple) else (space,) * len(outputs),
        scratch_shapes=scratch,
        compiler_params=params,
        cost_estimate=pl.CostEstimate(flops=estimate, bytes_accessed=1000, transcendentals=0),
        name=name,
    )(*inputs)


def exchange(packed):
    return lax.all_to_all(packed, "seq", split_axis=0, concat_axis=0, tiled=True)


def pair(terms, axis, mask):
    size = lax.axis_size(axis)
    return lax.ppermute(terms, axis, [(i, i ^ mask) for i in range(size)])


def sum_of_four(terms, axis, step):
    one, two, three = (pair(terms, axis, step * mask) for mask in (1, 2, 3))
    return (terms + one) + (two + three)


def move(message, s, x):
    perm = [(2 * z + c, 2 * ((z + s) % CHIPS) + (c ^ x)) for z in range(CHIPS) for c in range(2)]
    return lax.ppermute(message, "seq", perm)


def sent(messages):
    return [messages[0], *(move(m, s, 0) for m, s in zip(messages[1:], SHIFTS))]


def bfloat_parts(terms):
    parts = []
    for _ in range(3):
        part = lax.reduce_precision(terms, 8, 7)
        parts.append(jnp.pad(part, ((0, TOK - HEADS), (0, 1))))
        terms = terms - part
    return jnp.pad(jnp.concatenate(parts, axis=1), ((0, 0), (0, DIM - 96))).astype(BF)


def offsets_table(frames):
    offset = frames[:, None] - frames[None, :] + (SEQ - 1)
    slots = jnp.arange(2 * SEQ - 1, dtype=jnp.int32)
    return (offset[:, :, None] == slots[None, None, :]).astype(F32)


def per_device(
    q_spatial, k_spatial, v_spatial, q_temporal, k_temporal, rel_bias, clip_ids, cotangent
):
    index = lax.axis_index("seq").astype(jnp.int32)
    z, c = index >> 1, index & 1
    pos = jnp.stack([z, c])
    away = jnp.array([d for d, x in SLOTS], jnp.int32)
    swapped = jnp.array([x for d, x in SLOTS], jnp.int32)
    frames = 2 * ((z - away) & (CHIPS - 1)) + (c ^ swapped)

    tiles = 3 * HEADS + 1
    (packed,) = call(
        pack_kernel,
        "pack",
        [SMEM] + [HBM] * 3,
        [clip_ids, q_temporal, k_temporal, cotangent],
        [units(SEQ, tiles)],
        [
            pltpu.VMEM((3, ROWS, WIDTH), BF),
            pltpu.VMEM((SEQ, tiles, TOK, DIM), BF),
            pltpu.SemaphoreType.DMA((3, PARTS)),
            pltpu.SemaphoreType.DMA((3 * PARTS + 1,)),
        ],
        space=HBM,
        params=pltpu.CompilerParams(vmem_limit_bytes=56 * 1024 * 1024),
    )
    there = exchange(packed)

    spatial = [q_spatial, k_spatial, v_spatial]
    spatial, rel_bias, frames, _ = lax.optimization_barrier((spatial, rel_bias, frames, packed))
    wide = jnp.repeat(offsets_table(frames), TOK, axis=1)
    bias = jnp.einsum("hr,icr->hic", rel_bias, wide, precision=lax.Precision.HIGHEST)
    keep_so, give_so, sp_prob = call(
        spatial_fwd_kernel,
        "spatial_fwd",
        [SMEM] + [VMEM] * 3,
        [pos, *spatial],
        [units(CHIPS, HEADS)] * 2 + [probs()],
    )
    give_so, bias = lax.optimization_barrier((give_so, bias))
    got_so = move(give_so, 0, 1)
    so_messages = call(
        merge_kernel, "merge", [VMEM] * 3, [keep_so, got_so, bias], [units(2, HEADS)] * CHIPS
    )
    so = sent(so_messages)

    there, _, bias = lax.optimization_barrier((there, so_messages, bias))
    prob, mid = call(
        temporal_a_kernel,
        "temporal_a",
        [SMEM] + [VMEM] * 2,
        [frames, there, bias],
        [probs(), units(SEQ, HEADS)],
        [pltpu.VMEM((SEQ, HEADS, TOK, DIM), BF), pltpu.SemaphoreType.DMA((HEADS // GROUP,))],
        space=(VMEM, HBM),
    )
    grad_mid = exchange(mid)

    back, keep_back, give_back, score_rows = call(
        temporal_b_kernel,
        "temporal_b",
        [SMEM] + [VMEM] * (2 + CHIPS),
        [frames, there, prob, *so],
        [jax.ShapeDtypeStruct((SEQ, 2, TOK, WIDTH), BF)]
        + [units(CHIPS, HEADS)] * 2
        + [jax.ShapeDtypeStruct((HEADS, SEQ, ROWS), F32)],
        estimate=LONG,
    )
    terms = jnp.einsum("hic,icr->hr", score_rows, wide, precision=lax.Precision.HIGHEST)
    terms = terms + move(terms, 0, 1)
    got_back = move(give_back, 0, 1)
    last = sent(
        call(
            merge_last_kernel,
            "merge_last",
            [VMEM] * 3,
            [bfloat_parts(terms), keep_back, got_back],
            [jax.ShapeDtypeStruct((2 * HEADS + 1, TOK, DIM), BF)] * CHIPS,
        )
    )
    returned = exchange(back)

    grad_mid, _ = lax.optimization_barrier((grad_mid, last))
    grad_qs, grad_ks, grad_vs = call(
        spatial_bwd_kernel,
        "spatial_bwd",
        [VMEM] * 5,
        [*spatial, sp_prob, grad_mid],
        [frame()] * 3,
        estimate=LONG,
    )
    last, _ = lax.optimization_barrier((last, grad_vs))
    grad_kt, total = call(
        finish_kernel,
        "finish",
        [SMEM] + [VMEM] * CHIPS,
        [pos, *last],
        [frame(), jax.ShapeDtypeStruct((HEADS, 2 * SEQ - 1), F32)],
    )
    total_bias = sum_of_four(sum_of_four(total, "grp", 1), "grp", 4)
    result, grad_qt = call(
        unpack_kernel,
        "unpack",
        [VMEM],
        [returned],
        [frame()] * 2,
        [pltpu.SemaphoreType.DMA((2, SEQ))],
        space=HBM,
    )
    return result, grad_qs, grad_ks, grad_vs, grad_qt, grad_kt, total_bias


def solution(mesh):
    frames = P(("grp", "seq"), None, None)
    return jax.shard_map(
        per_device,
        mesh=mesh,
        in_specs=(frames,) * 5 + (P(), P("grp", "seq"), frames),
        out_specs=(frames,) * 6 + (P(),),
        check_vma=False,
    )
```

```python
import jax
import jax.numpy as jnp
from jax import lax
from jax.experimental import pallas as pl
from jax.experimental.pallas import tpu as pltpu
from jax.sharding import PartitionSpec as P

HEADS = 12
DIM = 128
RELS = 31
SEQ = 16
CHIPS = 8
TOK = 16
ROWS = SEQ * TOK
WIDTH = HEADS * DIM
SCALE = DIM ** (-0.5)
NEG = -1e30
BF = jnp.bfloat16
F32 = jnp.float32
PARAMS = pltpu.CompilerParams(vmem_limit_bytes=24 * 1024 * 1024)
PARTS = 4
LONG = 10**12
VMEM = pl.BlockSpec(memory_space=pltpu.VMEM)
SMEM = pl.BlockSpec(memory_space=pltpu.SMEM)
HBM = pl.BlockSpec(memory_space=pltpu.HBM)


def mm(left, right):
    return lax.dot_general(left, right, (((1,), (0,)), ((), ())), preferred_element_type=F32)


def mm_nt(left, right):
    return lax.dot_general(left, right, (((1,), (1,)), ((), ())), preferred_element_type=F32)


def mm_tn(left, right):
    return lax.dot_general(left, right, (((0,), (0,)), ((), ())), preferred_element_type=F32)


def softmax(scores):
    raw = jnp.exp(scores - jnp.max(scores, axis=-1, keepdims=True))
    return raw / jnp.sum(raw, axis=-1, keepdims=True)


def units(n, tiles):
    return jax.ShapeDtypeStruct((n, tiles, TOK, DIM), BF)


def frame():
    return jax.ShapeDtypeStruct((1, ROWS, WIDTH), BF)


def probs():
    return jax.ShapeDtypeStruct((HEADS, ROWS, ROWS), F32)


def range_row(chip, core):
    return pl.multiple_of((2 * (chip & (CHIPS - 1)) + core) * TOK, TOK)


def head(h):
    return slice(h * DIM, (h + 1) * DIM)


def rows_of(ref, tile):
    return ref[:, tile].reshape(ROWS, DIM)


SHIFTS = (1, -1, 3, -3, 2, -2, 4)
SLOTS = tuple((d, x) for x in range(2) for d in range(CHIPS))


def slot_rows(frames_ref, ref, tile):
    return jnp.concatenate([ref[frames_ref[s], tile] for s in range(SEQ)], axis=0)


def put_pairs(keep_ref, give_ref, tile, value):
    low = value.astype(BF)
    for d in range(CHIPS):
        keep_ref[d, tile] = low[d * TOK:(d + 1) * TOK]
        give_ref[d, tile] = low[(CHIPS + d) * TOK:(CHIPS + d + 1) * TOK]


def put_frames(frames_ref, ref, i, h, value):
    low = value.astype(BF)
    for s in range(SEQ):
        ref[frames_ref[s], i, :, head(h)] = low[s * TOK:(s + 1) * TOK]


def pack_kernel(clip_ref, q_ref, k_ref, up_ref, out_ref, held, made, sems, out_sems):
    copies = []
    size, units_of = ROWS // PARTS, SEQ // PARTS
    for i, ref in enumerate((q_ref, k_ref, up_ref)):
        for part in range(PARTS):
            rows = pl.ds(part * size, size)
            copies.append(
                pltpu.make_async_copy(ref.at[0, rows], held.at[i, rows], sems.at[i, part])
            )
            copies[-1].start()
    last = pl.ds(3 * HEADS, 1)
    clip = jnp.full((SEQ, TOK, DIM), clip_ref[0, 0], jnp.int32).astype(F32).astype(BF)
    made[:, 3 * HEADS] = clip
    outs = [pltpu.make_async_copy(made.at[:, last], out_ref.at[:, last], out_sems.at[3 * PARTS])]
    outs[-1].start()
    for i in range(3):
        for part in range(PARTS):
            copies[i * PARTS + part].wait()
            units = pl.ds(part * units_of, units_of)
            for h in range(HEADS):
                block = held[i, part * size:(part + 1) * size, head(h)]
                made[units, i * HEADS + h] = block.reshape(units_of, TOK, DIM)
            at = (units, pl.ds(i * HEADS, HEADS))
            outs.append(
                pltpu.make_async_copy(made.at[at], out_ref.at[at], out_sems.at[i * PARTS + part])
            )
            outs[-1].start()
    for copy in outs:
        copy.wait()


def spatial_fwd_kernel(pos_ref, q_ref, k_ref, v_ref, keep_ref, give_ref, prob_ref):
    z, first = pos_ref[0], pos_ref[1] == 0
    for h in range(HEADS):
        prob = softmax(mm_nt(q_ref[0, :, head(h)], k_ref[0, :, head(h)]) * SCALE)
        prob_ref[h] = prob
        out = mm(prob.astype(BF), v_ref[0, :, head(h)])
        for chip in range(CHIPS):
            even = out[2 * chip * TOK:(2 * chip + 1) * TOK]
            odd = out[(2 * chip + 1) * TOK:(2 * chip + 2) * TOK]
            shift = (chip - z) & (CHIPS - 1)
            keep_ref[shift, h] = jnp.where(first, even, odd).astype(BF)
            give_ref[shift, h] = jnp.where(first, odd, even).astype(BF)


def merge_kernel(keep_ref, got_ref, *outs):
    for out, shift in zip(outs, (0,) + SHIFTS):
        out[0] = keep_ref[shift % CHIPS]
        out[1] = got_ref[shift % CHIPS]


def merge_last_kernel(tile_ref, keep_ref, got_ref, *outs):
    for out, shift in zip(outs, (0,) + SHIFTS):
        out[:HEADS] = keep_ref[-shift % CHIPS]
        out[HEADS:2 * HEADS] = got_ref[-shift % CHIPS]
        out[2 * HEADS] = tile_ref[...]


def pair_rows(pos_ref, shift):
    z, c = pos_ref[0], pos_ref[1]
    return range_row(z - shift, c), range_row(z - shift, 1 - c)


def spatial_bwd_kernel(q_ref, k_ref, v_ref, prob_ref, mid_ref, gq_ref, gk_ref, gv_ref):
    for h in range(HEADS):
        q, k, v = q_ref[0, :, head(h)], k_ref[0, :, head(h)], v_ref[0, :, head(h)]
        up = rows_of(mid_ref, h)
        prob = prob_ref[h]
        grad_prob = mm_nt(up, v)
        gv_ref[0, :, head(h)] = mm_tn(prob.astype(BF), up).astype(BF)
        row_dot = jnp.sum(prob * grad_prob, axis=-1, keepdims=True)
        low = (prob * (grad_prob - row_dot) * SCALE).astype(BF)
        gq_ref[0, :, head(h)] = mm(low, k).astype(BF)
        gk_ref[0, :, head(h)] = mm_tn(low, q).astype(BF)


def bias_kernel(rel_ref, offsets_ref, out_ref):
    offsets = offsets_ref[...]
    for h in range(HEADS):
        table = jnp.zeros((SEQ, ROWS), F32)
        for r in range(RELS):
            table = jnp.where(offsets == r, rel_ref[h, r], table)
        out_ref[h] = table


def temporal_a_kernel(frames_ref, in_ref, bias_ref, prob_ref, mid_ref):
    row = lax.broadcasted_iota(jnp.int32, (ROWS, ROWS), 0)
    col = lax.broadcasted_iota(jnp.int32, (ROWS, ROWS), 1)
    clip = slot_rows(frames_ref, in_ref, 3 * HEADS).astype(F32)
    other = clip.T
    same = (row & (TOK - 1)) == (col & (TOK - 1))
    same &= jnp.concatenate([clip] * 2, axis=1) == jnp.concatenate([other] * 2, axis=0)
    mask = jnp.where(same, 0.0, NEG)
    for h in range(HEADS):
        q, k, up = (slot_rows(frames_ref, in_ref, i * HEADS + h) for i in range(3))
        bias = jnp.broadcast_to(bias_ref[h][:, None, :], (SEQ, TOK, ROWS)).reshape(ROWS, ROWS)
        prob = softmax((mm_nt(q, k) * SCALE + bias) + mask)
        prob_ref[h] = prob
        mid = mm_tn(prob.astype(BF), up).astype(BF)
        for s in range(SEQ):
            mid_ref[frames_ref[s], h] = mid[s * TOK:(s + 1) * TOK]


def temporal_b_kernel(frames_ref, in_ref, prob_ref, *refs):
    so_refs, (out_ref, keep_ref, give_ref, bias_ref) = dict(zip((0,) + SHIFTS, refs)), refs[-4:]
    so_at = [(so_refs[d if d <= CHIPS // 2 else d - CHIPS], x) for d, x in SLOTS]
    for h in range(HEADS):
        q, k, up = (slot_rows(frames_ref, in_ref, i * HEADS + h) for i in range(3))
        so = jnp.concatenate([ref[x, h] for ref, x in so_at], axis=0)
        prob = prob_ref[h]
        grad_prob = mm_nt(up, so)
        put_frames(frames_ref, out_ref, 0, h, mm(prob.astype(BF), so))
        score = prob * (grad_prob - jnp.sum(prob * grad_prob, axis=-1, keepdims=True))
        bias_ref[h] = jnp.sum(score.reshape(SEQ, TOK, ROWS), axis=1)
        low = (score * SCALE).astype(BF)
        put_frames(frames_ref, out_ref, 1, h, mm(low, k))
        put_pairs(keep_ref, give_ref, h, mm_tn(low, q))


def unpack_kernel(in_ref, res_ref, gq_ref, sems):
    copies = []
    for i, out in enumerate((res_ref, gq_ref)):
        for u in range(SEQ):
            rows = pl.ds(u * TOK, TOK)
            copies.append(pltpu.make_async_copy(in_ref.at[u, i], out.at[0, rows], sems.at[i, u]))
            copies[-1].start()
    for copy in copies:
        copy.wait()


def finish_kernel(pos_ref, *refs):
    messages, (gk_ref, bias_ref) = refs[:CHIPS], refs[CHIPS:]
    for ref, shift in zip(messages, (0,) + SHIFTS):
        for x, row in enumerate(pair_rows(pos_ref, shift)):
            for h in range(HEADS):
                gk_ref[0, pl.ds(row, TOK), head(h)] = ref[x * HEADS + h]
    z = pos_ref[0]
    total = jnp.zeros((TOK, DIM), F32)
    for chip in range(CHIPS):
        for ref, shift in zip(messages, (0,) + SHIFTS):
            mine = ((z - shift) & (CHIPS - 1)) == chip
            total += jnp.where(mine, ref[2 * HEADS].astype(F32), 0.0)
    total = total + pltpu.roll(total, DIM - 32, 1) + pltpu.roll(total, DIM - 64, 1)
    bias_ref[...] = total[:HEADS, :RELS]


def call(kernel, name, specs, inputs, outputs, scratch=(), estimate=1000, params=PARAMS, space=VMEM):
    return pl.pallas_call(
        kernel,
        out_shape=tuple(outputs),
        in_specs=specs,
        out_specs=(space,) * len(outputs),
        scratch_shapes=scratch,
        compiler_params=params,
        cost_estimate=pl.CostEstimate(flops=estimate, bytes_accessed=1000, transcendentals=0),
        name=name,
    )(*inputs)


def exchange(packed):
    return lax.all_to_all(packed, "seq", split_axis=0, concat_axis=0, tiled=True)


def pair(terms, axis, mask):
    size = lax.axis_size(axis)
    return lax.ppermute(terms, axis, [(i, i ^ mask) for i in range(size)])


def sum_of_four(terms, axis, step):
    one, two, three = (pair(terms, axis, step * mask) for mask in (1, 2, 3))
    return (terms + one) + (two + three)


def move(message, s, x):
    perm = [(2 * z + c, 2 * ((z + s) % CHIPS) + (c ^ x)) for z in range(CHIPS) for c in range(2)]
    return lax.ppermute(message, "seq", perm)


def sent(messages):
    return [messages[0], *(move(m, s, 0) for m, s in zip(messages[1:], SHIFTS))]


def bfloat_parts(terms):
    parts = []
    for _ in range(3):
        part = lax.reduce_precision(terms, 8, 7)
        parts.append(jnp.pad(part, ((0, TOK - HEADS), (0, 1))))
        terms = terms - part
    return jnp.pad(jnp.concatenate(parts, axis=1), ((0, 0), (0, DIM - 96))).astype(BF)


def per_device(
    q_spatial, k_spatial, v_spatial, q_temporal, k_temporal, rel_bias, clip_ids, cotangent
):
    index = lax.axis_index("seq").astype(jnp.int32)
    z, c = index >> 1, index & 1
    pos = jnp.stack([z, c])
    away = jnp.array([d for d, x in SLOTS], jnp.int32)
    swapped = jnp.array([x for d, x in SLOTS], jnp.int32)
    frames = 2 * ((z - away) & (CHIPS - 1)) + (c ^ swapped)

    tiles = 3 * HEADS + 1
    (packed,) = call(
        pack_kernel,
        "pack",
        [SMEM] + [HBM] * 3,
        [clip_ids, q_temporal, k_temporal, cotangent],
        [units(SEQ, tiles)],
        [
            pltpu.VMEM((3, ROWS, WIDTH), BF),
            pltpu.VMEM((SEQ, tiles, TOK, DIM), BF),
            pltpu.SemaphoreType.DMA((3, PARTS)),
            pltpu.SemaphoreType.DMA((3 * PARTS + 1,)),
        ],
        space=HBM,
        params=pltpu.CompilerParams(vmem_limit_bytes=56 * 1024 * 1024),
    )
    there = exchange(packed)

    spatial = [q_spatial, k_spatial, v_spatial]
    spatial, rel_bias, frames, _ = lax.optimization_barrier((spatial, rel_bias, frames, packed))
    offsets = frames[:, None] - jnp.repeat(frames, TOK)[None, :] + (SEQ - 1)
    (bias,) = call(
        bias_kernel,
        "bias",
        [SMEM, VMEM],
        [rel_bias, offsets],
        [jax.ShapeDtypeStruct((HEADS, SEQ, ROWS), F32)],
    )
    wide = (offsets[:, :, None] == jnp.arange(RELS, dtype=jnp.int32)).astype(F32)
    keep_so, give_so, sp_prob = call(
        spatial_fwd_kernel,
        "spatial_fwd",
        [SMEM] + [VMEM] * 3,
        [pos, *spatial],
        [units(CHIPS, HEADS)] * 2 + [probs()],
    )
    give_so, bias = lax.optimization_barrier((give_so, bias))
    got_so = move(give_so, 0, 1)
    so_messages = call(
        merge_kernel, "merge", [VMEM] * 2, [keep_so, got_so], [units(2, HEADS)] * CHIPS
    )
    so = sent(so_messages)

    there, _, bias = lax.optimization_barrier((there, so_messages, bias))
    prob, mid = call(
        temporal_a_kernel,
        "temporal_a",
        [SMEM] + [VMEM] * 2,
        [frames, there, bias],
        [probs(), units(SEQ, HEADS)],
    )
    grad_mid = exchange(mid)

    back, keep_back, give_back, score_rows = call(
        temporal_b_kernel,
        "temporal_b",
        [SMEM] + [VMEM] * (2 + CHIPS),
        [frames, there, prob, *so],
        [jax.ShapeDtypeStruct((SEQ, 2, TOK, WIDTH), BF)]
        + [units(CHIPS, HEADS)] * 2
        + [jax.ShapeDtypeStruct((HEADS, SEQ, ROWS), F32)],
        estimate=LONG,
    )
    terms = jnp.einsum("hic,icr->hr", score_rows, wide, precision=lax.Precision.HIGHEST)
    terms = terms + move(terms, 0, 1)
    got_back = move(give_back, 0, 1)
    last = sent(
        call(
            merge_last_kernel,
            "merge_last",
            [VMEM] * 3,
            [bfloat_parts(terms), keep_back, got_back],
            [jax.ShapeDtypeStruct((2 * HEADS + 1, TOK, DIM), BF)] * CHIPS,
        )
    )
    returned = exchange(back)

    grad_mid, _ = lax.optimization_barrier((grad_mid, last))
    grad_qs, grad_ks, grad_vs = call(
        spatial_bwd_kernel,
        "spatial_bwd",
        [VMEM] * 5,
        [*spatial, sp_prob, grad_mid],
        [frame()] * 3,
        estimate=LONG,
    )
    last, _ = lax.optimization_barrier((last, grad_vs))
    grad_kt, total = call(
        finish_kernel,
        "finish",
        [SMEM] + [VMEM] * CHIPS,
        [pos, *last],
        [frame(), jax.ShapeDtypeStruct((HEADS, RELS), F32)],
    )
    total_bias = sum_of_four(sum_of_four(total, "grp", 1), "grp", 4)
    result, grad_qt = call(
        unpack_kernel,
        "unpack",
        [VMEM],
        [returned],
        [frame()] * 2,
        [pltpu.SemaphoreType.DMA((2, SEQ))],
        space=HBM,
    )
    return result, grad_qs, grad_ks, grad_vs, grad_qt, grad_kt, total_bias


def solution(mesh):
    frames = P(("grp", "seq"), None, None)
    return jax.shard_map(
        per_device,
        mesh=mesh,
        in_specs=(frames,) * 5 + (P(), P("grp", "seq"), frames),
        out_specs=(frames,) * 6 + (P(),),
        check_vma=False,
    )
```

```python
import jax
import jax.numpy as jnp
from jax import lax
from jax.experimental import pallas as pl
from jax.experimental.pallas import tpu as pltpu
from jax.sharding import PartitionSpec as P

HEADS = 12
DIM = 128
RELS = 31
SEQ = 16
CHIPS = 8
TOK = 16
ROWS = SEQ * TOK
WIDTH = HEADS * DIM
SCALE = DIM ** (-0.5)
NEG = -1e30
BF = jnp.bfloat16
F32 = jnp.float32
PARAMS = pltpu.CompilerParams(vmem_limit_bytes=48 * 1024 * 1024)
PARTS = 4
LONG = 10**12
VMEM = pl.BlockSpec(memory_space=pltpu.VMEM)
SMEM = pl.BlockSpec(memory_space=pltpu.SMEM)
HBM = pl.BlockSpec(memory_space=pltpu.HBM)


def mm(left, right):
    return lax.dot_general(left, right, (((1,), (0,)), ((), ())), preferred_element_type=F32)


def mm_nt(left, right):
    return lax.dot_general(left, right, (((1,), (1,)), ((), ())), preferred_element_type=F32)


def mm_tn(left, right):
    return lax.dot_general(left, right, (((0,), (0,)), ((), ())), preferred_element_type=F32)


def softmax(scores):
    raw = jnp.exp(scores - jnp.max(scores, axis=-1, keepdims=True))
    return raw / jnp.sum(raw, axis=-1, keepdims=True)


def units(n, tiles):
    return jax.ShapeDtypeStruct((n, tiles, TOK, DIM), BF)


def frame():
    return jax.ShapeDtypeStruct((1, ROWS, WIDTH), BF)


def probs():
    return jax.ShapeDtypeStruct((HEADS, ROWS, ROWS), F32)


def range_row(chip, core):
    return pl.multiple_of((2 * (chip & (CHIPS - 1)) + core) * TOK, TOK)


def head(h):
    return slice(h * DIM, (h + 1) * DIM)


def rows_of(ref, tile):
    return ref[:, tile].reshape(ROWS, DIM)


SHIFTS = (1, -1, 3, -3, 2, -2, 4)
SLOTS = tuple((d, x) for x in range(2) for d in range(CHIPS))


def slot_rows(frames_ref, ref, tile):
    return jnp.concatenate([ref[frames_ref[s], tile] for s in range(SEQ)], axis=0)


def put_pairs(keep_ref, give_ref, tile, value):
    low = value.astype(BF)
    for d in range(CHIPS):
        keep_ref[d, tile] = low[d * TOK:(d + 1) * TOK]
        give_ref[d, tile] = low[(CHIPS + d) * TOK:(CHIPS + d + 1) * TOK]


def put_frames(frames_ref, ref, i, h, value):
    low = value.astype(BF)
    for s in range(SEQ):
        ref[frames_ref[s], i, :, head(h)] = low[s * TOK:(s + 1) * TOK]


def pack_kernel(clip_ref, q_ref, k_ref, up_ref, out_ref, held, made, sems, out_sems):
    copies = []
    size, units_of = ROWS // PARTS, SEQ // PARTS
    for i, ref in enumerate((q_ref, k_ref, up_ref)):
        for part in range(PARTS):
            rows = pl.ds(part * size, size)
            copies.append(
                pltpu.make_async_copy(ref.at[0, rows], held.at[i, rows], sems.at[i, part])
            )
            copies[-1].start()
    last = pl.ds(3 * HEADS, 1)
    clip = jnp.full((SEQ, TOK, DIM), clip_ref[0, 0], jnp.int32).astype(F32).astype(BF)
    made[:, 3 * HEADS] = clip
    outs = [pltpu.make_async_copy(made.at[:, last], out_ref.at[:, last], out_sems.at[3 * PARTS])]
    outs[-1].start()
    for i in range(3):
        for part in range(PARTS):
            copies[i * PARTS + part].wait()
            units = pl.ds(part * units_of, units_of)
            for h in range(HEADS):
                block = held[i, part * size:(part + 1) * size, head(h)]
                made[units, i * HEADS + h] = block.reshape(units_of, TOK, DIM)
            at = (units, pl.ds(i * HEADS, HEADS))
            outs.append(
                pltpu.make_async_copy(made.at[at], out_ref.at[at], out_sems.at[i * PARTS + part])
            )
            outs[-1].start()
    for copy in outs:
        copy.wait()


def spatial_fwd_kernel(pos_ref, q_ref, k_ref, v_ref, keep_ref, give_ref, prob_ref):
    z, first = pos_ref[0], pos_ref[1] == 0
    for h in range(HEADS):
        prob = softmax(mm_nt(q_ref[0, :, head(h)], k_ref[0, :, head(h)]) * SCALE)
        prob_ref[h] = prob
        out = mm(prob.astype(BF), v_ref[0, :, head(h)])
        for chip in range(CHIPS):
            even = out[2 * chip * TOK:(2 * chip + 1) * TOK]
            odd = out[(2 * chip + 1) * TOK:(2 * chip + 2) * TOK]
            shift = (chip - z) & (CHIPS - 1)
            keep_ref[shift, h] = jnp.where(first, even, odd).astype(BF)
            give_ref[shift, h] = jnp.where(first, odd, even).astype(BF)


def merge_kernel(keep_ref, got_ref, *outs):
    for out, shift in zip(outs, (0,) + SHIFTS):
        out[0] = keep_ref[shift % CHIPS]
        out[1] = got_ref[shift % CHIPS]


def merge_last_kernel(tile_ref, keep_ref, got_ref, *outs):
    for out, shift in zip(outs, (0,) + SHIFTS):
        out[:HEADS] = keep_ref[-shift % CHIPS]
        out[HEADS:2 * HEADS] = got_ref[-shift % CHIPS]
        out[2 * HEADS] = tile_ref[...]


def pair_rows(pos_ref, shift):
    z, c = pos_ref[0], pos_ref[1]
    return range_row(z - shift, c), range_row(z - shift, 1 - c)


def spatial_bwd_kernel(q_ref, k_ref, v_ref, prob_ref, mid_ref, gq_ref, gk_ref, gv_ref):
    for h in range(HEADS):
        q, k, v = q_ref[0, :, head(h)], k_ref[0, :, head(h)], v_ref[0, :, head(h)]
        up = rows_of(mid_ref, h)
        prob = prob_ref[h]
        grad_prob = mm_nt(up, v)
        gv_ref[0, :, head(h)] = mm_tn(prob.astype(BF), up).astype(BF)
        row_dot = jnp.sum(prob * grad_prob, axis=-1, keepdims=True)
        low = (prob * (grad_prob - row_dot) * SCALE).astype(BF)
        gq_ref[0, :, head(h)] = mm(low, k).astype(BF)
        gk_ref[0, :, head(h)] = mm_tn(low, q).astype(BF)


def bias_kernel(rel_ref, offsets_ref, out_ref):
    offsets = offsets_ref[...]
    for h in range(HEADS):
        table = jnp.zeros((SEQ, ROWS), F32)
        for r in range(RELS):
            table = jnp.where(offsets == r, rel_ref[h, r], table)
        out_ref[h] = table


def temporal_mask(frames_ref, in_ref):
    row = lax.broadcasted_iota(jnp.int32, (ROWS, ROWS), 0)
    col = lax.broadcasted_iota(jnp.int32, (ROWS, ROWS), 1)
    clip = slot_rows(frames_ref, in_ref, 3 * HEADS).astype(F32)
    other = clip.T
    same = (row & (TOK - 1)) == (col & (TOK - 1))
    same &= jnp.concatenate([clip] * 2, axis=1) == jnp.concatenate([other] * 2, axis=0)
    return jnp.where(same, 0.0, NEG)


def temporal_prob(q, k, bias, mask):
    bias = jnp.broadcast_to(bias[:, None, :], (SEQ, TOK, ROWS)).reshape(ROWS, ROWS)
    return softmax((mm_nt(q, k) * SCALE + bias) + mask)


def temporal_a_kernel(frames_ref, in_ref, bias_ref, mid_ref):
    mask = temporal_mask(frames_ref, in_ref)
    for h in range(HEADS):
        q, k, up = (slot_rows(frames_ref, in_ref, i * HEADS + h) for i in range(3))
        prob = temporal_prob(q, k, bias_ref[h], mask)
        mid = mm_tn(prob.astype(BF), up).astype(BF)
        for s in range(SEQ):
            mid_ref[frames_ref[s], h] = mid[s * TOK:(s + 1) * TOK]


def temporal_b_kernel(frames_ref, in_ref, bias_ref, *refs):
    so_refs, (out_ref, keep_ref, give_ref, rows_ref) = dict(zip((0,) + SHIFTS, refs)), refs[-4:]
    so_at = [(so_refs[d if d <= CHIPS // 2 else d - CHIPS], x) for d, x in SLOTS]
    mask = temporal_mask(frames_ref, in_ref)
    for h in range(HEADS):
        q, k, up = (slot_rows(frames_ref, in_ref, i * HEADS + h) for i in range(3))
        so = jnp.concatenate([ref[x, h] for ref, x in so_at], axis=0)
        prob = temporal_prob(q, k, bias_ref[h], mask)
        grad_prob = mm_nt(up, so)
        put_frames(frames_ref, out_ref, 0, h, mm(prob.astype(BF), so))
        score = prob * (grad_prob - jnp.sum(prob * grad_prob, axis=-1, keepdims=True))
        rows_ref[h] = jnp.sum(score.reshape(SEQ, TOK, ROWS), axis=1)
        low = (score * SCALE).astype(BF)
        put_frames(frames_ref, out_ref, 1, h, mm(low, k))
        put_pairs(keep_ref, give_ref, h, mm_tn(low, q))


def unpack_kernel(in_ref, res_ref, gq_ref, held, in_sems, out_sems):
    pieces = [(u, i) for u in range(SEQ) for i in range(2)]
    ins = [
        pltpu.make_async_copy(in_ref.at[u, i], held.at[u, i], in_sems.at[u, i]) for u, i in pieces
    ]
    for copy in ins:
        copy.start()
    outs = []
    for copy, (u, i) in zip(ins, pieces):
        copy.wait()
        out = (res_ref, gq_ref)[i].at[0, pl.ds(u * TOK, TOK)]
        outs.append(pltpu.make_async_copy(held.at[u, i], out, out_sems.at[u, i]))
        outs[-1].start()
    for copy in outs:
        copy.wait()


def finish_kernel(pos_ref, *refs):
    messages, (gk_ref, bias_ref) = refs[:CHIPS], refs[CHIPS:]
    for ref, shift in zip(messages, (0,) + SHIFTS):
        for x, row in enumerate(pair_rows(pos_ref, shift)):
            for h in range(HEADS):
                gk_ref[0, pl.ds(row, TOK), head(h)] = ref[x * HEADS + h]
    z = pos_ref[0]
    total = jnp.zeros((TOK, DIM), F32)
    for chip in range(CHIPS):
        for ref, shift in zip(messages, (0,) + SHIFTS):
            mine = ((z - shift) & (CHIPS - 1)) == chip
            total += jnp.where(mine, ref[2 * HEADS].astype(F32), 0.0)
    total = total + pltpu.roll(total, DIM - 32, 1) + pltpu.roll(total, DIM - 64, 1)
    bias_ref[...] = total[:HEADS, :RELS]


def call(kernel, name, specs, inputs, outputs, scratch=(), estimate=1000, params=PARAMS, space=VMEM):
    return pl.pallas_call(
        kernel,
        out_shape=tuple(outputs),
        in_specs=specs,
        out_specs=(space,) * len(outputs),
        scratch_shapes=scratch,
        compiler_params=params,
        cost_estimate=pl.CostEstimate(flops=estimate, bytes_accessed=1000, transcendentals=0),
        name=name,
    )(*inputs)


def exchange(packed):
    return lax.all_to_all(packed, "seq", split_axis=0, concat_axis=0, tiled=True)


def pair(terms, axis, mask):
    size = lax.axis_size(axis)
    return lax.ppermute(terms, axis, [(i, i ^ mask) for i in range(size)])


def sum_of_four(terms, axis, step):
    one, two, three = (pair(terms, axis, step * mask) for mask in (1, 2, 3))
    return (terms + one) + (two + three)


def move(message, s, x):
    perm = [(2 * z + c, 2 * ((z + s) % CHIPS) + (c ^ x)) for z in range(CHIPS) for c in range(2)]
    return lax.ppermute(message, "seq", perm)


def sent(messages):
    return [messages[0], *(move(m, s, 0) for m, s in zip(messages[1:], SHIFTS))]


def bfloat_parts(terms):
    parts = []
    for _ in range(3):
        part = lax.reduce_precision(terms, 8, 7)
        parts.append(jnp.pad(part, ((0, TOK - HEADS), (0, 1))))
        terms = terms - part
    return jnp.pad(jnp.concatenate(parts, axis=1), ((0, 0), (0, DIM - 96))).astype(BF)


def per_device(
    q_spatial, k_spatial, v_spatial, q_temporal, k_temporal, rel_bias, clip_ids, cotangent
):
    index = lax.axis_index("seq").astype(jnp.int32)
    z, c = index >> 1, index & 1
    pos = jnp.stack([z, c])
    away = jnp.array([d for d, x in SLOTS], jnp.int32)
    swapped = jnp.array([x for d, x in SLOTS], jnp.int32)
    frames = 2 * ((z - away) & (CHIPS - 1)) + (c ^ swapped)

    tiles = 3 * HEADS + 1
    (packed,) = call(
        pack_kernel,
        "pack",
        [SMEM] + [HBM] * 3,
        [clip_ids, q_temporal, k_temporal, cotangent],
        [units(SEQ, tiles)],
        [
            pltpu.VMEM((3, ROWS, WIDTH), BF),
            pltpu.VMEM((SEQ, tiles, TOK, DIM), BF),
            pltpu.SemaphoreType.DMA((3, PARTS)),
            pltpu.SemaphoreType.DMA((3 * PARTS + 1,)),
        ],
        space=HBM,
        params=pltpu.CompilerParams(vmem_limit_bytes=56 * 1024 * 1024),
    )
    there = exchange(packed)

    spatial = [q_spatial, k_spatial, v_spatial]
    spatial, rel_bias, frames, _ = lax.optimization_barrier((spatial, rel_bias, frames, packed))
    offsets = frames[:, None] - jnp.repeat(frames, TOK)[None, :] + (SEQ - 1)
    (bias,) = call(
        bias_kernel,
        "bias",
        [SMEM, VMEM],
        [rel_bias, offsets],
        [jax.ShapeDtypeStruct((HEADS, SEQ, ROWS), F32)],
    )
    wide = (offsets[:, :, None] == jnp.arange(RELS, dtype=jnp.int32)).astype(F32)
    keep_so, give_so, sp_prob = call(
        spatial_fwd_kernel,
        "spatial_fwd",
        [SMEM] + [VMEM] * 3,
        [pos, *spatial],
        [units(CHIPS, HEADS)] * 2 + [probs()],
    )
    give_so, bias = lax.optimization_barrier((give_so, bias))
    got_so = move(give_so, 0, 1)
    so_messages = call(
        merge_kernel, "merge", [VMEM] * 2, [keep_so, got_so], [units(2, HEADS)] * CHIPS
    )
    so = sent(so_messages)

    there, _, bias = lax.optimization_barrier((there, so_messages, bias))
    (mid,) = call(
        temporal_a_kernel,
        "temporal_a",
        [SMEM] + [VMEM] * 2,
        [frames, there, bias],
        [units(SEQ, HEADS)],
    )
    grad_mid = exchange(mid)

    back, keep_back, give_back, score_rows = call(
        temporal_b_kernel,
        "temporal_b",
        [SMEM] + [VMEM] * (2 + CHIPS),
        [frames, there, bias, *so],
        [jax.ShapeDtypeStruct((SEQ, 2, TOK, WIDTH), BF)]
        + [units(CHIPS, HEADS)] * 2
        + [jax.ShapeDtypeStruct((HEADS, SEQ, ROWS), F32)],
        estimate=LONG,
    )
    terms = jnp.einsum("hic,icr->hr", score_rows, wide, precision=lax.Precision.HIGHEST)
    terms = terms + move(terms, 0, 1)
    got_back = move(give_back, 0, 1)
    last = sent(
        call(
            merge_last_kernel,
            "merge_last",
            [VMEM] * 3,
            [bfloat_parts(terms), keep_back, got_back],
            [jax.ShapeDtypeStruct((2 * HEADS + 1, TOK, DIM), BF)] * CHIPS,
        )
    )
    returned = exchange(back)

    grad_mid, _ = lax.optimization_barrier((grad_mid, last))
    grad_qs, grad_ks, grad_vs = call(
        spatial_bwd_kernel,
        "spatial_bwd",
        [VMEM] * 5,
        [*spatial, sp_prob, grad_mid],
        [frame()] * 3,
        estimate=LONG,
    )
    last, _ = lax.optimization_barrier((last, grad_vs))
    grad_kt, total = call(
        finish_kernel,
        "finish",
        [SMEM] + [VMEM] * CHIPS,
        [pos, *last],
        [frame(), jax.ShapeDtypeStruct((HEADS, RELS), F32)],
    )
    total_bias = sum_of_four(sum_of_four(total, "grp", 1), "grp", 4)
    result, grad_qt = call(
        unpack_kernel,
        "unpack",
        [HBM],
        [returned],
        [frame()] * 2,
        [
            pltpu.VMEM((SEQ, 2, TOK, WIDTH), BF),
            pltpu.SemaphoreType.DMA((SEQ, 2)),
            pltpu.SemaphoreType.DMA((SEQ, 2)),
        ],
        space=HBM,
    )
    return result, grad_qs, grad_ks, grad_vs, grad_qt, grad_kt, total_bias


def solution(mesh):
    frames = P(("grp", "seq"), None, None)
    return jax.shard_map(
        per_device,
        mesh=mesh,
        in_specs=(frames,) * 5 + (P(), P("grp", "seq"), frames),
        out_specs=(frames,) * 6 + (P(),),
        check_vma=False,
    )
```

```python
import jax
import jax.numpy as jnp
from jax import lax
from jax.experimental import pallas as pl
from jax.experimental.pallas import tpu as pltpu
from jax.sharding import PartitionSpec as P

HEADS = 12
DIM = 128
RELS = 31
SEQ = 16
CHIPS = 8
TOK = 16
ROWS = SEQ * TOK
WIDTH = HEADS * DIM
SCALE = DIM ** (-0.5)
NEG = -1e30
BF = jnp.bfloat16
F32 = jnp.float32
PARAMS = pltpu.CompilerParams(vmem_limit_bytes=48 * 1024 * 1024)
PARTS = 4
LONG = 10**12
VMEM = pl.BlockSpec(memory_space=pltpu.VMEM)
SMEM = pl.BlockSpec(memory_space=pltpu.SMEM)
HBM = pl.BlockSpec(memory_space=pltpu.HBM)


def mm(left, right):
    return lax.dot_general(left, right, (((1,), (0,)), ((), ())), preferred_element_type=F32)


def mm_nt(left, right):
    return lax.dot_general(left, right, (((1,), (1,)), ((), ())), preferred_element_type=F32)


def mm_tn(left, right):
    return lax.dot_general(left, right, (((0,), (0,)), ((), ())), preferred_element_type=F32)


def softmax(scores):
    raw = jnp.exp(scores - jnp.max(scores, axis=-1, keepdims=True))
    return raw / jnp.sum(raw, axis=-1, keepdims=True)


def units(n, tiles):
    return jax.ShapeDtypeStruct((n, tiles, TOK, DIM), BF)


def frame():
    return jax.ShapeDtypeStruct((1, ROWS, WIDTH), BF)


def probs():
    return jax.ShapeDtypeStruct((HEADS, ROWS, ROWS), F32)


def range_row(chip, core):
    return pl.multiple_of((2 * (chip & (CHIPS - 1)) + core) * TOK, TOK)


def head(h):
    return slice(h * DIM, (h + 1) * DIM)


def rows_of(ref, tile):
    return ref[:, tile].reshape(ROWS, DIM)


SHIFTS = (1, -1, 3, -3, 2, -2, 4)
SLOTS = tuple((d, x) for x in range(2) for d in range(CHIPS))


def slot_rows(frames_ref, ref, tile):
    return jnp.concatenate([ref[frames_ref[s], tile] for s in range(SEQ)], axis=0)


def put_pairs(keep_ref, give_ref, tile, value):
    low = value.astype(BF)
    for d in range(CHIPS):
        keep_ref[d, tile] = low[d * TOK:(d + 1) * TOK]
        give_ref[d, tile] = low[(CHIPS + d) * TOK:(CHIPS + d + 1) * TOK]


def put_frames(frames_ref, ref, i, h, value):
    low = value.astype(BF)
    for s in range(SEQ):
        ref[frames_ref[s], i, :, head(h)] = low[s * TOK:(s + 1) * TOK]


def pack_kernel(clip_ref, q_ref, k_ref, up_ref, out_ref, held, made, sems, out_sems):
    copies = []
    size, units_of = ROWS // PARTS, SEQ // PARTS
    for i, ref in enumerate((q_ref, k_ref, up_ref)):
        for part in range(PARTS):
            rows = pl.ds(part * size, size)
            copies.append(
                pltpu.make_async_copy(ref.at[0, rows], held.at[i, rows], sems.at[i, part])
            )
            copies[-1].start()
    last = pl.ds(3 * HEADS, 1)
    clip = jnp.full((SEQ, TOK, DIM), clip_ref[0, 0], jnp.int32).astype(F32).astype(BF)
    made[:, 3 * HEADS] = clip
    outs = [pltpu.make_async_copy(made.at[:, last], out_ref.at[:, last], out_sems.at[3 * PARTS])]
    outs[-1].start()
    for i in range(3):
        for part in range(PARTS):
            copies[i * PARTS + part].wait()
            units = pl.ds(part * units_of, units_of)
            for h in range(HEADS):
                block = held[i, part * size:(part + 1) * size, head(h)]
                made[units, i * HEADS + h] = block.reshape(units_of, TOK, DIM)
            at = (units, pl.ds(i * HEADS, HEADS))
            outs.append(
                pltpu.make_async_copy(made.at[at], out_ref.at[at], out_sems.at[i * PARTS + part])
            )
            outs[-1].start()
    for copy in outs:
        copy.wait()


def spatial_fwd_kernel(pos_ref, q_ref, k_ref, v_ref, keep_ref, give_ref, prob_ref):
    z, first = pos_ref[0], pos_ref[1] == 0
    for h in range(HEADS):
        prob = softmax(mm_nt(q_ref[0, :, head(h)], k_ref[0, :, head(h)]) * SCALE)
        prob_ref[h] = prob
        out = mm(prob.astype(BF), v_ref[0, :, head(h)])
        for chip in range(CHIPS):
            even = out[2 * chip * TOK:(2 * chip + 1) * TOK]
            odd = out[(2 * chip + 1) * TOK:(2 * chip + 2) * TOK]
            shift = (chip - z) & (CHIPS - 1)
            keep_ref[shift, h] = jnp.where(first, even, odd).astype(BF)
            give_ref[shift, h] = jnp.where(first, odd, even).astype(BF)


def merge_kernel(keep_ref, got_ref, *outs):
    for out, shift in zip(outs, (0,) + SHIFTS):
        out[0] = keep_ref[shift % CHIPS]
        out[1] = got_ref[shift % CHIPS]


def merge_last_kernel(tile_ref, keep_ref, got_ref, *outs):
    for out, shift in zip(outs, (0,) + SHIFTS):
        out[:HEADS] = keep_ref[-shift % CHIPS]
        out[HEADS:2 * HEADS] = got_ref[-shift % CHIPS]
        out[2 * HEADS] = tile_ref[...]


def pair_rows(pos_ref, shift):
    z, c = pos_ref[0], pos_ref[1]
    return range_row(z - shift, c), range_row(z - shift, 1 - c)


def spatial_bwd_kernel(q_ref, k_ref, v_ref, prob_ref, mid_ref, gq_ref, gk_ref, gv_ref):
    for h in range(HEADS):
        q, k, v = q_ref[0, :, head(h)], k_ref[0, :, head(h)], v_ref[0, :, head(h)]
        up = rows_of(mid_ref, h)
        prob = prob_ref[h]
        grad_prob = mm_nt(up, v)
        gv_ref[0, :, head(h)] = mm_tn(prob.astype(BF), up).astype(BF)
        row_dot = jnp.sum(prob * grad_prob, axis=-1, keepdims=True)
        low = (prob * (grad_prob - row_dot) * SCALE).astype(BF)
        gq_ref[0, :, head(h)] = mm(low, k).astype(BF)
        gk_ref[0, :, head(h)] = mm_tn(low, q).astype(BF)


def bias_kernel(rel_ref, offsets_ref, out_ref):
    offsets = offsets_ref[...]
    for h in range(HEADS):
        table = jnp.zeros((SEQ, ROWS), F32)
        for r in range(RELS):
            table = jnp.where(offsets == r, rel_ref[h, r], table)
        out_ref[h] = table


def temporal_mask(frames_ref, in_ref):
    row = lax.broadcasted_iota(jnp.int32, (ROWS, ROWS), 0)
    col = lax.broadcasted_iota(jnp.int32, (ROWS, ROWS), 1)
    clip = slot_rows(frames_ref, in_ref, 3 * HEADS).astype(F32)
    other = clip.T
    same = (row & (TOK - 1)) == (col & (TOK - 1))
    same &= jnp.concatenate([clip] * 2, axis=1) == jnp.concatenate([other] * 2, axis=0)
    return jnp.where(same, 0.0, NEG)


def temporal_prob(q, k, bias, mask):
    bias = jnp.broadcast_to(bias[:, None, :], (SEQ, TOK, ROWS)).reshape(ROWS, ROWS)
    return softmax((mm_nt(q, k) * SCALE + bias) + mask)


def temporal_a_kernel(frames_ref, in_ref, bias_ref, mid_ref):
    mask = temporal_mask(frames_ref, in_ref)
    for h in range(HEADS):
        q, k, up = (slot_rows(frames_ref, in_ref, i * HEADS + h) for i in range(3))
        prob = temporal_prob(q, k, bias_ref[h], mask)
        mid = mm_tn(prob.astype(BF), up).astype(BF)
        for s in range(SEQ):
            mid_ref[frames_ref[s], h] = mid[s * TOK:(s + 1) * TOK]


def temporal_b_kernel(frames_ref, in_ref, bias_ref, *refs):
    so_refs, (out_ref, keep_ref, give_ref, rows_ref) = dict(zip((0,) + SHIFTS, refs)), refs[-4:]
    so_at = [(so_refs[d if d <= CHIPS // 2 else d - CHIPS], x) for d, x in SLOTS]
    mask = temporal_mask(frames_ref, in_ref)
    for h in range(HEADS):
        q, k, up = (slot_rows(frames_ref, in_ref, i * HEADS + h) for i in range(3))
        so = jnp.concatenate([ref[x, h] for ref, x in so_at], axis=0)
        prob = temporal_prob(q, k, bias_ref[h], mask)
        grad_prob = mm_nt(up, so)
        put_frames(frames_ref, out_ref, 0, h, mm(prob.astype(BF), so))
        score = prob * (grad_prob - jnp.sum(prob * grad_prob, axis=-1, keepdims=True))
        rows_ref[h] = jnp.sum(score.reshape(SEQ, TOK, ROWS), axis=1)
        low = (score * SCALE).astype(BF)
        put_frames(frames_ref, out_ref, 1, h, mm(low, k))
        put_pairs(keep_ref, give_ref, h, mm_tn(low, q))


def finish_kernel(pos_ref, *refs):
    messages, (gk_ref, bias_ref) = refs[:CHIPS], refs[CHIPS:]
    for ref, shift in zip(messages, (0,) + SHIFTS):
        for x, row in enumerate(pair_rows(pos_ref, shift)):
            for h in range(HEADS):
                gk_ref[0, pl.ds(row, TOK), head(h)] = ref[x * HEADS + h]
    z = pos_ref[0]
    total = jnp.zeros((TOK, DIM), F32)
    for chip in range(CHIPS):
        for ref, shift in zip(messages, (0,) + SHIFTS):
            mine = ((z - shift) & (CHIPS - 1)) == chip
            total += jnp.where(mine, ref[2 * HEADS].astype(F32), 0.0)
    total = total + pltpu.roll(total, DIM - 32, 1) + pltpu.roll(total, DIM - 64, 1)
    bias_ref[...] = total[:HEADS, :RELS]


def call(kernel, name, specs, inputs, outputs, scratch=(), estimate=1000, params=PARAMS, space=VMEM):
    return pl.pallas_call(
        kernel,
        out_shape=tuple(outputs),
        in_specs=specs,
        out_specs=(space,) * len(outputs),
        scratch_shapes=scratch,
        compiler_params=params,
        cost_estimate=pl.CostEstimate(flops=estimate, bytes_accessed=1000, transcendentals=0),
        name=name,
    )(*inputs)


def exchange(packed):
    return lax.all_to_all(packed, "seq", split_axis=0, concat_axis=0, tiled=True)


def pair(terms, axis, mask):
    size = lax.axis_size(axis)
    return lax.ppermute(terms, axis, [(i, i ^ mask) for i in range(size)])


def sum_of_four(terms, axis, step):
    one, two, three = (pair(terms, axis, step * mask) for mask in (1, 2, 3))
    return (terms + one) + (two + three)


def move(message, s, x):
    perm = [(2 * z + c, 2 * ((z + s) % CHIPS) + (c ^ x)) for z in range(CHIPS) for c in range(2)]
    return lax.ppermute(message, "seq", perm)


def sent(messages):
    return [messages[0], *(move(m, s, 0) for m, s in zip(messages[1:], SHIFTS))]


def bfloat_parts(terms):
    parts = []
    for _ in range(3):
        part = lax.reduce_precision(terms, 8, 7)
        parts.append(jnp.pad(part, ((0, TOK - HEADS), (0, 1))))
        terms = terms - part
    return jnp.pad(jnp.concatenate(parts, axis=1), ((0, 0), (0, DIM - 96))).astype(BF)


def per_device(
    q_spatial, k_spatial, v_spatial, q_temporal, k_temporal, rel_bias, clip_ids, cotangent
):
    index = lax.axis_index("seq").astype(jnp.int32)
    z, c = index >> 1, index & 1
    pos = jnp.stack([z, c])
    away = jnp.array([d for d, x in SLOTS], jnp.int32)
    swapped = jnp.array([x for d, x in SLOTS], jnp.int32)
    frames = 2 * ((z - away) & (CHIPS - 1)) + (c ^ swapped)

    tiles = 3 * HEADS + 1
    (packed,) = call(
        pack_kernel,
        "pack",
        [SMEM] + [HBM] * 3,
        [clip_ids, q_temporal, k_temporal, cotangent],
        [units(SEQ, tiles)],
        [
            pltpu.VMEM((3, ROWS, WIDTH), BF),
            pltpu.VMEM((SEQ, tiles, TOK, DIM), BF),
            pltpu.SemaphoreType.DMA((3, PARTS)),
            pltpu.SemaphoreType.DMA((3 * PARTS + 1,)),
        ],
        space=HBM,
        params=pltpu.CompilerParams(vmem_limit_bytes=56 * 1024 * 1024),
    )
    there = exchange(packed)

    spatial = [q_spatial, k_spatial, v_spatial]
    spatial, rel_bias, frames, _ = lax.optimization_barrier((spatial, rel_bias, frames, packed))
    offsets = frames[:, None] - jnp.repeat(frames, TOK)[None, :] + (SEQ - 1)
    (bias,) = call(
        bias_kernel,
        "bias",
        [SMEM, VMEM],
        [rel_bias, offsets],
        [jax.ShapeDtypeStruct((HEADS, SEQ, ROWS), F32)],
    )
    wide = (offsets[:, :, None] == jnp.arange(RELS, dtype=jnp.int32)).astype(F32)
    keep_so, give_so, sp_prob = call(
        spatial_fwd_kernel,
        "spatial_fwd",
        [SMEM] + [VMEM] * 3,
        [pos, *spatial],
        [units(CHIPS, HEADS)] * 2 + [probs()],
    )
    give_so, bias = lax.optimization_barrier((give_so, bias))
    got_so = move(give_so, 0, 1)
    so_messages = call(
        merge_kernel, "merge", [VMEM] * 2, [keep_so, got_so], [units(2, HEADS)] * CHIPS
    )
    so = sent(so_messages)

    there, _, bias = lax.optimization_barrier((there, so_messages, bias))
    (mid,) = call(
        temporal_a_kernel,
        "temporal_a",
        [SMEM] + [VMEM] * 2,
        [frames, there, bias],
        [units(SEQ, HEADS)],
    )
    grad_mid = exchange(mid)

    back, keep_back, give_back, score_rows = call(
        temporal_b_kernel,
        "temporal_b",
        [SMEM] + [VMEM] * (2 + CHIPS),
        [frames, there, bias, *so],
        [jax.ShapeDtypeStruct((SEQ, 2, TOK, WIDTH), BF)]
        + [units(CHIPS, HEADS)] * 2
        + [jax.ShapeDtypeStruct((HEADS, SEQ, ROWS), F32)],
        estimate=LONG,
    )
    terms = jnp.einsum("hic,icr->hr", score_rows, wide, precision=lax.Precision.HIGHEST)
    terms = terms + move(terms, 0, 1)
    got_back = move(give_back, 0, 1)
    last = sent(
        call(
            merge_last_kernel,
            "merge_last",
            [VMEM] * 3,
            [bfloat_parts(terms), keep_back, got_back],
            [jax.ShapeDtypeStruct((2 * HEADS + 1, TOK, DIM), BF)] * CHIPS,
        )
    )
    returned = exchange(back)

    grad_mid, _ = lax.optimization_barrier((grad_mid, last))
    grad_qs, grad_ks, grad_vs = call(
        spatial_bwd_kernel,
        "spatial_bwd",
        [VMEM] * 5,
        [*spatial, sp_prob, grad_mid],
        [frame()] * 3,
        estimate=LONG,
    )
    last, _ = lax.optimization_barrier((last, grad_vs))
    grad_kt, total = call(
        finish_kernel,
        "finish",
        [SMEM] + [VMEM] * CHIPS,
        [pos, *last],
        [frame(), jax.ShapeDtypeStruct((HEADS, RELS), F32)],
    )
    total_bias = sum_of_four(sum_of_four(total, "grp", 1), "grp", 4)
    result, grad_qt = (returned[:, i].reshape(1, ROWS, WIDTH) for i in range(2))
    return result, grad_qs, grad_ks, grad_vs, grad_qt, grad_kt, total_bias


def solution(mesh):
    frames = P(("grp", "seq"), None, None)
    return jax.shard_map(
        per_device,
        mesh=mesh,
        in_specs=(frames,) * 5 + (P(), P("grp", "seq"), frames),
        out_specs=(frames,) * 6 + (P(),),
        check_vma=False,
    )
```

```python
import jax
import jax.numpy as jnp
from jax import lax
from jax.experimental import pallas as pl
from jax.experimental.pallas import tpu as pltpu
from jax.sharding import PartitionSpec as P

HEADS = 12
DIM = 128
RELS = 31
SEQ = 16
CHIPS = 8
TOK = 16
ROWS = SEQ * TOK
WIDTH = HEADS * DIM
SCALE = DIM ** (-0.5)
NEG = -1e30
BF = jnp.bfloat16
F32 = jnp.float32
PARAMS = pltpu.CompilerParams(vmem_limit_bytes=48 * 1024 * 1024)
PARTS = 4
LONG = 10**11
VMEM = pl.BlockSpec(memory_space=pltpu.VMEM)
SMEM = pl.BlockSpec(memory_space=pltpu.SMEM)
HBM = pl.BlockSpec(memory_space=pltpu.HBM)


def mm(left, right):
    return lax.dot_general(left, right, (((1,), (0,)), ((), ())), preferred_element_type=F32)


def mm_nt(left, right):
    return lax.dot_general(left, right, (((1,), (1,)), ((), ())), preferred_element_type=F32)


def mm_tn(left, right):
    return lax.dot_general(left, right, (((0,), (0,)), ((), ())), preferred_element_type=F32)


def softmax(scores):
    raw = jnp.exp(scores - jnp.max(scores, axis=-1, keepdims=True))
    return raw / jnp.sum(raw, axis=-1, keepdims=True)


def units(n, tiles):
    return jax.ShapeDtypeStruct((n, tiles, TOK, DIM), BF)


def frame():
    return jax.ShapeDtypeStruct((1, ROWS, WIDTH), BF)


def probs():
    return jax.ShapeDtypeStruct((HEADS, ROWS, ROWS), F32)


def range_row(chip, core):
    return pl.multiple_of((2 * (chip & (CHIPS - 1)) + core) * TOK, TOK)


def head(h):
    return slice(h * DIM, (h + 1) * DIM)


def rows_of(ref, tile):
    return ref[:, tile].reshape(ROWS, DIM)


SHIFTS = (1, -1, 3, -3, 2, -2, 4)
SLOTS = tuple((d, x) for x in range(2) for d in range(CHIPS))


def slot_rows(frames_ref, ref, tile):
    return jnp.concatenate([ref[frames_ref[s], tile] for s in range(SEQ)], axis=0)


def put_pairs(keep_ref, give_ref, tile, value):
    low = value.astype(BF)
    for d in range(CHIPS):
        keep_ref[d, tile] = low[d * TOK:(d + 1) * TOK]
        give_ref[d, tile] = low[(CHIPS + d) * TOK:(CHIPS + d + 1) * TOK]


def put_frames(frames_ref, ref, i, h, value):
    low = value.astype(BF)
    for s in range(SEQ):
        ref[frames_ref[s], i, :, head(h)] = low[s * TOK:(s + 1) * TOK]


def pack_kernel(clip_ref, q_ref, k_ref, up_ref, out_ref, held, made, sems, out_sems):
    copies = []
    size, units_of = ROWS // PARTS, SEQ // PARTS
    for i, ref in enumerate((q_ref, k_ref, up_ref)):
        for part in range(PARTS):
            rows = pl.ds(part * size, size)
            copies.append(
                pltpu.make_async_copy(ref.at[0, rows], held.at[i, rows], sems.at[i, part])
            )
            copies[-1].start()
    last = pl.ds(3 * HEADS, 1)
    clip = jnp.full((SEQ, TOK, DIM), clip_ref[0, 0], jnp.int32).astype(F32).astype(BF)
    made[:, 3 * HEADS] = clip
    outs = [pltpu.make_async_copy(made.at[:, last], out_ref.at[:, last], out_sems.at[3 * PARTS])]
    outs[-1].start()
    for i in range(3):
        for part in range(PARTS):
            copies[i * PARTS + part].wait()
            units = pl.ds(part * units_of, units_of)
            for h in range(HEADS):
                block = held[i, part * size:(part + 1) * size, head(h)]
                made[units, i * HEADS + h] = block.reshape(units_of, TOK, DIM)
            at = (units, pl.ds(i * HEADS, HEADS))
            outs.append(
                pltpu.make_async_copy(made.at[at], out_ref.at[at], out_sems.at[i * PARTS + part])
            )
            outs[-1].start()
    for copy in outs:
        copy.wait()


def spatial_fwd_kernel(pos_ref, q_ref, k_ref, v_ref, keep_ref, give_ref, prob_ref):
    z, first = pos_ref[0], pos_ref[1] == 0
    for h in range(HEADS):
        prob = softmax(mm_nt(q_ref[0, :, head(h)], k_ref[0, :, head(h)]) * SCALE)
        prob_ref[h] = prob
        out = mm(prob.astype(BF), v_ref[0, :, head(h)])
        for chip in range(CHIPS):
            even = out[2 * chip * TOK:(2 * chip + 1) * TOK]
            odd = out[(2 * chip + 1) * TOK:(2 * chip + 2) * TOK]
            shift = (chip - z) & (CHIPS - 1)
            keep_ref[shift, h] = jnp.where(first, even, odd).astype(BF)
            give_ref[shift, h] = jnp.where(first, odd, even).astype(BF)


def merge_kernel(keep_ref, got_ref, *outs):
    for out, shift in zip(outs, (0,) + SHIFTS):
        out[0] = keep_ref[shift % CHIPS]
        out[1] = got_ref[shift % CHIPS]


def merge_last_kernel(tile_ref, keep_ref, got_ref, *outs):
    for out, shift in zip(outs, (0,) + SHIFTS):
        out[:HEADS] = keep_ref[-shift % CHIPS]
        out[HEADS:2 * HEADS] = got_ref[-shift % CHIPS]
        out[2 * HEADS] = tile_ref[...]


def pair_rows(pos_ref, shift):
    z, c = pos_ref[0], pos_ref[1]
    return range_row(z - shift, c), range_row(z - shift, 1 - c)


def spatial_bwd_kernel(q_ref, k_ref, v_ref, prob_ref, mid_ref, gq_ref, gk_ref, gv_ref):
    for h in range(HEADS):
        q, k, v = q_ref[0, :, head(h)], k_ref[0, :, head(h)], v_ref[0, :, head(h)]
        up = rows_of(mid_ref, h)
        prob = prob_ref[h]
        grad_prob = mm_nt(up, v)
        gv_ref[0, :, head(h)] = mm_tn(prob.astype(BF), up).astype(BF)
        row_dot = jnp.sum(prob * grad_prob, axis=-1, keepdims=True)
        low = (prob * (grad_prob - row_dot) * SCALE).astype(BF)
        gq_ref[0, :, head(h)] = mm(low, k).astype(BF)
        gk_ref[0, :, head(h)] = mm_tn(low, q).astype(BF)


def bias_kernel(rel_ref, offsets_ref, out_ref):
    offsets = offsets_ref[...]
    for h in range(HEADS):
        table = jnp.zeros((SEQ, ROWS), F32)
        for r in range(RELS):
            table = jnp.where(offsets == r, rel_ref[h, r], table)
        out_ref[h] = table


def temporal_mask(frames_ref, in_ref):
    row = lax.broadcasted_iota(jnp.int32, (ROWS, ROWS), 0)
    col = lax.broadcasted_iota(jnp.int32, (ROWS, ROWS), 1)
    clip = slot_rows(frames_ref, in_ref, 3 * HEADS).astype(F32)
    other = clip.T
    same = (row & (TOK - 1)) == (col & (TOK - 1))
    same &= jnp.concatenate([clip] * 2, axis=1) == jnp.concatenate([other] * 2, axis=0)
    return jnp.where(same, 0.0, NEG)


def temporal_prob(q, k, bias, mask):
    bias = jnp.broadcast_to(bias[:, None, :], (SEQ, TOK, ROWS)).reshape(ROWS, ROWS)
    return softmax((mm_nt(q, k) * SCALE + bias) + mask)


def temporal_a_kernel(frames_ref, in_ref, bias_ref, mid_ref):
    mask = temporal_mask(frames_ref, in_ref)
    for h in range(HEADS):
        q, k, up = (slot_rows(frames_ref, in_ref, i * HEADS + h) for i in range(3))
        prob = temporal_prob(q, k, bias_ref[h], mask)
        mid = mm_tn(prob.astype(BF), up).astype(BF)
        for s in range(SEQ):
            mid_ref[frames_ref[s], h] = mid[s * TOK:(s + 1) * TOK]


def temporal_b_kernel(frames_ref, in_ref, bias_ref, *refs):
    so_refs, (out_ref, keep_ref, give_ref, rows_ref) = dict(zip((0,) + SHIFTS, refs)), refs[-4:]
    so_at = [(so_refs[d if d <= CHIPS // 2 else d - CHIPS], x) for d, x in SLOTS]
    mask = temporal_mask(frames_ref, in_ref)
    for h in range(HEADS):
        q, k, up = (slot_rows(frames_ref, in_ref, i * HEADS + h) for i in range(3))
        so = jnp.concatenate([ref[x, h] for ref, x in so_at], axis=0)
        prob = temporal_prob(q, k, bias_ref[h], mask)
        grad_prob = mm_nt(up, so)
        put_frames(frames_ref, out_ref, 0, h, mm(prob.astype(BF), so))
        score = prob * (grad_prob - jnp.sum(prob * grad_prob, axis=-1, keepdims=True))
        rows_ref[h] = jnp.sum(score.reshape(SEQ, TOK, ROWS), axis=1)
        low = (score * SCALE).astype(BF)
        put_frames(frames_ref, out_ref, 1, h, mm(low, k))
        put_pairs(keep_ref, give_ref, h, mm_tn(low, q))


def unpack_kernel(in_ref, res_ref, gq_ref, sems):
    copies = []
    for u in range(SEQ):
        for i, out in enumerate((res_ref, gq_ref)):
            rows = pl.ds(u * TOK, TOK)
            copies.append(pltpu.make_async_copy(in_ref.at[u, i], out.at[0, rows], sems.at[u, i]))
            copies[-1].start()
    for copy in copies:
        copy.wait()


def finish_kernel(pos_ref, *refs):
    messages, (gk_ref, bias_ref) = refs[:CHIPS], refs[CHIPS:]
    for ref, shift in zip(messages, (0,) + SHIFTS):
        for x, row in enumerate(pair_rows(pos_ref, shift)):
            for h in range(HEADS):
                gk_ref[0, pl.ds(row, TOK), head(h)] = ref[x * HEADS + h]
    z = pos_ref[0]
    total = jnp.zeros((TOK, DIM), F32)
    for chip in range(CHIPS):
        for ref, shift in zip(messages, (0,) + SHIFTS):
            mine = ((z - shift) & (CHIPS - 1)) == chip
            total += jnp.where(mine, ref[2 * HEADS].astype(F32), 0.0)
    total = total + pltpu.roll(total, DIM - 32, 1) + pltpu.roll(total, DIM - 64, 1)
    bias_ref[...] = total[:HEADS, :RELS]


def call(kernel, name, specs, inputs, outputs, scratch=(), estimate=1000, params=PARAMS, space=VMEM):
    return pl.pallas_call(
        kernel,
        out_shape=tuple(outputs),
        in_specs=specs,
        out_specs=(space,) * len(outputs),
        scratch_shapes=scratch,
        compiler_params=params,
        cost_estimate=pl.CostEstimate(flops=estimate, bytes_accessed=1000, transcendentals=0),
        name=name,
    )(*inputs)


def exchange(packed):
    return lax.all_to_all(packed, "seq", split_axis=0, concat_axis=0, tiled=True)


def pair(terms, axis, mask):
    size = lax.axis_size(axis)
    return lax.ppermute(terms, axis, [(i, i ^ mask) for i in range(size)])


def sum_of_four(terms, axis, step):
    one, two, three = (pair(terms, axis, step * mask) for mask in (1, 2, 3))
    return (terms + one) + (two + three)


def move(message, s, x):
    perm = [(2 * z + c, 2 * ((z + s) % CHIPS) + (c ^ x)) for z in range(CHIPS) for c in range(2)]
    return lax.ppermute(message, "seq", perm)


def sent(messages):
    return [messages[0], *(move(m, s, 0) for m, s in zip(messages[1:], SHIFTS))]


def bfloat_parts(terms):
    parts = []
    for _ in range(3):
        part = lax.reduce_precision(terms, 8, 7)
        parts.append(jnp.pad(part, ((0, TOK - HEADS), (0, 1))))
        terms = terms - part
    return jnp.pad(jnp.concatenate(parts, axis=1), ((0, 0), (0, DIM - 96))).astype(BF)


def per_device(
    q_spatial, k_spatial, v_spatial, q_temporal, k_temporal, rel_bias, clip_ids, cotangent
):
    index = lax.axis_index("seq").astype(jnp.int32)
    z, c = index >> 1, index & 1
    pos = jnp.stack([z, c])
    away = jnp.array([d for d, x in SLOTS], jnp.int32)
    swapped = jnp.array([x for d, x in SLOTS], jnp.int32)
    frames = 2 * ((z - away) & (CHIPS - 1)) + (c ^ swapped)

    tiles = 3 * HEADS + 1
    (packed,) = call(
        pack_kernel,
        "pack",
        [SMEM] + [HBM] * 3,
        [clip_ids, q_temporal, k_temporal, cotangent],
        [units(SEQ, tiles)],
        [
            pltpu.VMEM((3, ROWS, WIDTH), BF),
            pltpu.VMEM((SEQ, tiles, TOK, DIM), BF),
            pltpu.SemaphoreType.DMA((3, PARTS)),
            pltpu.SemaphoreType.DMA((3 * PARTS + 1,)),
        ],
        space=HBM,
        params=pltpu.CompilerParams(vmem_limit_bytes=56 * 1024 * 1024),
    )
    there = exchange(packed)

    spatial = [q_spatial, k_spatial, v_spatial]
    spatial, rel_bias, frames, _ = lax.optimization_barrier((spatial, rel_bias, frames, packed))
    offsets = frames[:, None] - jnp.repeat(frames, TOK)[None, :] + (SEQ - 1)
    (bias,) = call(
        bias_kernel,
        "bias",
        [SMEM, VMEM],
        [rel_bias, offsets],
        [jax.ShapeDtypeStruct((HEADS, SEQ, ROWS), F32)],
    )
    wide = (offsets[:, :, None] == jnp.arange(RELS, dtype=jnp.int32)).astype(F32)
    keep_so, give_so, sp_prob = call(
        spatial_fwd_kernel,
        "spatial_fwd",
        [SMEM] + [VMEM] * 3,
        [pos, *spatial],
        [units(CHIPS, HEADS)] * 2 + [probs()],
    )
    give_so, bias = lax.optimization_barrier((give_so, bias))
    got_so = move(give_so, 0, 1)
    so_messages = call(
        merge_kernel, "merge", [VMEM] * 2, [keep_so, got_so], [units(2, HEADS)] * CHIPS
    )
    so = sent(so_messages)

    there, _, bias = lax.optimization_barrier((there, so_messages, bias))
    (mid,) = call(
        temporal_a_kernel,
        "temporal_a",
        [SMEM] + [VMEM] * 2,
        [frames, there, bias],
        [units(SEQ, HEADS)],
    )
    grad_mid = exchange(mid)

    back, keep_back, give_back, score_rows = call(
        temporal_b_kernel,
        "temporal_b",
        [SMEM] + [VMEM] * (2 + CHIPS),
        [frames, there, bias, *so],
        [jax.ShapeDtypeStruct((SEQ, 2, TOK, WIDTH), BF)]
        + [units(CHIPS, HEADS)] * 2
        + [jax.ShapeDtypeStruct((HEADS, SEQ, ROWS), F32)],
        estimate=LONG,
    )
    terms = jnp.einsum("hic,icr->hr", score_rows, wide, precision=lax.Precision.HIGHEST)
    terms = terms + move(terms, 0, 1)
    got_back = move(give_back, 0, 1)
    last = sent(
        call(
            merge_last_kernel,
            "merge_last",
            [VMEM] * 3,
            [bfloat_parts(terms), keep_back, got_back],
            [jax.ShapeDtypeStruct((2 * HEADS + 1, TOK, DIM), BF)] * CHIPS,
        )
    )
    returned = exchange(back)

    grad_mid, _ = lax.optimization_barrier((grad_mid, last))
    grad_qs, grad_ks, grad_vs = call(
        spatial_bwd_kernel,
        "spatial_bwd",
        [VMEM] * 5,
        [*spatial, sp_prob, grad_mid],
        [frame()] * 3,
        estimate=LONG,
    )
    last, _ = lax.optimization_barrier((last, grad_vs))
    grad_kt, total = call(
        finish_kernel,
        "finish",
        [SMEM] + [VMEM] * CHIPS,
        [pos, *last],
        [frame(), jax.ShapeDtypeStruct((HEADS, RELS), F32)],
    )
    total_bias = sum_of_four(sum_of_four(total, "grp", 1), "grp", 4)
    result, grad_qt = call(
        unpack_kernel,
        "unpack",
        [VMEM],
        [returned],
        [frame()] * 2,
        [pltpu.SemaphoreType.DMA((SEQ, 2))],
        space=HBM,
    )
    return result, grad_qs, grad_ks, grad_vs, grad_qt, grad_kt, total_bias


def solution(mesh):
    frames = P(("grp", "seq"), None, None)
    return jax.shard_map(
        per_device,
        mesh=mesh,
        in_specs=(frames,) * 5 + (P(), P("grp", "seq"), frames),
        out_specs=(frames,) * 6 + (P(),),
        check_vma=False,
    )
```

```python
import jax
import jax.numpy as jnp
from jax import lax
from jax.experimental import pallas as pl
from jax.experimental.pallas import tpu as pltpu
from jax.sharding import PartitionSpec as P

HEADS = 12
DIM = 128
RELS = 31
SEQ = 16
CHIPS = 8
TOK = 16
ROWS = SEQ * TOK
WIDTH = HEADS * DIM
SCALE = DIM ** (-0.5)
NEG = -1e30
BF = jnp.bfloat16
F32 = jnp.float32
PARAMS = pltpu.CompilerParams(vmem_limit_bytes=48 * 1024 * 1024)
PARTS = 4
LONG = 10**11
VMEM = pl.BlockSpec(memory_space=pltpu.VMEM)
SMEM = pl.BlockSpec(memory_space=pltpu.SMEM)
HBM = pl.BlockSpec(memory_space=pltpu.HBM)


def mm(left, right):
    return lax.dot_general(left, right, (((1,), (0,)), ((), ())), preferred_element_type=F32)


def mm_nt(left, right):
    return lax.dot_general(left, right, (((1,), (1,)), ((), ())), preferred_element_type=F32)


def mm_tn(left, right):
    return lax.dot_general(left, right, (((0,), (0,)), ((), ())), preferred_element_type=F32)


def softmax(scores):
    raw = jnp.exp(scores - jnp.max(scores, axis=-1, keepdims=True))
    return raw / jnp.sum(raw, axis=-1, keepdims=True)


def units(n, tiles):
    return jax.ShapeDtypeStruct((n, tiles, TOK, DIM), BF)


def frame():
    return jax.ShapeDtypeStruct((1, ROWS, WIDTH), BF)


def probs():
    return jax.ShapeDtypeStruct((HEADS, ROWS, ROWS), F32)


def range_row(chip, core):
    return pl.multiple_of((2 * (chip & (CHIPS - 1)) + core) * TOK, TOK)


def head(h):
    return slice(h * DIM, (h + 1) * DIM)


def rows_of(ref, tile):
    return ref[:, tile].reshape(ROWS, DIM)


SHIFTS = (1, -1, 4, 3, -3, 2, -2)
SLOTS = tuple((d, x) for x in range(2) for d in range(CHIPS))


def slot_rows(frames_ref, ref, tile):
    return jnp.concatenate([ref[frames_ref[s], tile] for s in range(SEQ)], axis=0)


def put_pairs(keep_ref, give_ref, tile, value):
    low = value.astype(BF)
    for d in range(CHIPS):
        keep_ref[d, tile] = low[d * TOK:(d + 1) * TOK]
        give_ref[d, tile] = low[(CHIPS + d) * TOK:(CHIPS + d + 1) * TOK]


def put_frames(frames_ref, ref, i, h, value):
    low = value.astype(BF)
    for s in range(SEQ):
        ref[frames_ref[s], i, :, head(h)] = low[s * TOK:(s + 1) * TOK]


def pack_kernel(clip_ref, q_ref, k_ref, up_ref, out_ref, held, made, sems, out_sems):
    copies = []
    size, units_of = ROWS // PARTS, SEQ // PARTS
    for i, ref in enumerate((q_ref, k_ref, up_ref)):
        for part in range(PARTS):
            rows = pl.ds(part * size, size)
            copies.append(
                pltpu.make_async_copy(ref.at[0, rows], held.at[i, rows], sems.at[i, part])
            )
            copies[-1].start()
    last = pl.ds(3 * HEADS, 1)
    clip = jnp.full((SEQ, TOK, DIM), clip_ref[0, 0], jnp.int32).astype(F32).astype(BF)
    made[:, 3 * HEADS] = clip
    outs = [pltpu.make_async_copy(made.at[:, last], out_ref.at[:, last], out_sems.at[3 * PARTS])]
    outs[-1].start()
    for i in range(3):
        for part in range(PARTS):
            copies[i * PARTS + part].wait()
            units = pl.ds(part * units_of, units_of)
            for h in range(HEADS):
                block = held[i, part * size:(part + 1) * size, head(h)]
                made[units, i * HEADS + h] = block.reshape(units_of, TOK, DIM)
            at = (units, pl.ds(i * HEADS, HEADS))
            outs.append(
                pltpu.make_async_copy(made.at[at], out_ref.at[at], out_sems.at[i * PARTS + part])
            )
            outs[-1].start()
    for copy in outs:
        copy.wait()


def spatial_fwd_kernel(pos_ref, q_ref, k_ref, v_ref, keep_ref, give_ref, prob_ref):
    z, first = pos_ref[0], pos_ref[1] == 0
    for h in range(HEADS):
        prob = softmax(mm_nt(q_ref[0, :, head(h)], k_ref[0, :, head(h)]) * SCALE)
        prob_ref[h] = prob
        out = mm(prob.astype(BF), v_ref[0, :, head(h)])
        for chip in range(CHIPS):
            even = out[2 * chip * TOK:(2 * chip + 1) * TOK]
            odd = out[(2 * chip + 1) * TOK:(2 * chip + 2) * TOK]
            shift = (chip - z) & (CHIPS - 1)
            keep_ref[shift, h] = jnp.where(first, even, odd).astype(BF)
            give_ref[shift, h] = jnp.where(first, odd, even).astype(BF)


def merge_kernel(keep_ref, got_ref, *outs):
    for out, shift in zip(outs, (0,) + SHIFTS):
        out[0] = keep_ref[shift % CHIPS]
        out[1] = got_ref[shift % CHIPS]


def merge_last_kernel(tile_ref, keep_ref, got_ref, *outs):
    for out, shift in zip(outs, (0,) + SHIFTS):
        out[:HEADS] = keep_ref[-shift % CHIPS]
        out[HEADS:2 * HEADS] = got_ref[-shift % CHIPS]
        out[2 * HEADS] = tile_ref[...]


def pair_rows(pos_ref, shift):
    z, c = pos_ref[0], pos_ref[1]
    return range_row(z - shift, c), range_row(z - shift, 1 - c)


def spatial_bwd_kernel(q_ref, k_ref, v_ref, prob_ref, mid_ref, gq_ref, gk_ref, gv_ref):
    for h in range(HEADS):
        q, k, v = q_ref[0, :, head(h)], k_ref[0, :, head(h)], v_ref[0, :, head(h)]
        up = rows_of(mid_ref, h)
        prob = prob_ref[h]
        grad_prob = mm_nt(up, v)
        gv_ref[0, :, head(h)] = mm_tn(prob.astype(BF), up).astype(BF)
        row_dot = jnp.sum(prob * grad_prob, axis=-1, keepdims=True)
        low = (prob * (grad_prob - row_dot) * SCALE).astype(BF)
        gq_ref[0, :, head(h)] = mm(low, k).astype(BF)
        gk_ref[0, :, head(h)] = mm_tn(low, q).astype(BF)


def bias_kernel(rel_ref, offsets_ref, out_ref):
    offsets = offsets_ref[...]
    for h in range(HEADS):
        table = jnp.zeros((SEQ, ROWS), F32)
        for r in range(RELS):
            table = jnp.where(offsets == r, rel_ref[h, r], table)
        out_ref[h] = table


def temporal_mask(frames_ref, in_ref):
    row = lax.broadcasted_iota(jnp.int32, (ROWS, ROWS), 0)
    col = lax.broadcasted_iota(jnp.int32, (ROWS, ROWS), 1)
    clip = slot_rows(frames_ref, in_ref, 3 * HEADS).astype(F32)
    other = clip.T
    same = (row & (TOK - 1)) == (col & (TOK - 1))
    same &= jnp.concatenate([clip] * 2, axis=1) == jnp.concatenate([other] * 2, axis=0)
    return jnp.where(same, 0.0, NEG)


def temporal_prob(q, k, bias, mask):
    bias = jnp.broadcast_to(bias[:, None, :], (SEQ, TOK, ROWS)).reshape(ROWS, ROWS)
    return softmax((mm_nt(q, k) * SCALE + bias) + mask)


def temporal_a_kernel(frames_ref, in_ref, bias_ref, mid_ref):
    mask = temporal_mask(frames_ref, in_ref)
    for h in range(HEADS):
        q, k, up = (slot_rows(frames_ref, in_ref, i * HEADS + h) for i in range(3))
        prob = temporal_prob(q, k, bias_ref[h], mask)
        mid = mm_tn(prob.astype(BF), up).astype(BF)
        for s in range(SEQ):
            mid_ref[frames_ref[s], h] = mid[s * TOK:(s + 1) * TOK]


def temporal_b_kernel(frames_ref, in_ref, bias_ref, *refs):
    so_refs, (out_ref, keep_ref, give_ref, rows_ref) = dict(zip((0,) + SHIFTS, refs)), refs[-4:]
    so_at = [(so_refs[d if d <= CHIPS // 2 else d - CHIPS], x) for d, x in SLOTS]
    mask = temporal_mask(frames_ref, in_ref)
    for h in range(HEADS):
        q, k, up = (slot_rows(frames_ref, in_ref, i * HEADS + h) for i in range(3))
        so = jnp.concatenate([ref[x, h] for ref, x in so_at], axis=0)
        prob = temporal_prob(q, k, bias_ref[h], mask)
        grad_prob = mm_nt(up, so)
        put_frames(frames_ref, out_ref, 0, h, mm(prob.astype(BF), so))
        score = prob * (grad_prob - jnp.sum(prob * grad_prob, axis=-1, keepdims=True))
        rows_ref[h] = jnp.sum(score.reshape(SEQ, TOK, ROWS), axis=1)
        low = (score * SCALE).astype(BF)
        put_frames(frames_ref, out_ref, 1, h, mm(low, k))
        put_pairs(keep_ref, give_ref, h, mm_tn(low, q))


def unpack_kernel(in_ref, res_ref, gq_ref, sems):
    copies = []
    for u in range(SEQ):
        for i, out in enumerate((res_ref, gq_ref)):
            rows = pl.ds(u * TOK, TOK)
            copies.append(pltpu.make_async_copy(in_ref.at[u, i], out.at[0, rows], sems.at[u, i]))
            copies[-1].start()
    for copy in copies:
        copy.wait()


def finish_kernel(pos_ref, *refs):
    messages, (gk_ref, bias_ref) = refs[:CHIPS], refs[CHIPS:]
    for ref, shift in zip(messages, (0,) + SHIFTS):
        for x, row in enumerate(pair_rows(pos_ref, shift)):
            for h in range(HEADS):
                gk_ref[0, pl.ds(row, TOK), head(h)] = ref[x * HEADS + h]
    z = pos_ref[0]
    total = jnp.zeros((TOK, DIM), F32)
    for chip in range(CHIPS):
        for ref, shift in zip(messages, (0,) + SHIFTS):
            mine = ((z - shift) & (CHIPS - 1)) == chip
            total += jnp.where(mine, ref[2 * HEADS].astype(F32), 0.0)
    total = total + pltpu.roll(total, DIM - 32, 1) + pltpu.roll(total, DIM - 64, 1)
    bias_ref[...] = total[:HEADS, :RELS]


def call(kernel, name, specs, inputs, outputs, scratch=(), estimate=1000, params=PARAMS, space=VMEM):
    return pl.pallas_call(
        kernel,
        out_shape=tuple(outputs),
        in_specs=specs,
        out_specs=(space,) * len(outputs),
        scratch_shapes=scratch,
        compiler_params=params,
        cost_estimate=pl.CostEstimate(flops=estimate, bytes_accessed=1000, transcendentals=0),
        name=name,
    )(*inputs)


def exchange(packed):
    return lax.all_to_all(packed, "seq", split_axis=0, concat_axis=0, tiled=True)


def pair(terms, axis, mask):
    size = lax.axis_size(axis)
    return lax.ppermute(terms, axis, [(i, i ^ mask) for i in range(size)])


def sum_of_four(terms, axis, step):
    one, two, three = (pair(terms, axis, step * mask) for mask in (1, 2, 3))
    return (terms + one) + (two + three)


def move(message, s, x):
    perm = [(2 * z + c, 2 * ((z + s) % CHIPS) + (c ^ x)) for z in range(CHIPS) for c in range(2)]
    return lax.ppermute(message, "seq", perm)


def sent(messages):
    return [messages[0], *(move(m, s, 0) for m, s in zip(messages[1:], SHIFTS))]


def bfloat_parts(terms):
    parts = []
    for _ in range(3):
        part = lax.reduce_precision(terms, 8, 7)
        parts.append(jnp.pad(part, ((0, TOK - HEADS), (0, 1))))
        terms = terms - part
    return jnp.pad(jnp.concatenate(parts, axis=1), ((0, 0), (0, DIM - 96))).astype(BF)


def per_device(
    q_spatial, k_spatial, v_spatial, q_temporal, k_temporal, rel_bias, clip_ids, cotangent
):
    index = lax.axis_index("seq").astype(jnp.int32)
    z, c = index >> 1, index & 1
    pos = jnp.stack([z, c])
    away = jnp.array([d for d, x in SLOTS], jnp.int32)
    swapped = jnp.array([x for d, x in SLOTS], jnp.int32)
    frames = 2 * ((z - away) & (CHIPS - 1)) + (c ^ swapped)

    tiles = 3 * HEADS + 1
    (packed,) = call(
        pack_kernel,
        "pack",
        [SMEM] + [HBM] * 3,
        [clip_ids, q_temporal, k_temporal, cotangent],
        [units(SEQ, tiles)],
        [
            pltpu.VMEM((3, ROWS, WIDTH), BF),
            pltpu.VMEM((SEQ, tiles, TOK, DIM), BF),
            pltpu.SemaphoreType.DMA((3, PARTS)),
            pltpu.SemaphoreType.DMA((3 * PARTS + 1,)),
        ],
        space=HBM,
        params=pltpu.CompilerParams(vmem_limit_bytes=56 * 1024 * 1024),
    )
    there = exchange(packed)

    spatial = [q_spatial, k_spatial, v_spatial]
    spatial, rel_bias, frames, _ = lax.optimization_barrier((spatial, rel_bias, frames, packed))
    offsets = frames[:, None] - jnp.repeat(frames, TOK)[None, :] + (SEQ - 1)
    (bias,) = call(
        bias_kernel,
        "bias",
        [SMEM, VMEM],
        [rel_bias, offsets],
        [jax.ShapeDtypeStruct((HEADS, SEQ, ROWS), F32)],
    )
    wide = (offsets[:, :, None] == jnp.arange(RELS, dtype=jnp.int32)).astype(F32)
    keep_so, give_so, sp_prob = call(
        spatial_fwd_kernel,
        "spatial_fwd",
        [SMEM] + [VMEM] * 3,
        [pos, *spatial],
        [units(CHIPS, HEADS)] * 2 + [probs()],
    )
    give_so, bias = lax.optimization_barrier((give_so, bias))
    got_so = move(give_so, 0, 1)
    so_messages = call(
        merge_kernel, "merge", [VMEM] * 2, [keep_so, got_so], [units(2, HEADS)] * CHIPS
    )
    so = sent(so_messages)

    there, _, bias = lax.optimization_barrier((there, so_messages, bias))
    (mid,) = call(
        temporal_a_kernel,
        "temporal_a",
        [SMEM] + [VMEM] * 2,
        [frames, there, bias],
        [units(SEQ, HEADS)],
    )
    grad_mid = exchange(mid)

    back, keep_back, give_back, score_rows = call(
        temporal_b_kernel,
        "temporal_b",
        [SMEM] + [VMEM] * (2 + CHIPS),
        [frames, there, bias, *so],
        [jax.ShapeDtypeStruct((SEQ, 2, TOK, WIDTH), BF)]
        + [units(CHIPS, HEADS)] * 2
        + [jax.ShapeDtypeStruct((HEADS, SEQ, ROWS), F32)],
        estimate=LONG,
    )
    terms = jnp.einsum("hic,icr->hr", score_rows, wide, precision=lax.Precision.HIGHEST)
    terms = terms + move(terms, 0, 1)
    got_back = move(give_back, 0, 1)
    last = sent(
        call(
            merge_last_kernel,
            "merge_last",
            [VMEM] * 3,
            [bfloat_parts(terms), keep_back, got_back],
            [jax.ShapeDtypeStruct((2 * HEADS + 1, TOK, DIM), BF)] * CHIPS,
        )
    )
    returned = exchange(back)

    grad_mid, _ = lax.optimization_barrier((grad_mid, last))
    grad_qs, grad_ks, grad_vs = call(
        spatial_bwd_kernel,
        "spatial_bwd",
        [VMEM] * 5,
        [*spatial, sp_prob, grad_mid],
        [frame()] * 3,
        estimate=LONG,
    )
    last, _ = lax.optimization_barrier((last, grad_vs))
    grad_kt, total = call(
        finish_kernel,
        "finish",
        [SMEM] + [VMEM] * CHIPS,
        [pos, *last],
        [frame(), jax.ShapeDtypeStruct((HEADS, RELS), F32)],
    )
    total_bias = sum_of_four(sum_of_four(total, "grp", 1), "grp", 4)
    result, grad_qt = call(
        unpack_kernel,
        "unpack",
        [VMEM],
        [returned],
        [frame()] * 2,
        [pltpu.SemaphoreType.DMA((SEQ, 2))],
        space=HBM,
    )
    return result, grad_qs, grad_ks, grad_vs, grad_qt, grad_kt, total_bias


def solution(mesh):
    frames = P(("grp", "seq"), None, None)
    return jax.shard_map(
        per_device,
        mesh=mesh,
        in_specs=(frames,) * 5 + (P(), P("grp", "seq"), frames),
        out_specs=(frames,) * 6 + (P(),),
        check_vma=False,
    )
```

```python
import jax
import jax.numpy as jnp
from jax import lax
from jax.experimental import pallas as pl
from jax.experimental.pallas import tpu as pltpu
from jax.sharding import PartitionSpec as P

HEADS = 12
DIM = 128
RELS = 31
SEQ = 16
CHIPS = 8
TOK = 16
ROWS = SEQ * TOK
WIDTH = HEADS * DIM
SCALE = DIM ** (-0.5)
NEG = -1e30
BF = jnp.bfloat16
F32 = jnp.float32
PARAMS = pltpu.CompilerParams(vmem_limit_bytes=48 * 1024 * 1024)
PARTS = 4
LONG = 10**11
VMEM = pl.BlockSpec(memory_space=pltpu.VMEM)
SMEM = pl.BlockSpec(memory_space=pltpu.SMEM)
HBM = pl.BlockSpec(memory_space=pltpu.HBM)


def mm(left, right):
    return lax.dot_general(left, right, (((1,), (0,)), ((), ())), preferred_element_type=F32)


def mm_nt(left, right):
    return lax.dot_general(left, right, (((1,), (1,)), ((), ())), preferred_element_type=F32)


def mm_tn(left, right):
    return lax.dot_general(left, right, (((0,), (0,)), ((), ())), preferred_element_type=F32)


def softmax(scores):
    raw = jnp.exp(scores - jnp.max(scores, axis=-1, keepdims=True))
    return raw / jnp.sum(raw, axis=-1, keepdims=True)


def units(n, tiles):
    return jax.ShapeDtypeStruct((n, tiles, TOK, DIM), BF)


def frame():
    return jax.ShapeDtypeStruct((1, ROWS, WIDTH), BF)


def probs():
    return jax.ShapeDtypeStruct((HEADS, ROWS, ROWS), F32)


def range_row(chip, core):
    return pl.multiple_of((2 * (chip & (CHIPS - 1)) + core) * TOK, TOK)


def head(h):
    return slice(h * DIM, (h + 1) * DIM)


def rows_of(ref, tile):
    return ref[:, tile].reshape(ROWS, DIM)


SHIFTS = (1, -1, 3, -3, 4, 2, -2)
SLOTS = tuple((d, x) for x in range(2) for d in range(CHIPS))


def slot_rows(frames_ref, ref, tile):
    return jnp.concatenate([ref[frames_ref[s], tile] for s in range(SEQ)], axis=0)


def put_pairs(keep_ref, give_ref, tile, value):
    low = value.astype(BF)
    for d in range(CHIPS):
        keep_ref[d, tile] = low[d * TOK:(d + 1) * TOK]
        give_ref[d, tile] = low[(CHIPS + d) * TOK:(CHIPS + d + 1) * TOK]


def put_frames(frames_ref, ref, i, h, value):
    low = value.astype(BF)
    for s in range(SEQ):
        ref[frames_ref[s], i, :, head(h)] = low[s * TOK:(s + 1) * TOK]


def pack_kernel(clip_ref, q_ref, k_ref, up_ref, out_ref, held, made, sems, out_sems):
    copies = []
    size, units_of = ROWS // PARTS, SEQ // PARTS
    for i, ref in enumerate((q_ref, k_ref, up_ref)):
        for part in range(PARTS):
            rows = pl.ds(part * size, size)
            copies.append(
                pltpu.make_async_copy(ref.at[0, rows], held.at[i, rows], sems.at[i, part])
            )
            copies[-1].start()
    last = pl.ds(3 * HEADS, 1)
    clip = jnp.full((SEQ, TOK, DIM), clip_ref[0, 0], jnp.int32).astype(F32).astype(BF)
    made[:, 3 * HEADS] = clip
    outs = [pltpu.make_async_copy(made.at[:, last], out_ref.at[:, last], out_sems.at[3 * PARTS])]
    outs[-1].start()
    for i in range(3):
        for part in range(PARTS):
            copies[i * PARTS + part].wait()
            units = pl.ds(part * units_of, units_of)
            for h in range(HEADS):
                block = held[i, part * size:(part + 1) * size, head(h)]
                made[units, i * HEADS + h] = block.reshape(units_of, TOK, DIM)
            at = (units, pl.ds(i * HEADS, HEADS))
            outs.append(
                pltpu.make_async_copy(made.at[at], out_ref.at[at], out_sems.at[i * PARTS + part])
            )
            outs[-1].start()
    for copy in outs:
        copy.wait()


def spatial_fwd_kernel(pos_ref, q_ref, k_ref, v_ref, keep_ref, give_ref, prob_ref):
    z, first = pos_ref[0], pos_ref[1] == 0
    for h in range(HEADS):
        prob = softmax(mm_nt(q_ref[0, :, head(h)], k_ref[0, :, head(h)]) * SCALE)
        prob_ref[h] = prob
        out = mm(prob.astype(BF), v_ref[0, :, head(h)])
        for chip in range(CHIPS):
            even = out[2 * chip * TOK:(2 * chip + 1) * TOK]
            odd = out[(2 * chip + 1) * TOK:(2 * chip + 2) * TOK]
            shift = (chip - z) & (CHIPS - 1)
            keep_ref[shift, h] = jnp.where(first, even, odd).astype(BF)
            give_ref[shift, h] = jnp.where(first, odd, even).astype(BF)


def merge_kernel(keep_ref, got_ref, *outs):
    for out, shift in zip(outs, (0,) + SHIFTS):
        out[0] = keep_ref[shift % CHIPS]
        out[1] = got_ref[shift % CHIPS]


def merge_last_kernel(tile_ref, keep_ref, got_ref, *outs):
    for out, shift in zip(outs, (0,) + SHIFTS):
        out[:HEADS] = keep_ref[-shift % CHIPS]
        out[HEADS:2 * HEADS] = got_ref[-shift % CHIPS]
        out[2 * HEADS] = tile_ref[...]


def pair_rows(pos_ref, shift):
    z, c = pos_ref[0], pos_ref[1]
    return range_row(z - shift, c), range_row(z - shift, 1 - c)


def spatial_bwd_kernel(q_ref, k_ref, v_ref, prob_ref, mid_ref, gq_ref, gk_ref, gv_ref):
    for h in range(HEADS):
        q, k, v = q_ref[0, :, head(h)], k_ref[0, :, head(h)], v_ref[0, :, head(h)]
        up = rows_of(mid_ref, h)
        prob = prob_ref[h]
        grad_prob = mm_nt(up, v)
        gv_ref[0, :, head(h)] = mm_tn(prob.astype(BF), up).astype(BF)
        row_dot = jnp.sum(prob * grad_prob, axis=-1, keepdims=True)
        low = (prob * (grad_prob - row_dot) * SCALE).astype(BF)
        gq_ref[0, :, head(h)] = mm(low, k).astype(BF)
        gk_ref[0, :, head(h)] = mm_tn(low, q).astype(BF)


def bias_kernel(rel_ref, offsets_ref, out_ref):
    offsets = offsets_ref[...]
    for h in range(HEADS):
        table = jnp.zeros((SEQ, ROWS), F32)
        for r in range(RELS):
            table = jnp.where(offsets == r, rel_ref[h, r], table)
        out_ref[h] = table


def temporal_mask(frames_ref, in_ref):
    row = lax.broadcasted_iota(jnp.int32, (ROWS, ROWS), 0)
    col = lax.broadcasted_iota(jnp.int32, (ROWS, ROWS), 1)
    clip = slot_rows(frames_ref, in_ref, 3 * HEADS).astype(F32)
    other = clip.T
    same = (row & (TOK - 1)) == (col & (TOK - 1))
    same &= jnp.concatenate([clip] * 2, axis=1) == jnp.concatenate([other] * 2, axis=0)
    return jnp.where(same, 0.0, NEG)


def temporal_prob(q, k, bias, mask):
    bias = jnp.broadcast_to(bias[:, None, :], (SEQ, TOK, ROWS)).reshape(ROWS, ROWS)
    return softmax((mm_nt(q, k) * SCALE + bias) + mask)


def temporal_a_kernel(frames_ref, in_ref, bias_ref, mid_ref):
    mask = temporal_mask(frames_ref, in_ref)
    for h in range(HEADS):
        q, k, up = (slot_rows(frames_ref, in_ref, i * HEADS + h) for i in range(3))
        prob = temporal_prob(q, k, bias_ref[h], mask)
        mid = mm_tn(prob.astype(BF), up).astype(BF)
        for s in range(SEQ):
            mid_ref[frames_ref[s], h] = mid[s * TOK:(s + 1) * TOK]


def temporal_b_kernel(frames_ref, in_ref, bias_ref, *refs):
    so_refs, (out_ref, keep_ref, give_ref, rows_ref) = dict(zip((0,) + SHIFTS, refs)), refs[-4:]
    so_at = [(so_refs[d if d <= CHIPS // 2 else d - CHIPS], x) for d, x in SLOTS]
    mask = temporal_mask(frames_ref, in_ref)
    for h in range(HEADS):
        q, k, up = (slot_rows(frames_ref, in_ref, i * HEADS + h) for i in range(3))
        so = jnp.concatenate([ref[x, h] for ref, x in so_at], axis=0)
        prob = temporal_prob(q, k, bias_ref[h], mask)
        grad_prob = mm_nt(up, so)
        put_frames(frames_ref, out_ref, 0, h, mm(prob.astype(BF), so))
        score = prob * (grad_prob - jnp.sum(prob * grad_prob, axis=-1, keepdims=True))
        rows_ref[h] = jnp.sum(score.reshape(SEQ, TOK, ROWS), axis=1)
        low = (score * SCALE).astype(BF)
        put_frames(frames_ref, out_ref, 1, h, mm(low, k))
        put_pairs(keep_ref, give_ref, h, mm_tn(low, q))


def unpack_kernel(in_ref, res_ref, gq_ref, sems):
    copies = []
    for u in range(SEQ):
        for i, out in enumerate((res_ref, gq_ref)):
            rows = pl.ds(u * TOK, TOK)
            copies.append(pltpu.make_async_copy(in_ref.at[u, i], out.at[0, rows], sems.at[u, i]))
            copies[-1].start()
    for copy in copies:
        copy.wait()


def finish_kernel(pos_ref, *refs):
    messages, (gk_ref, bias_ref) = refs[:CHIPS], refs[CHIPS:]
    for ref, shift in zip(messages, (0,) + SHIFTS):
        for x, row in enumerate(pair_rows(pos_ref, shift)):
            for h in range(HEADS):
                gk_ref[0, pl.ds(row, TOK), head(h)] = ref[x * HEADS + h]
    z = pos_ref[0]
    total = jnp.zeros((TOK, DIM), F32)
    for chip in range(CHIPS):
        for ref, shift in zip(messages, (0,) + SHIFTS):
            mine = ((z - shift) & (CHIPS - 1)) == chip
            total += jnp.where(mine, ref[2 * HEADS].astype(F32), 0.0)
    total = total + pltpu.roll(total, DIM - 32, 1) + pltpu.roll(total, DIM - 64, 1)
    bias_ref[...] = total[:HEADS, :RELS]


def call(kernel, name, specs, inputs, outputs, scratch=(), estimate=1000, params=PARAMS, space=VMEM):
    return pl.pallas_call(
        kernel,
        out_shape=tuple(outputs),
        in_specs=specs,
        out_specs=(space,) * len(outputs),
        scratch_shapes=scratch,
        compiler_params=params,
        cost_estimate=pl.CostEstimate(flops=estimate, bytes_accessed=1000, transcendentals=0),
        name=name,
    )(*inputs)


def exchange(packed):
    return lax.all_to_all(packed, "seq", split_axis=0, concat_axis=0, tiled=True)


def pair(terms, axis, mask):
    size = lax.axis_size(axis)
    return lax.ppermute(terms, axis, [(i, i ^ mask) for i in range(size)])


def sum_of_four(terms, axis, step):
    one, two, three = (pair(terms, axis, step * mask) for mask in (1, 2, 3))
    return (terms + one) + (two + three)


def move(message, s, x):
    perm = [(2 * z + c, 2 * ((z + s) % CHIPS) + (c ^ x)) for z in range(CHIPS) for c in range(2)]
    return lax.ppermute(message, "seq", perm)


def sent(messages):
    return [messages[0], *(move(m, s, 0) for m, s in zip(messages[1:], SHIFTS))]


def bfloat_parts(terms):
    parts = []
    for _ in range(3):
        part = lax.reduce_precision(terms, 8, 7)
        parts.append(jnp.pad(part, ((0, TOK - HEADS), (0, 1))))
        terms = terms - part
    return jnp.pad(jnp.concatenate(parts, axis=1), ((0, 0), (0, DIM - 96))).astype(BF)


def per_device(
    q_spatial, k_spatial, v_spatial, q_temporal, k_temporal, rel_bias, clip_ids, cotangent
):
    index = lax.axis_index("seq").astype(jnp.int32)
    z, c = index >> 1, index & 1
    pos = jnp.stack([z, c])
    away = jnp.array([d for d, x in SLOTS], jnp.int32)
    swapped = jnp.array([x for d, x in SLOTS], jnp.int32)
    frames = 2 * ((z - away) & (CHIPS - 1)) + (c ^ swapped)

    tiles = 3 * HEADS + 1
    (packed,) = call(
        pack_kernel,
        "pack",
        [SMEM] + [HBM] * 3,
        [clip_ids, q_temporal, k_temporal, cotangent],
        [units(SEQ, tiles)],
        [
            pltpu.VMEM((3, ROWS, WIDTH), BF),
            pltpu.VMEM((SEQ, tiles, TOK, DIM), BF),
            pltpu.SemaphoreType.DMA((3, PARTS)),
            pltpu.SemaphoreType.DMA((3 * PARTS + 1,)),
        ],
        space=HBM,
        params=pltpu.CompilerParams(vmem_limit_bytes=56 * 1024 * 1024),
    )
    there = exchange(packed)

    spatial = [q_spatial, k_spatial, v_spatial]
    spatial, rel_bias, frames, _ = lax.optimization_barrier((spatial, rel_bias, frames, packed))
    offsets = frames[:, None] - jnp.repeat(frames, TOK)[None, :] + (SEQ - 1)
    (bias,) = call(
        bias_kernel,
        "bias",
        [SMEM, VMEM],
        [rel_bias, offsets],
        [jax.ShapeDtypeStruct((HEADS, SEQ, ROWS), F32)],
    )
    wide = (offsets[:, :, None] == jnp.arange(RELS, dtype=jnp.int32)).astype(F32)
    keep_so, give_so, sp_prob = call(
        spatial_fwd_kernel,
        "spatial_fwd",
        [SMEM] + [VMEM] * 3,
        [pos, *spatial],
        [units(CHIPS, HEADS)] * 2 + [probs()],
    )
    give_so, bias = lax.optimization_barrier((give_so, bias))
    got_so = move(give_so, 0, 1)
    so_messages = call(
        merge_kernel, "merge", [VMEM] * 2, [keep_so, got_so], [units(2, HEADS)] * CHIPS
    )
    so = sent(so_messages)

    there, _, bias = lax.optimization_barrier((there, so_messages, bias))
    (mid,) = call(
        temporal_a_kernel,
        "temporal_a",
        [SMEM] + [VMEM] * 2,
        [frames, there, bias],
        [units(SEQ, HEADS)],
    )
    grad_mid = exchange(mid)

    back, keep_back, give_back, score_rows = call(
        temporal_b_kernel,
        "temporal_b",
        [SMEM] + [VMEM] * (2 + CHIPS),
        [frames, there, bias, *so],
        [jax.ShapeDtypeStruct((SEQ, 2, TOK, WIDTH), BF)]
        + [units(CHIPS, HEADS)] * 2
        + [jax.ShapeDtypeStruct((HEADS, SEQ, ROWS), F32)],
        estimate=LONG,
    )
    terms = jnp.einsum("hic,icr->hr", score_rows, wide, precision=lax.Precision.HIGHEST)
    terms = terms + move(terms, 0, 1)
    got_back = move(give_back, 0, 1)
    last = sent(
        call(
            merge_last_kernel,
            "merge_last",
            [VMEM] * 3,
            [bfloat_parts(terms), keep_back, got_back],
            [jax.ShapeDtypeStruct((2 * HEADS + 1, TOK, DIM), BF)] * CHIPS,
        )
    )
    returned = exchange(back)

    grad_mid, _ = lax.optimization_barrier((grad_mid, last))
    grad_qs, grad_ks, grad_vs = call(
        spatial_bwd_kernel,
        "spatial_bwd",
        [VMEM] * 5,
        [*spatial, sp_prob, grad_mid],
        [frame()] * 3,
        estimate=LONG,
    )
    last, _ = lax.optimization_barrier((last, grad_vs))
    grad_kt, total = call(
        finish_kernel,
        "finish",
        [SMEM] + [VMEM] * CHIPS,
        [pos, *last],
        [frame(), jax.ShapeDtypeStruct((HEADS, RELS), F32)],
    )
    total_bias = sum_of_four(sum_of_four(total, "grp", 1), "grp", 4)
    result, grad_qt = call(
        unpack_kernel,
        "unpack",
        [VMEM],
        [returned],
        [frame()] * 2,
        [pltpu.SemaphoreType.DMA((SEQ, 2))],
        space=HBM,
    )
    return result, grad_qs, grad_ks, grad_vs, grad_qt, grad_kt, total_bias


def solution(mesh):
    frames = P(("grp", "seq"), None, None)
    return jax.shard_map(
        per_device,
        mesh=mesh,
        in_specs=(frames,) * 5 + (P(), P("grp", "seq"), frames),
        out_specs=(frames,) * 6 + (P(),),
        check_vma=False,
    )
```
